32 devices in a mesh: dp: 8 (over y, x, core), tensor: 4 (over z).
Axes of the slice: x: 2, y: 2, z: 4, core: 2. Of those that a mesh axis runs over, the one named last changes fastest.
Arguments:
- tokens: bfloat16 [8192, 2048], P('dp', 'tensor'), may hold values from -6 to 6
- cotangent: bfloat16 [8192, 2048], P('dp', 'tensor'), may hold values from -6 to 6
- norm1_gain: bfloat16 [2048], P('tensor'), may hold values from 0.5 to 1.5
- w_query: bfloat16 [2048, 2048], P(None, 'tensor'), may hold values from -0.125 to 0.125
- w_key: bfloat16 [2048, 2048], P(None, 'tensor'), may hold values from -0.125 to 0.125
- w_value: bfloat16 [2048, 2048], P(None, 'tensor'), may hold values from -0.125 to 0.125
- query_gain: bfloat16 [2048], P('tensor'), may hold values from 0.25 to 1.75
- key_gain: bfloat16 [2048], P('tensor'), may hold values from 0.25 to 1.75
- w_output: bfloat16 [2048, 2048], P('tensor'), may hold values from -0.75 to 0.75
- norm2_gain: bfloat16 [2048], P('tensor'), may hold values from 0.5 to 1.5
- router: bfloat16 [2048, 6], replicated, may hold values from -0.09375 to 0.09375
- w_gate: bfloat16 [6, 2048, 1024], P(None, None, 'tensor'), may hold values from -0.125 to 0.125
- w_up: bfloat16 [6, 2048, 1024], P(None, None, 'tensor'), may hold values from -0.125 to 0.125
- w_down: bfloat16 [6, 1024, 2048], P(None, 'tensor'), may hold values from -1 to 1
- routes: int32 [8192, 3], P('dp'), may hold values from 0 to 5, as said below
- prefix: int32 [8], P('dp'), may hold values from 102 to 512
- slot_order: int32 [8, 3072], P('dp'), may hold values from 0 to 3071, each once within a row
Outputs:
- mixed: bfloat16 [8192, 2048], P('dp', 'tensor')
- grad_tokens: float32 [8192, 2048], P('dp', 'tensor')
- grad_norm1_gain: float32 [2048], P('tensor')
- grad_query: float32 [2048, 2048], P(None, 'tensor')
- grad_key: float32 [2048, 2048], P(None, 'tensor')
- grad_value: float32 [2048, 2048], P(None, 'tensor')
- grad_query_gain: float32 [2048], P('tensor')
- grad_key_gain: float32 [2048], P('tensor')
- grad_output: float32 [2048, 2048], P('tensor')
- grad_norm2_gain: float32 [2048], P('tensor')
- grad_router: float32 [2048, 6], replicated
- grad_gate: float32 [6, 2048, 1024], P(None, None, 'tensor')
- grad_up: float32 [6, 2048, 1024], P(None, None, 'tensor')
- grad_down: float32 [6, 1024, 2048], P(None, 'tensor')
The draws below stay inside these ranges and needn't reach their ends.
Inputs may be any that keep to these rules, and one draw needn't show every extreme that they name: `routes`: each token names 3 different experts. `slot_order`: each row names every pair index of its sequence once.
All inputs are finite; a program needn't handle non-finite values.
Results may differ from the reference program's by a relative error of at most 0.028.
Values may be sent and summed in bfloat16 or wider, within the bound.
No kernel may reach another device: no remote copies, remote signals or barrier semaphores. Data moves between devices by JAX's collectives and lax.ppermute only.
A program may use at most 384 MiB of HBM per device.

```python
import jax
import jax.numpy as jnp
from jax import lax

D = 2048
HEADS = 16
HEAD_DIM = 128
FF = 1024
EXPERTS = 6
TOP = 3
TOK_DEV = 1024
SEQUENCES = 8
TOKENS = 8192
PAIRS = 3072
CAP = 640


def draw_routes(key, part):
    key = jax.random.fold_in(key, 11)
    key_scores = jax.random.fold_in(key, 1)
    key_favour = jax.random.fold_in(key, 2)
    key_turns = jax.random.fold_in(key, 3)
    scores = jax.random.randint(key_scores, (TOKENS, EXPERTS), 0, 1048576, dtype=jnp.int32)
    favoured = jax.random.randint(key_favour, (SEQUENCES,), 0, EXPERTS, dtype=jnp.int32)
    row_seq = jnp.arange(TOKENS, dtype=jnp.int32) // TOK_DEV
    favoured_rows = favoured[row_seq]
    columns = jnp.arange(EXPERTS, dtype=jnp.int32)
    lifted = scores + jnp.where(favoured_rows[:, None] == columns[None, :], 314573, 0).astype(jnp.int32)
    distinct = lifted * EXPERTS + columns[None, :]
    top_values, chosen = lax.top_k(distinct, TOP)
    turns = jax.random.randint(key_turns, (TOKENS,), 0, TOP, dtype=jnp.int32)
    order = (jnp.arange(TOP, dtype=jnp.int32)[None, :] + turns[:, None]) % TOP
    return jnp.take_along_axis(chosen.astype(jnp.int32), order, axis=1).astype(jnp.int32)


def plant(array, stream_key, low, largest):
    spot = [jax.random.randint(jax.random.fold_in(stream_key, axis), (), 0, length) for axis, length in enumerate(array.shape)]
    main_axis = array.shape.index(max(array.shape))
    next_to = spot[:main_axis] + [(spot[main_axis] + 1) % array.shape[main_axis]] + spot[main_axis + 1:]
    return array.at[tuple(spot)].set(low).at[tuple(next_to)].set(largest)


def block_scale(stream_key, shape, pieces, least, top_value):
    level = 1.0
    for position, parts in pieces:
        draws = jax.random.uniform(jax.random.fold_in(jax.random.fold_in(stream_key, 6), position), (parts,), jnp.float32, least / len(pieces), top_value / len(pieces))
        level = level * jnp.repeat(jnp.exp(draws), shape[position] // parts).reshape((-1,) + (1,) * (len(shape) - 1 - position))
    return level


def gaussian(stream_key, dims, scale, reach, split=(), kind=jnp.bfloat16):
    values = jax.random.normal(stream_key, dims, jnp.float32) * scale
    if len(split) > 0:
        values = block_scale(stream_key, dims, split, -0.22, 0.18) * values
    return jnp.clip(values, min=-reach, max=reach).astype(kind)


def setup_inputs(seed: int = 0) -> dict:
    streams_of = jax.random.split(jax.random.key(seed), 18)
    return {
        "tokens": gaussian(streams_of[0], (TOKENS, D), 1.0, 6.0, ((0, 8), (1, 4))),
        "cotangent": gaussian(streams_of[1], (TOKENS, D), 1.0, 6.0, ((0, 8), (1, 4))),
        "norm1_gain": jnp.clip(1.0 + 0.1 * jax.random.normal(streams_of[2], (D,), jnp.float32), 0.5, 1.5).astype(jnp.bfloat16),
        "w_query": gaussian(streams_of[3], (D, D), D ** -0.5, 0.125, ((1, 4),)),
        "w_key": gaussian(streams_of[4], (D, D), D ** -0.5, 0.125, ((1, 4),)),
        "w_value": gaussian(streams_of[5], (D, D), D ** -0.5, 0.125, ((1, 4),)),
        "query_gain": jnp.clip(1.0 + 0.15 * jax.random.normal(streams_of[6], (D,), jnp.float32), 0.25, 1.75).astype(jnp.bfloat16),
        "key_gain": jnp.clip(1.0 + 0.15 * jax.random.normal(streams_of[7], (D,), jnp.float32), 0.25, 1.75).astype(jnp.bfloat16),
        "w_output": gaussian(streams_of[8], (D, D), (max(D // 32, 1)) ** -0.5, 0.75, ((0, 4),)),
        "norm2_gain": jnp.clip(1.0 + 0.1 * jax.random.normal(streams_of[9], (D,), jnp.float32), 0.5, 1.5).astype(jnp.bfloat16),
        "router": gaussian(streams_of[10], (D, EXPERTS), (2 * D) ** -0.5, 0.09375),
        "w_gate": gaussian(streams_of[11], (EXPERTS, D, FF), D ** -0.5, 0.125, ((2, 4),)),
        "w_up": gaussian(streams_of[12], (EXPERTS, D, FF), D ** -0.5, 0.125, ((2, 4),)),
        "w_down": gaussian(streams_of[13], (EXPERTS, FF, D), (max(FF // 32, 1)) ** -0.5, 1.0, ((1, 4),)),
        "routes": draw_routes(jax.random.fold_in(streams_of[17], 71), 0),
        "prefix": plant(jax.random.randint(streams_of[15], (SEQUENCES,), TOK_DEV // 10, TOK_DEV // 2 + 1), jax.random.fold_in(streams_of[15], 1), TOK_DEV // 10, (TOK_DEV // 2 + 1) - 1).astype(jnp.int32),
        "slot_order": jax.vmap(lambda own: jax.random.permutation(own, PAIRS))(jax.random.split(streams_of[16], SEQUENCES)).reshape((SEQUENCES, PAIRS)).astype(jnp.int32),
    }


EPSILON = 1e-05
ROPE_BASE = 10000.0
MASKED = -1e+30
HIGHEST = lax.Precision.HIGHEST

@jax.custom_vjp
def low(v):
    return lax.optimization_barrier(v.astype(jnp.bfloat16)).astype(jnp.float32)

@jax.custom_vjp
def low_back(v):
    return v

def low_keep(v):
    return (low(v), None)

def low_pass(kept, grad):
    return (grad,)

def back_keep(v):
    return (v, None)

def back_low(kept, grad):
    return (low(grad),)
low.defvjp(low_keep, low_pass)
low_back.defvjp(back_keep, back_low)

def rope_tables(length, head_size):
    halfway = head_size // 2
    freqs = ROPE_BASE ** (-(jnp.arange(halfway, dtype=jnp.float32) * 2.0 / head_size))
    angles = jnp.arange(length, dtype=jnp.float32)[:, None] * freqs[None, :]
    angles = jnp.concatenate([angles, angles], axis=1)
    return (jnp.cos(angles), jnp.sin(angles))

def rotate(field, cosine, sine):
    halfway = field.shape[-1] // 2
    turned = jnp.concatenate([-field[..., halfway:], field[..., :halfway]], axis=-1)
    return field * cosine[:, None, :] + turned * sine[:, None, :]

def rms_scale(field):
    return lax.rsqrt(lax.optimization_barrier(jnp.mean(field * field, axis=1, keepdims=True)) + EPSILON)

def softmax_rows(scores):
    highest = lax.optimization_barrier(jnp.max(scores, axis=-1, keepdims=True))
    exponent = jnp.exp(scores - highest)
    return exponent / lax.optimization_barrier(jnp.sum(exponent, axis=-1, keepdims=True))

def place(routes_seq, order_seq):
    flat_routes = routes_seq.reshape(-1)
    ordered = flat_routes[order_seq]
    choose = (ordered[:, None] == jnp.arange(EXPERTS, dtype=jnp.int32)[None, :]).astype(jnp.int32)
    slot_ranks = lax.optimization_barrier(jnp.sum(jnp.cumsum(choose, axis=0) * choose, axis=1)) - 1
    slot_index = jnp.zeros_like(flat_routes).at[order_seq].set(slot_ranks)
    target = jnp.where(slot_index < CAP, flat_routes * CAP + slot_index, EXPERTS * CAP).astype(jnp.int32)
    pair_ids = jnp.arange(flat_routes.shape[0], dtype=jnp.int32)
    source_pair = jnp.full((EXPERTS * CAP + 1,), flat_routes.shape[0], jnp.int32).at[target].set(pair_ids)
    return (source_pair[:EXPERTS * CAP], target)

def attend(queries, keys_all, values_all, prefix_len):
    length = queries.shape[0]
    rows_block = min(512, length)
    positions = jnp.arange(length, dtype=jnp.int32)
    factor = HEAD_DIM ** (-0.5)

    def one_block(offset):
        query_rows = lax.dynamic_slice_in_dim(queries, offset, rows_block, 0)
        raw_scores = jnp.einsum('qhd,khd->hqk', query_rows, keys_all, precision=HIGHEST) * factor
        scores = low_back(raw_scores)
        row_pos = offset + jnp.arange(rows_block, dtype=jnp.int32)
        allowed = (positions[None, :] <= row_pos[:, None]) | (positions[None, :] < prefix_len)
        weights = low(softmax_rows(jnp.where(allowed[None], scores, MASKED)))
        return jnp.einsum('hqk,khd->qhd', weights, values_all, precision=HIGHEST)
    starts = jnp.arange(length // rows_block, dtype=jnp.int32) * rows_block
    return lax.map(jax.checkpoint(one_block), starts).reshape(length, -1)

def sequence_layer(tokens_seq, prefix_len, routes_seq, order_seq, params):
    gain_one, w_query, w_key, w_value, gain_query, gain_key, w_output, gain_two, router, w_gate, w_up, w_down = params
    length = tokens_seq.shape[0]
    normed_one = low(tokens_seq * rms_scale(tokens_seq) * gain_one)
    query_pre = low_back(jnp.dot(normed_one, w_query, precision=HIGHEST))
    key_pre = low_back(jnp.dot(normed_one, w_key, precision=HIGHEST))
    value_rows = low_back(low(jnp.dot(normed_one, w_value, precision=HIGHEST)))
    query_normed = query_pre * rms_scale(query_pre) * gain_query
    key_normed = key_pre * rms_scale(key_pre) * gain_key
    cosine, sine = rope_tables(length, HEAD_DIM)
    query_rot = low_back(low(rotate(query_normed.reshape(length, HEADS, HEAD_DIM), cosine, sine)))
    key_rot = low_back(low(rotate(key_normed.reshape(length, HEADS, HEAD_DIM), cosine, sine)))
    attended = low_back(low(attend(query_rot, key_rot, value_rows.reshape(length, HEADS, HEAD_DIM), prefix_len)))
    residual = tokens_seq + low_back(jnp.dot(attended, w_output, precision=HIGHEST))
    normed_two = low(residual * rms_scale(residual) * gain_two)
    logits = low_back(jnp.dot(normed_two, router, precision=HIGHEST))
    expert_probs = softmax_rows(logits)
    choose = (routes_seq[:, :, None] == jnp.arange(EXPERTS, dtype=jnp.int32)[None, None, :]).astype(tokens_seq.dtype)
    gates = lax.optimization_barrier(jnp.sum(choose * expert_probs[:, None, :], axis=2))
    source_pair, target = place(routes_seq, order_seq)
    source_token = source_pair // TOP
    padded = jnp.concatenate([normed_two, jnp.zeros((1, D), tokens_seq.dtype)], axis=0)
    dispatched = padded[source_token].reshape(EXPERTS, CAP, D)
    pre_gate = low_back(jnp.einsum('ecd,edf->ecf', dispatched, w_gate, precision=HIGHEST))
    pre_up = low_back(jnp.einsum('ecd,edf->ecf', dispatched, w_up, precision=HIGHEST))
    hidden = low(pre_gate * jax.nn.sigmoid(pre_gate) * pre_up)
    expert_out = low_back(jnp.einsum('ecf,efd->ecd', hidden, w_down, precision=HIGHEST)).reshape(EXPERTS * CAP, D)
    expert_pad = jnp.concatenate([expert_out, jnp.zeros((1, D), tokens_seq.dtype)], axis=0)
    mixture = lax.optimization_barrier(jnp.sum(gates[:, :, None] * expert_pad[target].reshape(length, TOP, D), axis=1))
    return residual + mixture

def reference(tokens, cotangent, norm1_gain, w_query, w_key, w_value, query_gain, key_gain, w_output, norm2_gain, router, w_gate, w_up, w_down, routes, prefix, slot_order):
    params = tuple((weight.astype(jnp.float32) for weight in (norm1_gain, w_query, w_key, w_value, query_gain, key_gain, w_output, norm2_gain, router, w_gate, w_up, w_down)))
    routes_all = routes.reshape(SEQUENCES, TOK_DEV, TOP)
    step_layer = jax.checkpoint(sequence_layer)

    def forward(tokens_all, weights):

        def advance(carry, item):
            tokens_seq, prefix_len, routes_seq, order_seq = item
            return (carry, step_layer(tokens_seq, prefix_len, routes_seq, order_seq, weights))
        finish, outputs = lax.scan(advance, jnp.zeros((), jnp.float32), (tokens_all, prefix, routes_all, slot_order))
        return outputs
    tokens_all = tokens.astype(jnp.float32).reshape(SEQUENCES, TOK_DEV, D)
    outputs, pull_back = jax.vjp(forward, tokens_all, params)
    grad_all, grads = pull_back(cotangent.astype(jnp.float32).reshape(SEQUENCES, TOK_DEV, D))
    return (outputs.reshape(TOKENS, D).astype(jnp.bfloat16), grad_all.reshape(TOKENS, D), grads[0], grads[1], grads[2], grads[3], grads[4], grads[5], grads[6], grads[7], grads[8], grads[9], grads[10], grads[11])
```

```python
import functools

import jax
import jax.numpy as jnp
from jax import lax
from jax.experimental import pallas as pl
from jax.experimental.pallas import tpu as pltpu
from jax.sharding import PartitionSpec as P

HEAD_DIM = 128
EXPERTS = 6
TOP = 3
CAP = 640
PREFIX_MAX = 512

EPSILON = 1e-05
ROPE_BASE = 10000.0
MASKED = -1e30
BF = jnp.bfloat16
F32 = jnp.float32
VMEM_LIMIT = 56 * 1024 * 1024


def params():
    return pltpu.CompilerParams(vmem_limit_bytes=VMEM_LIMIT)


def cost(flops, nbytes, trans=0):
    return pl.CostEstimate(flops=int(flops), bytes_accessed=int(nbytes), transcendentals=int(trans))


def dot(a, b):
    return jnp.dot(a, b, preferred_element_type=F32)


def dot_t(a, b):
    return lax.dot_general(a, b, (((1,), (1,)), ((), ())), preferred_element_type=F32)


def row_sums(field):
    ones = jnp.ones((8, field.shape[1]), F32)
    return lax.dot_general(
        ones, field, (((1,), (1,)), ((), ())), precision=lax.Precision.HIGHEST,
        preferred_element_type=F32,
    )


def ring(size):
    return [(at, (at + 1) % size) for at in range(size)]


def gather_ring(block, size):
    held = [block]
    for _ in range(size - 1):
        held.append(lax.ppermute(held[-1], "tensor", ring(size)))
    return held


def scatter_ring(part, mine, size):
    received = None
    for step in range(1, size):
        term = part((mine - step) % size)
        if received is not None:
            term = term.astype(F32) + received.astype(F32)
        received = lax.ppermute(term.astype(BF), "tensor", ring(size))
    return part(mine).astype(F32) + received.astype(F32)


def sum_direct(field, size):
    total = field
    for step in range(1, size):
        total = total + lax.ppermute(
            field, "tensor", [(at, (at + step) % size) for at in range(size)]
        )
    return total


def exchange(blocks, mine, size):
    own = lax.dynamic_slice_in_dim(blocks, mine, 1, 0)
    out = lax.dynamic_update_slice_in_dim(jnp.zeros_like(blocks), own, mine, 0)
    for step in range(1, size):
        send = lax.dynamic_slice_in_dim(blocks, (mine + step) % size, 1, 0)
        got = lax.ppermute(send, "tensor", [(at, (at + step) % size) for at in range(size)])
        out = lax.dynamic_update_slice_in_dim(out, got, (mine - step) % size, 0)
    return out


def swap(field, mask, n):
    return lax.ppermute(field, "dp", [(at, at ^ mask) for at in range(n)])


def swap_orders(n):
    masks = [1 << bit for bit in range(n.bit_length() - 1)]
    return masks, masks[:1] + masks[1:][::-1]


def rel_table(order):
    bits = len(order)
    return [
        sum(order[s] for s in range(bits) if (p >> (bits - 1 - s)) & 1) for p in range(1 << bits)
    ]


def dp_sum(send, keep, order, n):
    received = swap(send, order[0], n)
    size = n // 2
    for mask in order[1:]:
        size //= 2
        send = keep[size:] + received[size:]
        keep = keep[:size] + received[:size]
        received = swap(send, mask, n)
    total = keep + received
    for mask in order[1:][::-1]:
        total = jnp.concatenate([total, swap(total, mask, n)], axis=0)
    return total, swap(total, order[0], n)


def dp_sum_small(field, n):
    for mask in swap_orders(n)[0]:
        field = field + swap(field, mask, n)
    return field


def qkv_kernel(x_ref, gain_ref, wq_ref, wk_ref, wv_ref, n1_ref, q_ref, k_ref, v_ref, sums_ref):
    blocks, rows, cols = x_ref.shape
    full = blocks * cols
    fields = [x_ref[t].astype(F32) for t in range(blocks)]
    squares = fields[0] * fields[0]
    for t in range(1, blocks):
        squares = squares + fields[t] * fields[t]
    scale = lax.rsqrt(jnp.sum(squares, axis=1, keepdims=True) / full + EPSILON)
    for t in range(blocks):
        gain = gain_ref[t, 0:1, :].astype(F32)
        n1_ref[:, t * cols : (t + 1) * cols] = (fields[t] * scale * gain).astype(BF)
    normed = n1_ref[...]
    query = dot(normed, wq_ref[...])
    key = dot(normed, wk_ref[...])
    q_ref[...] = query
    k_ref[...] = key
    v_ref[...] = dot(normed, wv_ref[...]).astype(BF)
    which = lax.broadcasted_iota(jnp.int32, (8, rows), 0)
    sums_ref[...] = jnp.where(
        which == 0,
        row_sums(query * query),
        jnp.where(which == 1, row_sums(key * key), row_sums(squares)),
    )


def qkv_call(x_aug, wq, wk, wv, length):
    blocks, _, cols = x_aug.shape
    full = blocks * cols
    out = wq.shape[1]
    rows = min(256, length)
    whole = pl.BlockSpec((full, out), lambda g: (0, 0))
    tile = pl.BlockSpec((rows, out), lambda g: (g, 0))
    return pl.pallas_call(
        qkv_kernel,
        grid=(length // rows,),
        in_specs=[
            pl.BlockSpec((blocks, rows, cols), lambda g: (0, g, 0)),
            pl.BlockSpec((blocks, 16, cols), lambda g: (0, length // 16, 0)),
            whole,
            whole,
            whole,
        ],
        out_specs=[
            pl.BlockSpec((rows, full), lambda g: (g, 0)),
            tile,
            tile,
            tile,
            pl.BlockSpec((8, rows), lambda g: (0, g)),
        ],
        out_shape=[
            jax.ShapeDtypeStruct((length, full), BF),
            jax.ShapeDtypeStruct((length, out), F32),
            jax.ShapeDtypeStruct((length, out), F32),
            jax.ShapeDtypeStruct((length, out), BF),
            jax.ShapeDtypeStruct((8, length), F32),
        ],
        compiler_params=params(),
        cost_estimate=cost(6 * length * full * out, 10 * length * full + 6 * full * out),
    )(x_aug, x_aug, wq, wk, wv)


def head_scales(sums_refs, full):
    total = sums_refs[0][...]
    for ref in sums_refs[1:]:
        total = total + ref[...]
    return jnp.transpose(lax.rsqrt(total / full + EPSILON))


def masked_scores(query, key, first, prefix):
    scores = dot_t(query, key) * (HEAD_DIM**-0.5)
    row = first + lax.broadcasted_iota(jnp.int32, scores.shape, 0)
    col = lax.broadcasted_iota(jnp.int32, scores.shape, 1)
    return jnp.where((col <= row) | (col < prefix), scores, MASKED)


def attn_forward_kernel(full, size, prefix_ref, q_ref, k_ref, v_ref, gq_ref, gk_ref, cos_ref, sin_ref, *rest):
    sums_refs, (att_ref, lse_ref, qr_ref, kr_ref) = rest[:size], rest[size:]
    length = q_ref.shape[0]
    rows = min(256, length)
    scales = head_scales(sums_refs, full)
    cosine, sine = cos_ref[...], sin_ref[...]
    for pre_ref, gain_ref, out_ref, at in ((q_ref, gq_ref, qr_ref, 0), (k_ref, gk_ref, kr_ref, 1)):
        field = pre_ref[...] * scales[:, at : at + 1] * gain_ref[...].astype(F32)
        out_ref[...] = (field * cosine + pltpu.roll(field, HEAD_DIM // 2, 1) * sine).astype(BF)
    prefix = prefix_ref[0]
    for first in range(0, length, rows):
        last = min(length, max(PREFIX_MAX, first + rows))
        scores = masked_scores(qr_ref[first : first + rows, :], kr_ref[:last, :], first, prefix)
        highest = jnp.max(scores, axis=1, keepdims=True)
        exponent = jnp.exp(scores - highest)
        total = jnp.sum(exponent, axis=1, keepdims=True)
        mixed = dot(exponent.astype(BF), v_ref[:last, :])
        att_ref[first : first + rows, :] = (mixed / total).astype(BF)
        lse_ref[first : first + rows, :] = jnp.broadcast_to(
            highest + jnp.log(total), (rows, HEAD_DIM)
        )


def attn_forward(prefix, q_pre, k_pre, v_rows, gq, gk, cosine, sine, sums):
    length, width = q_pre.shape
    full = width * len(sums)
    head = pl.BlockSpec((length, HEAD_DIM), lambda h, *_: (0, h))
    gain = pl.BlockSpec((1, HEAD_DIM), lambda h, *_: (0, h))
    table = pl.BlockSpec((length, HEAD_DIM), lambda h, *_: (0, 0))
    sums_spec = pl.BlockSpec((8, length), lambda h, *_: (0, 0))
    return pl.pallas_call(
        functools.partial(attn_forward_kernel, full, len(sums)),
        grid_spec=pltpu.PrefetchScalarGridSpec(
            num_scalar_prefetch=1,
            grid=(width // HEAD_DIM,),
            in_specs=[head, head, head, gain, gain, table, table] + [sums_spec] * len(sums),
            out_specs=[head] * 4,
        ),
        out_shape=[
            jax.ShapeDtypeStruct((length, width), BF),
            jax.ShapeDtypeStruct((length, width), F32),
            jax.ShapeDtypeStruct((length, width), BF),
            jax.ShapeDtypeStruct((length, width), BF),
        ],
        compiler_params=params(),
        cost_estimate=cost(4 * length * length * width, 20 * length * width, length * length * 4),
    )(prefix, q_pre, k_pre, v_rows, gq, gk, cosine, sine, *sums)


def attn_backward_kernel(
    full, size, prefix_ref, q_ref, k_ref, qr_ref, kr_ref, v_ref, do_ref, lse_ref, gq_ref, gk_ref,
    cos_ref, sin_ref, *rest,
):
    sums_refs, rest = rest[:size], rest[size:]
    dq_ref, dk_ref, dv_ref, gains_ref, rows_ref, kacc, vacc = rest
    head = pl.program_id(0)
    length = q_ref.shape[0]
    rows = min(256, length)
    prefix = prefix_ref[0]
    factor = HEAD_DIM**-0.5
    kacc[...] = jnp.zeros_like(kacc)
    vacc[...] = jnp.zeros_like(vacc)
    contract = (((0,), (0,)), ((), ()))
    for first in range(0, length, rows):
        last = min(length, max(PREFIX_MAX, first + rows))
        here = slice(first, first + rows)
        scores = masked_scores(qr_ref[here, :], kr_ref[:last, :], first, prefix)
        weights = jnp.exp(scores - lse_ref[here, 0:1])
        grad_rows = do_ref[here, :]
        weight_grad = dot_t(grad_rows, v_ref[:last, :])
        centred = jnp.sum(weight_grad * weights, axis=1, keepdims=True)
        score_grad = (weights * (weight_grad - centred)).astype(BF)
        dq_ref[here, :] = dot(score_grad, kr_ref[:last, :]) * factor
        kacc[:last, :] += lax.dot_general(
            score_grad, qr_ref[here, :], contract, preferred_element_type=F32
        )
        vacc[:last, :] += lax.dot_general(
            weights.astype(BF), grad_rows, contract, preferred_element_type=F32
        )
    dv_ref[...] = vacc[...].astype(BF)
    scales = head_scales(sums_refs, full)
    cosine, sine = cos_ref[...], sin_ref[...]
    which = lax.broadcasted_iota(jnp.int32, (8, length), 0)
    lanes = lax.broadcasted_iota(jnp.int32, (8, HEAD_DIM), 0)
    row_terms = jnp.zeros((8, length), F32)
    gain_terms = jnp.zeros((8, HEAD_DIM), F32)
    for at, (pre_ref, gain_ref, out_ref, raw) in enumerate(
        ((q_ref, gq_ref, dq_ref, dq_ref[...]), (k_ref, gk_ref, dk_ref, kacc[...] * factor))
    ):
        raw = raw.astype(BF).astype(F32)
        normed_grad = raw * cosine - pltpu.roll(raw, HEAD_DIM // 2, 1) * sine
        out_ref[...] = normed_grad
        product = normed_grad * pre_ref[...]
        row_terms = jnp.where(
            which == at, row_sums(product * gain_ref[...].astype(F32)), row_terms
        )
        gain_terms = jnp.where(
            lanes == at,
            jnp.sum(product * scales[:, at : at + 1], axis=0, keepdims=True),
            gain_terms,
        )
    gains_ref[...] = gain_terms

    @pl.when(head == 0)
    def _():
        rows_ref[...] = row_terms

    @pl.when(head > 0)
    def _():
        rows_ref[...] += row_terms


def attn_backward(prefix, q_pre, k_pre, q_rot, k_rot, v_rows, out_grad, lse, gq, gk, cosine, sine, sums):
    length, width = q_pre.shape
    full = width * len(sums)
    head = pl.BlockSpec((length, HEAD_DIM), lambda h, *_: (0, h))
    gain = pl.BlockSpec((1, HEAD_DIM), lambda h, *_: (0, h))
    table = pl.BlockSpec((length, HEAD_DIM), lambda h, *_: (0, 0))
    sums_spec = pl.BlockSpec((8, length), lambda h, *_: (0, 0))
    return pl.pallas_call(
        functools.partial(attn_backward_kernel, full, len(sums)),
        grid_spec=pltpu.PrefetchScalarGridSpec(
            num_scalar_prefetch=1,
            grid=(width // HEAD_DIM,),
            in_specs=[head] * 7 + [gain, gain, table, table] + [sums_spec] * len(sums),
            out_specs=[head, head, head, pl.BlockSpec((8, HEAD_DIM), lambda h, *_: (0, h)), sums_spec],
            scratch_shapes=[pltpu.VMEM((length, HEAD_DIM), F32)] * 2,
        ),
        out_shape=[
            jax.ShapeDtypeStruct((length, width), F32),
            jax.ShapeDtypeStruct((length, width), F32),
            jax.ShapeDtypeStruct((length, width), BF),
            jax.ShapeDtypeStruct((8, width), F32),
            jax.ShapeDtypeStruct((8, length), F32),
        ],
        compiler_params=params(),
        cost_estimate=cost(10 * length * length * width, 36 * length * width, length * length * 4),
    )(prefix, q_pre, k_pre, q_rot, k_rot, v_rows, out_grad, lse, gq, gk, cosine, sine, *sums)


def norm_back_kernel(full, size, q_ref, k_ref, v_ref, dq_ref, dk_ref, dv_ref, gq_ref, gk_ref, *rest):
    sums_refs, back_refs, (out_ref, stat_ref) = rest[:size], rest[size : 2 * size], rest[2 * size :]
    width = q_ref.shape[1]
    scales = head_scales(sums_refs, full)
    back = back_refs[0][...]
    for ref in back_refs[1:]:
        back = back + ref[...]
    back = jnp.transpose(back)
    grads = []
    stat = dv_ref[...].astype(F32) * v_ref[...].astype(F32)
    for at, (pre_ref, grad_ref, gain_ref) in enumerate(
        ((q_ref, dq_ref, gq_ref), (k_ref, dk_ref, gk_ref))
    ):
        scale = scales[:, at : at + 1]
        pre = pre_ref[...]
        grad = (
            scale * gain_ref[...].astype(F32) * grad_ref[...]
            - pre * (scale * scale * scale * back[:, at : at + 1] / full)
        ).astype(BF)
        stat = stat + grad.astype(F32) * pre
        grads.append(grad)
    out_ref[:, :width] = grads[0]
    out_ref[:, width : 2 * width] = grads[1]
    out_ref[:, 2 * width :] = dv_ref[...]
    stat_ref[...] = row_sums(stat)


def norm_back(q_pre, k_pre, v_rows, dq, dk, dv, gq, gk, sums, back):
    length, width = q_pre.shape
    full = width * len(sums)
    rows = min(256, length)
    tile = pl.BlockSpec((rows, width), lambda g: (g, 0))
    wide = pl.BlockSpec((rows, 3 * width), lambda g: (g, 0))
    gain = pl.BlockSpec((1, width), lambda g: (0, 0))
    line = pl.BlockSpec((8, rows), lambda g: (0, g))
    return pl.pallas_call(
        functools.partial(norm_back_kernel, full, len(sums)),
        grid=(length // rows,),
        in_specs=[tile] * 6 + [gain, gain] + [line] * (2 * len(sums)),
        out_specs=[wide, line],
        out_shape=[
            jax.ShapeDtypeStruct((length, 3 * width), BF),
            jax.ShapeDtypeStruct((8, length), F32),
        ],
        compiler_params=params(),
        cost_estimate=cost(20 * length * width, 28 * length * width),
    )(q_pre, k_pre, v_rows, dq, dk, dv, gq, gk, *sums, *back)


def expert_kernel(own, aliased, chunk_ref, n2_ref, cot_ref, router_ref, keep_ref, wg_ref, wu_ref, wd_ref, *rest):
    rest = list(rest)
    res_ref = rest.pop(0) if own else None
    rest = rest[aliased:]
    h2t_ref, dg_ref, du_ref, n2t_ref, mix_ref, dn2_ref, gg_ref, probs_ref, mix, dn2, gates = rest
    expert = pl.program_id(0)
    blocks, rows, cols = cot_ref.shape
    lane = lax.broadcasted_iota(jnp.int32, (rows, 128), 1)

    @pl.when(expert == 0)
    def _():
        logits = jnp.where(lane < EXPERTS, dot(n2_ref[...], router_ref[...]), MASKED)
        exponent = jnp.exp(logits - jnp.max(logits, axis=1, keepdims=True))
        probs = exponent / jnp.sum(exponent, axis=1, keepdims=True)
        probs_ref[...] = probs
        gates[...] = probs * keep_ref[...]
        gg_ref[...] = jnp.zeros_like(gg_ref)
        n2t_ref[...] = jnp.transpose(n2_ref[...])
        dn2[...] = jnp.zeros_like(dn2)
        if own:
            mix[...] = res_ref[...]
        else:
            mix[...] = jnp.zeros_like(mix)

    normed = n2_ref[...]
    w_down = wd_ref[0]
    pre_gate = dot(normed, wg_ref[0])
    pre_up = dot(normed, wu_ref[0])
    back = dot_t(cot_ref[0], w_down[:, :cols])
    for t in range(1, blocks):
        back = back + dot_t(cot_ref[t], w_down[:, t * cols : (t + 1) * cols])
    here = lane == expert
    gate = jnp.sum(jnp.where(here, gates[...], 0.0), axis=1, keepdims=True)
    sigmoid = jax.nn.sigmoid(pre_gate)
    activated = pre_gate * sigmoid
    hidden = (activated * pre_up).astype(BF).astype(F32)
    gate_grad = jnp.sum(back * hidden, axis=1, keepdims=True)
    gg_ref[...] += jnp.where(here, gate_grad * keep_ref[...], 0.0)
    back = back * gate
    h2 = (hidden * gate).astype(BF)
    dg = (back * pre_up * sigmoid * (1.0 + pre_gate * (1.0 - sigmoid))).astype(BF)
    du = (back * activated).astype(BF)
    h2t_ref[...] = jnp.transpose(h2)
    dg_ref[...] = dg
    du_ref[...] = du
    mix[...] += dot(h2, w_down)
    dn2[...] += dot_t(dg, wg_ref[0]) + dot_t(du, wu_ref[0])

    @pl.when(expert == EXPERTS - 1)
    def _():
        dn2_ref[...] = dn2[...].astype(BF)
        for t in range(blocks):
            mix_ref[t] = mix[:, t * cols : (t + 1) * cols].astype(BF)


def expert_call(chunk, n2, cot, router, keep, wg, wu, wd, residual, carried):
    rows, full = n2.shape
    blocks, length, cols = cot.shape
    hidden = wg.shape[2]
    own = residual is not None
    in_specs = [
        pl.BlockSpec((rows, full), lambda e, c: (0, 0)),
        pl.BlockSpec((blocks, rows, cols), lambda e, c: (0, c[0], 0)),
        pl.BlockSpec((full, 128), lambda e, c: (0, 0)),
        pl.BlockSpec((rows, 128), lambda e, c: (c[0], 0)),
        pl.BlockSpec((1, full, hidden), lambda e, c: (e, 0, 0)),
        pl.BlockSpec((1, full, hidden), lambda e, c: (e, 0, 0)),
        pl.BlockSpec((1, hidden, full), lambda e, c: (e, 0, 0)),
    ]
    operands = [chunk, n2, cot, router, keep, wg, wu, wd]
    if own:
        in_specs.append(pl.BlockSpec((rows, full), lambda e, c: (0, 0)))
        operands.append(residual)
    aliases = {len(operands) + k: k for k in range(len(carried))}
    in_specs += [pl.BlockSpec(memory_space=pl.ANY)] * len(carried)
    operands += list(carried)
    slab = pl.BlockSpec((rows, hidden), lambda e, c: (c[0], e))
    return pl.pallas_call(
        functools.partial(expert_kernel, own, len(carried)),
        grid_spec=pltpu.PrefetchScalarGridSpec(
            num_scalar_prefetch=1,
            grid=(EXPERTS,),
            in_specs=in_specs,
            out_specs=[
                pl.BlockSpec((hidden, rows), lambda e, c: (e, c[0])),
                slab,
                slab,
                pl.BlockSpec((full, rows), lambda e, c: (0, c[0])),
                pl.BlockSpec((blocks, rows, cols), lambda e, c: (0, c[0], 0)),
                pl.BlockSpec((rows, full), lambda e, c: (0, 0)),
                pl.BlockSpec((rows, 128), lambda e, c: (0, 0)),
                pl.BlockSpec((rows, 128), lambda e, c: (0, 0)),
            ],
            scratch_shapes=[
                pltpu.VMEM((rows, full), F32),
                pltpu.VMEM((rows, full), F32),
                pltpu.VMEM((rows, 128), F32),
            ],
        ),
        out_shape=[
            jax.ShapeDtypeStruct((EXPERTS * hidden, length), BF),
            jax.ShapeDtypeStruct((length, EXPERTS * hidden), BF),
            jax.ShapeDtypeStruct((length, EXPERTS * hidden), BF),
            jax.ShapeDtypeStruct((full, length), BF),
            jax.ShapeDtypeStruct((blocks, length, cols), BF),
            jax.ShapeDtypeStruct((rows, full), BF),
            jax.ShapeDtypeStruct((rows, 128), F32),
            jax.ShapeDtypeStruct((rows, 128), F32),
        ],
        input_output_aliases=aliases,
        compiler_params=params(),
        cost_estimate=cost(
            12 * rows * full * EXPERTS * hidden, 6 * full * EXPERTS * hidden + 10 * rows * full
        ),
    )(*operands)


def gate_up_kernel(n2t_ref, dg_ref, du_ref, gate_ref, up_ref):
    turned = n2t_ref[...]
    gate_ref[0] = dot(turned, dg_ref[...]).astype(BF)
    up_ref[0] = dot(turned, du_ref[...]).astype(BF)


def gate_up_grads(n2t, dg, du):
    full, length = n2t.shape
    hidden = dg.shape[1] // EXPERTS
    slab = pl.BlockSpec((length, hidden), lambda e: (0, e))
    out = pl.BlockSpec((1, full, hidden), lambda e: (e, 0, 0))
    return pl.pallas_call(
        gate_up_kernel,
        grid=(EXPERTS,),
        in_specs=[pl.BlockSpec((full, length), lambda e: (0, 0)), slab, slab],
        out_specs=[out, out],
        out_shape=[jax.ShapeDtypeStruct((EXPERTS, full, hidden), BF)] * 2,
        compiler_params=params(),
        cost_estimate=cost(4 * length * full * EXPERTS * hidden, 10 * full * EXPERTS * hidden),
    )(n2t, dg, du)


def down_kernel(h2t_ref, cot_ref, out_ref):
    product = dot(h2t_ref[...], cot_ref[0]).astype(BF)
    hidden = out_ref.shape[1]
    for e in range(EXPERTS):
        out_ref[e] = product[e * hidden : (e + 1) * hidden]


def down_grads(h2t, cot):
    wide, length = h2t.shape
    blocks, _, cols = cot.shape
    hidden = wide // EXPERTS
    return pl.pallas_call(
        down_kernel,
        grid=(blocks,),
        in_specs=[
            pl.BlockSpec((wide, length), lambda t: (0, 0)),
            pl.BlockSpec((1, length, cols), lambda t: (t, 0, 0)),
        ],
        out_specs=pl.BlockSpec((EXPERTS, hidden, cols), lambda t: (0, 0, t)),
        out_shape=jax.ShapeDtypeStruct((EXPERTS, hidden, blocks * cols), BF),
        compiler_params=params(),
        cost_estimate=cost(2 * length * wide * blocks * cols, 4 * wide * blocks * cols),
    )(h2t, cot)


def middle_kernel(mine_ref, att_ref, wo_ref, x_ref, gain_ref, res_ref, n2_ref):
    step = pl.program_id(0)
    blocks, rows, cols = x_ref.shape

    @pl.when(step == 0)
    def _():
        for t in range(blocks):
            res_ref[:, t * cols : (t + 1) * cols] = x_ref[t].astype(F32)

    res_ref[...] += dot(att_ref[0], wo_ref[...])

    @pl.when(step == blocks - 1)
    def _():
        residual = res_ref[...]
        scale = lax.rsqrt(jnp.mean(residual * residual, axis=1, keepdims=True) + EPSILON)
        for t in range(blocks):
            here = slice(t * cols, (t + 1) * cols)
            gain = gain_ref[t, 1:2, :].astype(F32)
            n2_ref[:, here] = (residual[:, here] * scale * gain).astype(BF)


def middle(mine, att, w_out, x_aug):
    blocks, rows, width = att.shape
    full = w_out.shape[1]
    cols = full // blocks
    last = x_aug.shape[1] // 16 - 1
    return pl.pallas_call(
        middle_kernel,
        grid_spec=pltpu.PrefetchScalarGridSpec(
            num_scalar_prefetch=1,
            grid=(blocks,),
            in_specs=[
                pl.BlockSpec((1, rows, width), lambda t, m: (t, 0, 0)),
                pl.BlockSpec((width, full), lambda t, m: (t, 0)),
                pl.BlockSpec((blocks, rows, cols), lambda t, m: (0, m[0], 0)),
                pl.BlockSpec((blocks, 16, cols), lambda t, m: (0, last, 0)),
            ],
            out_specs=[pl.BlockSpec((rows, full), lambda t, m: (0, 0))] * 2,
        ),
        out_shape=[
            jax.ShapeDtypeStruct((rows, full), F32),
            jax.ShapeDtypeStruct((rows, full), BF),
        ],
        compiler_params=params(),
        cost_estimate=cost(2 * rows * full * full, 2 * full * full),
    )(mine, att, w_out, x_aug, x_aug)


def middle_back_kernel(
    size, mine_ref, own_ref, received_ref, probs_ref, router_ref, res_ref, n2_ref, cot_ref, gain_ref, wo_ref, *rest
):
    grads_refs, (branch_ref, out_ref, parts_ref) = rest[:size], rest[size:]
    step = pl.program_id(0)
    blocks, rows, cols = cot_ref.shape
    full = blocks * cols

    @pl.when(step == 0)
    def _():
        probs = probs_ref[...]
        prob_grad = grads_refs[0][...]
        for ref in grads_refs[1:]:
            prob_grad = prob_grad + ref[...]
        centred = jnp.sum(prob_grad * probs, axis=1, keepdims=True)
        logit_grad = (probs * (prob_grad - centred)).astype(BF)
        grad = (
            own_ref[...].astype(F32)
            + received_ref[...].astype(F32)
            + dot_t(logit_grad, router_ref[...])
        )
        residual = res_ref[...]
        scale = lax.rsqrt(jnp.mean(residual * residual, axis=1, keepdims=True) + EPSILON)
        stat = jnp.zeros((rows, 1), F32)
        for t in range(blocks):
            here = slice(t * cols, (t + 1) * cols)
            gain = gain_ref[t, 1:2, :].astype(F32)
            stat = stat + jnp.sum(residual[:, here] * gain * grad[:, here], axis=1, keepdims=True)
        stat = scale * scale * scale * stat / full
        for t in range(blocks):
            here = slice(t * cols, (t + 1) * cols)
            gain = gain_ref[t, 1:2, :].astype(F32)
            branch_ref[:, here] = (
                cot_ref[t].astype(F32) + scale * gain * grad[:, here] - residual[:, here] * stat
            ).astype(BF)
        router_part = lax.dot_general(
            logit_grad, n2_ref[...], (((0,), (0,)), ((), ())), preferred_element_type=F32
        )[:8]
        norm_part = jnp.sum(grad * residual * scale, axis=0, keepdims=True)
        which = lax.broadcasted_iota(jnp.int32, (8, full), 0)
        parts_ref[...] = jnp.where(which == EXPERTS, norm_part, router_part)

    out_ref[0] = dot_t(branch_ref[...], wo_ref[...]).astype(BF)


def middle_back(mine, own, received, probs, router, residual, n2, cot, x_aug, w_out, gate_grads):
    blocks, _, cols = cot.shape
    rows, full = residual.shape
    width = full // blocks
    last = x_aug.shape[1] // 16 - 1
    whole = pl.BlockSpec((rows, full), lambda t, m: (0, 0))
    lanes = pl.BlockSpec((rows, 128), lambda t, m: (0, 0))
    return pl.pallas_call(
        functools.partial(middle_back_kernel, len(gate_grads)),
        grid_spec=pltpu.PrefetchScalarGridSpec(
            num_scalar_prefetch=1,
            grid=(blocks,),
            in_specs=[
                whole,
                whole,
                lanes,
                pl.BlockSpec((full, 128), lambda t, m: (0, 0)),
                whole,
                whole,
                pl.BlockSpec((blocks, rows, cols), lambda t, m: (0, m[0], 0)),
                pl.BlockSpec((blocks, 16, cols), lambda t, m: (0, last, 0)),
                pl.BlockSpec((width, full), lambda t, m: (t, 0)),
            ]
            + [lanes] * len(gate_grads),
            out_specs=[
                whole,
                pl.BlockSpec((1, rows, width), lambda t, m: (t, 0, 0)),
                pl.BlockSpec((8, full), lambda t, m: (0, 0)),
            ],
        ),
        out_shape=[
            jax.ShapeDtypeStruct((rows, full), BF),
            jax.ShapeDtypeStruct((blocks, rows, width), BF),
            jax.ShapeDtypeStruct((8, full), F32),
        ],
        compiler_params=params(),
        cost_estimate=cost(2 * rows * full * full, 2 * full * full),
    )(mine, own, received, probs, router, residual, n2, cot, x_aug, w_out, *gate_grads)


def reversed_bits(at, bits):
    return sum(((at >> b) & 1) << (bits - 1 - b) for b in range(bits)) if bits else at


def column_grad_kernel(table_ref, left_ref, right_ref, a_ref, b_ref):
    product = dot(jnp.transpose(left_ref[...]), right_ref[...]).astype(BF)
    half = a_ref.shape[2]
    a_ref[0] = product[:, :half]
    b_ref[0] = product[:, half:]


def column_grads(table, left, right, n):
    length, full = left.shape
    width = right.shape[1]
    half = width // 2
    piece = full // n
    bits = n.bit_length() - 2
    steps = n // 2
    return pl.pallas_call(
        column_grad_kernel,
        grid_spec=pltpu.PrefetchScalarGridSpec(
            num_scalar_prefetch=1,
            grid=(steps,),
            in_specs=[
                pl.BlockSpec((length, piece), lambda g, t: (0, t[g])),
                pl.BlockSpec((length, width), lambda g, t: (0, 0)),
            ],
            out_specs=[
                pl.BlockSpec((1, piece, half), lambda g, t: (g, 0, 0)),
                pl.BlockSpec((1, piece, half), lambda g, t: (reversed_bits(g, bits), 0, 0)),
            ],
        ),
        out_shape=[jax.ShapeDtypeStruct((steps, piece, half), BF)] * 2,
        compiler_params=params(),
        cost_estimate=cost(
            2 * length * piece * steps * width, 2 * length * (piece * steps + width)
        ),
    )(table, left, right)


def row_grad_kernel(table_ref, left_ref, right_ref, a_ref, b_ref, turned_left):
    @pl.when(pl.program_id(0) == 0)
    def _():
        turned_left[...] = jnp.transpose(left_ref[...])

    right = right_ref[0] if len(right_ref.shape) == 3 else right_ref[...]
    product = dot(turned_left[...], right).astype(BF)
    half = a_ref.shape[1]
    a_ref[0] = product[:half]
    b_ref[0] = product[half:]


def row_grads(table, left, right, n):
    length, width = left.shape
    full = right.shape[-1] * (right.shape[0] if right.ndim == 3 else 1)
    piece = full // n
    bits = n.bit_length() - 2
    steps = n // 2
    if right.ndim == 3:
        per = right.shape[2] // piece
        right_spec = pl.BlockSpec(
            (1, length, piece), lambda g, t: (t[g] // per, 0, lax.rem(t[g], per))
        )
    else:
        right_spec = pl.BlockSpec((length, piece), lambda g, t: (0, t[g]))
    half = width // 2
    return pl.pallas_call(
        row_grad_kernel,
        grid_spec=pltpu.PrefetchScalarGridSpec(
            num_scalar_prefetch=1,
            grid=(steps,),
            in_specs=[pl.BlockSpec((length, width), lambda g, t: (0, 0)), right_spec],
            out_specs=[
                pl.BlockSpec((1, half, piece), lambda g, t: (g, 0, 0)),
                pl.BlockSpec((1, half, piece), lambda g, t: (reversed_bits(g, bits), 0, 0)),
            ],
            scratch_shapes=[pltpu.VMEM((width, length), BF)],
        ),
        out_shape=[jax.ShapeDtypeStruct((steps, half, piece), BF)] * 2,
        compiler_params=params(),
        cost_estimate=cost(
            2 * length * piece * steps * width, 2 * length * (piece * steps + width)
        ),
    )(table, left, right)


def piece_specs(shape, steps, row):
    block = (1,) + shape
    return [
        pl.BlockSpec(block, lambda a, pos: (jnp.minimum(pos[row, a], steps - 1), 0, 0)),
        pl.BlockSpec(block, lambda a, pos: (jnp.maximum(pos[row, a] - steps, 0), 0, 0)),
    ]


def pick(pos_ref, row, steps, low_ref, high_ref):
    low = pos_ref[row, pl.program_id(0)] < steps
    return jnp.where(low, low_ref[0].astype(F32), high_ref[0].astype(F32))


def projections_kernel(steps, pos_ref, la_ref, ha_ref, lb_ref, hb_ref, q_ref, k_ref, v_ref):
    first = pick(pos_ref, 0, steps, la_ref, ha_ref)
    second = pick(pos_ref, 1, steps, lb_ref, hb_ref)
    width = q_ref.shape[1]
    half = width // 2
    q_ref[...] = first[:, :width]
    k_ref[:, :half] = first[:, width:]
    k_ref[:, half:] = second[:, :half]
    v_ref[...] = second[:, half:]


def widen_projections(pos, a, b, n):
    steps, piece, width = a[0].shape
    out = 2 * width // 3
    return pl.pallas_call(
        functools.partial(projections_kernel, steps),
        grid_spec=pltpu.PrefetchScalarGridSpec(
            num_scalar_prefetch=1,
            grid=(n,),
            in_specs=piece_specs((piece, width), steps, 0) + piece_specs((piece, width), steps, 1),
            out_specs=[pl.BlockSpec((piece, out), lambda g, pos: (g, 0))] * 3,
        ),
        out_shape=[jax.ShapeDtypeStruct((piece * n, out), F32)] * 3,
        compiler_params=params(),
        cost_estimate=cost(0, 18 * n * piece * out),
    )(pos, *a, *b)


def rows_kernel(steps, pos_ref, la_ref, ha_ref, lb_ref, hb_ref, out_ref):
    half = la_ref.shape[1]
    out_ref[:half, :] = pick(pos_ref, 0, steps, la_ref, ha_ref)
    out_ref[half:, :] = pick(pos_ref, 1, steps, lb_ref, hb_ref)


def widen_rows(pos, a, b, n):
    steps, half, piece = a[0].shape
    return pl.pallas_call(
        functools.partial(rows_kernel, steps),
        grid_spec=pltpu.PrefetchScalarGridSpec(
            num_scalar_prefetch=1,
            grid=(n,),
            in_specs=piece_specs((half, piece), steps, 0) + piece_specs((half, piece), steps, 1),
            out_specs=pl.BlockSpec((2 * half, piece), lambda g, pos: (0, g)),
        ),
        out_shape=jax.ShapeDtypeStruct((2 * half, piece * n), F32),
        compiler_params=params(),
        cost_estimate=cost(0, 12 * n * piece * half),
    )(pos, *a, *b)


def kept_experts(routes, order):
    length = routes.shape[0]
    token, which = order // TOP, order % TOP
    onehot = (token[:, None] == jnp.arange(length, dtype=jnp.int32)[None, :]).astype(BF)
    named = (routes[:, :, None] == jnp.arange(8, dtype=jnp.int32)).astype(BF).reshape(length, TOP * 8)
    ordered = dot(onehot, named).reshape(-1, TOP, 8)
    choose = jnp.sum(
        jnp.where(which[:, None, None] == jnp.arange(TOP)[None, :, None], ordered, 0.0), axis=1
    )
    kept = jnp.where(jnp.cumsum(choose, axis=0) <= CAP, choose, 0.0).astype(BF)
    kept = jnp.pad(kept, ((0, 0), (0, 120)))
    return lax.dot_general(onehot, kept, (((0,), (0,)), ((), ())), preferred_element_type=F32)


def stacked(blocks, mine):
    size = len(blocks)
    out = jnp.zeros((size,) + blocks[0].shape, blocks[0].dtype)
    for step, block in enumerate(blocks):
        out = lax.dynamic_update_slice_in_dim(out, block[None], (mine - step) % size, 0)
    return out


def on_device(
    tokens, cotangent, norm1_gain, w_query, w_key, w_value, query_gain, key_gain, w_output,
    norm2_gain, router, w_gate, w_up, w_down, routes, prefix, slot_order,
):
    size, n = lax.axis_size("tensor"), lax.axis_size("dp")
    mine, group = lax.axis_index("tensor"), lax.axis_index("dp")
    length, cols = tokens.shape
    full = cols * size
    rows = length // size

    order_a, order_b = swap_orders(n)
    rel_a, rel_b = rel_table(order_a), rel_table(order_b)
    table = jnp.asarray(rel_a, jnp.int32) ^ group
    positions = jnp.stack(
        [
            jnp.asarray([rel.index(v) for v in range(n)], jnp.int32)[
                jnp.arange(n, dtype=jnp.int32) ^ group
            ]
            for rel in (rel_a, rel_b)
        ]
    )
    half = n // 2

    part = w_output.shape[0] // n
    w_piece = lax.dynamic_slice_in_dim(w_output, group * part, part, 0)
    w_out = lax.all_gather(w_piece, ("tensor", "dp"), axis=0, tiled=True)
    extra = jnp.zeros((14, cols), BF)
    block = jnp.concatenate([tokens, norm1_gain[None], norm2_gain[None], extra], axis=0)
    x_blocks = gather_ring(block, size)
    x_blocks[-1], late_cot = lax.optimization_barrier((x_blocks[-1], cotangent))
    x_aug = stacked(x_blocks, mine)
    cot = lax.all_gather(late_cot, "tensor", axis=0)
    normed_one, q_pre, k_pre, v_rows, own_sums = qkv_call(x_aug, w_query, w_key, w_value, length)
    keep = kept_experts(routes, slot_order[0])
    router_wide = jnp.pad(router, ((0, 0), (0, 128 - EXPERTS)))
    here = mine.astype(jnp.int32)[None]

    def everyone(field):
        return [field] + [
            lax.ppermute(field, "tensor", [(at, (at + step) % size) for at in range(size)])
            for step in range(1, size)
        ]

    sums = everyone(own_sums)

    halfway = HEAD_DIM // 2
    freqs = ROPE_BASE ** (-(jnp.arange(halfway, dtype=F32) * 2.0 / HEAD_DIM))
    angles = jnp.arange(length, dtype=F32)[:, None] * freqs[None, :]
    cosine = jnp.concatenate([jnp.cos(angles)] * 2, axis=1)
    sine = jnp.concatenate([-jnp.sin(angles), jnp.sin(angles)], axis=1)
    gq, gk = query_gain[None], key_gain[None]
    attended, lse, q_rot, k_rot = attn_forward(
        prefix, q_pre, k_pre, v_rows, gq, gk, cosine, sine, sums
    )

    att_rows = exchange(attended.reshape(size, rows, -1), mine, size)
    residual, normed_two = middle(here, att_rows, w_out, x_aug)

    chunks = gather_ring(normed_two, size)
    carried = ()
    received = None
    gate_grads = []
    for step, chunk in enumerate(chunks):
        at = ((mine - step) % size).astype(jnp.int32)
        outs = expert_call(
            at[None], chunk, cot, router_wide, keep, w_gate, w_up, w_down,
            residual if step == 0 else None, carried,
        )
        carried, (dn2, gg, probs) = outs[:5], outs[5:]
        if step == 0:
            own_dn2, gate_grads, expert_probs = dn2, [gg], probs
            continue
        term = dn2 if received is None else dn2 + received
        received = lax.ppermute(term, "tensor", ring(size))
        gate_grads.append(
            lax.ppermute(gg, "tensor", [(i, (i - step) % size) for i in range(size)])
        )
    h2t, dg, du, n2t, mix = carried

    grad_gate, grad_up = gate_up_grads(n2t, dg, du)
    grad_down = down_grads(h2t, cot)
    grad_gate, grad_up, grad_down = lax.psum((grad_gate, grad_up, grad_down), "dp")

    branch_rows, out_rows, small = middle_back(
        here, own_dn2, received, expert_probs, router_wide, residual, normed_two, cot, x_aug,
        w_out, gate_grads,
    )
    small = sum_direct(small, size)

    out_grad = exchange(out_rows, mine, size).reshape(length, -1)
    branch = stacked(gather_ring(branch_rows, size), mine).reshape(length, full)
    dq, dk, dv, gain_grads, own_back = attn_backward(
        prefix, q_pre, k_pre, q_rot, k_rot, v_rows, out_grad, lse, gq, gk, cosine, sine, sums
    )
    back = everyone(own_back)
    send_out = row_grads(table[half:], attended, branch, n)
    keep_out = row_grads(table[:half], attended, branch, n)
    sum_out_a = dp_sum(send_out[0], keep_out[0], order_a, n)
    sum_out_b = dp_sum(send_out[1], keep_out[1], order_b, n)
    grad_qkv, own_stat = norm_back(q_pre, k_pre, v_rows, dq, dk, dv, gq, gk, sums, back)
    stat_one = sum_direct(own_stat, size)[0]

    w_all = jnp.concatenate([w_query, w_key, w_value], axis=1)

    def input_part(at):
        return dot_t(grad_qkv, lax.dynamic_slice_in_dim(w_all, at * cols, cols, 0))

    send_in = column_grads(table[half:], normed_one, grad_qkv, n)
    keep_in = column_grads(table[:half], normed_one, grad_qkv, n)
    sum_in_a = dp_sum(send_in[0], keep_in[0], order_a, n)
    sum_in_b = dp_sum(send_in[1], keep_in[1], order_b, n)
    normed_one_grad = scatter_ring(input_part, mine, size)

    own_tokens = tokens.astype(F32)
    gain_one = norm1_gain.astype(F32)[None]
    scale_one = lax.rsqrt(own_sums[2] / full + EPSILON)
    stat_row = (stat_one / full) * scale_one * scale_one
    own_branch = lax.dynamic_slice_in_dim(branch, mine * cols, cols, 1).astype(F32)
    grad_tokens = (
        own_branch
        + scale_one[:, None] * gain_one * normed_one_grad
        - own_tokens * stat_row[:, None]
    )
    norm1_part = jnp.sum(normed_one_grad * own_tokens * scale_one[:, None], axis=0)

    mixed = scatter_ring(
        lambda at: lax.dynamic_index_in_dim(mix, at, 0, keepdims=False), mine, size
    ).astype(BF)

    own_norm2 = lax.dynamic_slice_in_dim(small[EXPERTS], mine * cols, cols, 0)
    packed = jnp.concatenate(
        [small[:EXPERTS].reshape(-1), own_norm2, gain_grads[0], gain_grads[1]]
    )
    packed = dp_sum_small(packed.reshape(-1, 128), n).reshape(-1)
    grad_norm1_gain = dp_sum_small(norm1_part, n)
    marks = [EXPERTS * full, EXPERTS * full + cols, EXPERTS * full + 2 * cols]
    grad_router = packed[: marks[0]].reshape(EXPERTS, full).T
    grad_norm2_gain = packed[marks[0] : marks[1]]
    grad_query_gain = packed[marks[1] : marks[2]]
    grad_key_gain = packed[marks[2] :]

    grad_output = widen_rows(positions, sum_out_a, sum_out_b, n)
    grad_query, grad_key, grad_value = widen_projections(positions, sum_in_a, sum_in_b, n)
    return (
        mixed, grad_tokens, grad_norm1_gain, grad_query, grad_key, grad_value, grad_query_gain,
        grad_key_gain, grad_output, grad_norm2_gain, grad_router, grad_gate.astype(F32), grad_up.astype(F32),
        grad_down.astype(F32),
    )


def solution(mesh):
    rows, weight_cols, weight_rows = P("dp", "tensor"), P(None, "tensor"), P("tensor", None)
    vector, expert_cols, expert_rows = P("tensor"), P(None, None, "tensor"), P(None, "tensor", None)
    return jax.shard_map(
        on_device,
        mesh=mesh,
        in_specs=(
            rows, rows, vector, weight_cols, weight_cols, weight_cols, vector, vector, weight_rows,
            vector, P(), expert_cols, expert_cols, expert_rows, P("dp", None), P("dp"),
            P("dp", None),
        ),
        out_specs=(
            rows, rows, vector, weight_cols, weight_cols, weight_cols, vector, vector, weight_rows,
            vector, P(), expert_cols, expert_cols, expert_rows,
        ),
        check_vma=False,
    )
```

```python
import functools

import jax
import jax.numpy as jnp
from jax import lax
from jax.experimental import pallas as pl
from jax.experimental.pallas import tpu as pltpu
from jax.sharding import PartitionSpec as P

HEAD_DIM = 128
EXPERTS = 6
TOP = 3
CAP = 640
PREFIX_MAX = 512

EPSILON = 1e-05
ROPE_BASE = 10000.0
MASKED = -1e30
GROUP = 8
LONG = 2e13
BF = jnp.bfloat16
F32 = jnp.float32
VMEM_LIMIT = 56 * 1024 * 1024


class Chain:
    token = None


def launch(
    body, operands, *, grid, in_specs, out_specs, out_shape, work=1, prefetch=0, scratch=(), aliases=None,
    token=0, others=(),
):
    operands = list(operands)
    unread = [field for field in (Chain.token, *others) if field is not None]
    unread = [field for field in unread if all(field is not own for own in operands)]
    first, last = len(operands), len(operands) + len(unread)

    def kernel(*refs):
        body(*refs[:first], *refs[last:])

    out = pl.pallas_call(
        kernel,
        grid_spec=pltpu.PrefetchScalarGridSpec(
            num_scalar_prefetch=prefetch,
            grid=grid,
            in_specs=list(in_specs) + [pl.BlockSpec(memory_space=pl.ANY)] * len(unread),
            out_specs=out_specs,
            scratch_shapes=list(scratch),
        ),
        out_shape=out_shape,
        input_output_aliases=aliases or {},
        compiler_params=pltpu.CompilerParams(vmem_limit_bytes=VMEM_LIMIT),
        cost_estimate=pl.CostEstimate(flops=int(work), bytes_accessed=1, transcendentals=0),
    )(*operands, *unread)
    Chain.token = out[token] if isinstance(out, (list, tuple)) else out
    return out


def dot(a, b):
    return jnp.dot(a, b, preferred_element_type=F32)


def dot_t(a, b):
    return lax.dot_general(a, b, (((1,), (1,)), ((), ())), preferred_element_type=F32)


def row_sums(field):
    folded = field[:, :128]
    for at in range(128, field.shape[1], 128):
        folded = folded + field[:, at : at + 128]
    return jnp.sum(jnp.transpose(folded), axis=0, keepdims=True)


def ring(size):
    return [(at, (at + 1) % size) for at in range(size)]


def send(value, step, size):
    return lax.ppermute(value, "tensor", [(at, (at + step) % size) for at in range(size)])


def swap(value, mask, n):
    return lax.ppermute(value, "dp", [(at, at ^ mask) for at in range(n)])


def take(blocks, at):
    return lax.dynamic_slice_in_dim(blocks, at, 1, 0)


def place(size, received, mine, own):
    out = lax.dynamic_update_slice_in_dim(jnp.zeros((size,) + own.shape[1:], own.dtype), own, mine, 0)
    for step, block in enumerate(received, 1):
        out = lax.dynamic_update_slice_in_dim(out, block, (mine - step) % size, 0)
    return out


def swap(field, mask, n):
    return lax.ppermute(field, "dp", [(at, at ^ mask) for at in range(n)])


def swap_masks(n):
    return [1 << bit for bit in range(n.bit_length() - 1)]


def rel_table(masks):
    bits = len(masks)
    return [
        sum(masks[s] for s in range(bits) if (p >> (bits - 1 - s)) & 1) for p in range(1 << bits)
    ]


def blockwise(body, ins, outs, others=(), work=1):
    chunks = max(c for c in (1, 2, 3, 4) if ins[0].shape[1] % (16 * c) == 0)

    def spec(shape):
        return pl.BlockSpec((shape[0], shape[1] // chunks, shape[2]), lambda g: (0, g, 0))

    def kernel(*refs):
        body(refs[: len(ins)], refs[len(ins) :])

    return launch(
        kernel,
        [*ins],
        grid=(chunks,),
        in_specs=[spec(field.shape) for field in ins],
        out_specs=[spec(shape) for shape in outs],
        out_shape=[jax.ShapeDtypeStruct(shape, BF) for shape in outs],
        others=others,
        work=work,
    )


def added(a, b):
    return (a.astype(F32) + b.astype(F32)).astype(BF)


def copied(field, others=()):
    def body(ins, outs):
        outs[0][...] = ins[0][...]

    return blockwise(body, [field[None]], [(1,) + field.shape], others)[0][0]


def side_by_side(fields):
    def body(ins, outs):
        at = 0
        for ref in ins:
            outs[0][:, :, at : at + ref.shape[2]] = ref[...]
            at += ref.shape[2]

    width = sum(field.shape[1] for field in fields)
    return blockwise(body, [field[None] for field in fields], [(1, fields[0].shape[0], width)])[0][0]


def add_blocks(a, b, work=1):
    def body(ins, outs):
        outs[0][...] = added(ins[0][...], ins[1][...])

    return blockwise(body, [a, b], [a.shape], work=work)[0]


class Sum:
    def __init__(self, n, parts, first):
        self.n, self.parts = n, parts
        self.masks = swap_masks(n)
        self.stage = 0
        self.flying = [swap(first, self.masks[0], n)]

    def send(self, fields, stage):
        self.flying = []
        for part, field in enumerate(fields):
            mask = self.masks[stage] if part == 0 else self.masks[-stage]
            self.flying.append(swap(field, mask, self.n))

    def split(self, keeps, received):
        count, rows, width = keeps[0].shape
        wide = width // self.parts if len(keeps) < self.parts else width

        def body(ins, outs):
            for part in range(self.parts):
                at = part if len(keeps) == self.parts else 0
                here = slice(part * wide, (part + 1) * wide) if at != part else slice(0, wide)
                for i in range(count):
                    total = added(ins[2 * at][i, :, here], ins[2 * at + 1][i, :, here])
                    if part == 0:
                        away, place_at = i >= count // 2, i % (count // 2)
                    else:
                        away, place_at = i % 2 == 1, i // 2
                    outs[2 * part + (0 if away else 1)][place_at] = total

        ins = [field for pair in zip(keeps, received, strict=True) for field in pair]
        outs = blockwise(body, ins, [(count // 2, rows, wide)] * (2 * self.parts))
        return outs[0::2], outs[1::2]

    def total(self, keeps, received):
        def body(ins, outs):
            for part, out in enumerate(outs):
                out[...] = added(ins[2 * part][...], ins[2 * part + 1][...])

        ins = [field for pair in zip(keeps, received, strict=True) for field in pair]
        return blockwise(body, ins, [field.shape for field in keeps])

    def joined(self, last, keeps, received):
        count, rows, wide = keeps[0].shape

        def body(ins, outs):
            for part in range(self.parts):
                out = outs[0] if last else outs[part]
                here = slice(part * wide, (part + 1) * wide) if last else slice(0, wide)
                for i in range(count):
                    low, high = (i, count + i) if part == 0 else (2 * i, 2 * i + 1)
                    out[low, :, here] = ins[2 * part][i]
                    out[high, :, here] = ins[2 * part + 1][i]

        ins = [field for pair in zip(keeps, received, strict=True) for field in pair]
        if last:
            return blockwise(body, ins, [(2 * count, rows, wide * self.parts)])
        return blockwise(body, ins, [(2 * count, rows, wide)] * self.parts)

    def step(self):
        bits = len(self.masks)
        if self.stage == 2 * bits - 1:
            return
        received = self.flying
        self.stage += 1
        if self.stage < bits:
            keep = [self.keep] if self.stage == 1 else self.keep
            away, self.keep = self.split(keep, received)
            self.send(away, self.stage)
            return
        back = 2 * bits - 1 - self.stage
        if self.stage == bits:
            self.keep = self.total(self.keep, received)
        else:
            self.keep = self.joined(back == 0, self.keep, received)
        if back:
            self.send(self.keep, back)
        else:
            self.keep = self.keep[0]
            self.flying = [swap(self.keep, self.masks[0], self.n)]

    def finish(self):
        return self.keep, self.flying[0]


def copied_pair(first, second, work):
    fold = second.shape[0] // first.shape[0]

    def body(ins, outs):
        outs[0][...] = ins[0][...]
        outs[1][...] = ins[1][...]

    folded = second.reshape(fold, first.shape[0], second.shape[1])
    a, b = blockwise(
        body, [first[None], folded], [(1,) + first.shape, folded.shape], work=work
    )
    return a[0], b.reshape(second.shape)


def qkv_kernel(owners_ref, *refs):
    blocks, refs = refs[:-9], refs[-9:]
    gain_ref, wq_ref, wk_ref, wv_ref, n1_ref, q_ref, k_ref, v_ref, sums_ref = refs
    rows, cols = blocks[0].shape
    full = len(blocks) * cols
    fields = [block[...].astype(F32) for block in blocks]
    squares = fields[0] * fields[0]
    for field in fields[1:]:
        squares = squares + field * field
    scale = lax.rsqrt(jnp.sum(squares, axis=1, keepdims=True) / full + EPSILON)
    for k, field in enumerate(fields):
        at = owners_ref[k]
        gain = gain_ref[at, 0:1, :].astype(F32)
        first = pl.multiple_of(at * cols, 128)
        n1_ref[:, pl.ds(first, cols)] = (field * scale * gain).astype(BF)
    normed = n1_ref[...]
    query = dot(normed, wq_ref[...])
    key = dot(normed, wk_ref[...])
    q_ref[...] = query
    k_ref[...] = key
    v_ref[...] = dot(normed, wv_ref[...]).astype(BF)
    which = lax.broadcasted_iota(jnp.int32, (8, rows), 0)
    sums_ref[...] = jnp.where(
        which == 0,
        row_sums(query * query),
        jnp.where(which == 1, row_sums(key * key), row_sums(squares)),
    )


def qkv_call(owners, blocks, gains, wq, wk, wv):
    length, cols = blocks[0].shape
    full = cols * len(blocks)
    out = wq.shape[1]
    rows = min(256, length)
    whole = pl.BlockSpec((full, out), lambda g, o: (0, 0))
    tile = pl.BlockSpec((rows, out), lambda g, o: (g, 0))
    return launch(
        qkv_kernel,
        [owners, *blocks, gains, wq, wk, wv],
        prefetch=1,
        grid=(length // rows,),
        in_specs=[pl.BlockSpec((rows, cols), lambda g, o: (g, 0))] * len(blocks)
        + [pl.BlockSpec((len(blocks), 16, cols), lambda g, o: (0, 0, 0)), whole, whole, whole],
        out_specs=[
            pl.BlockSpec((rows, full), lambda g, o: (g, 0)),
            tile,
            tile,
            tile,
            pl.BlockSpec((8, rows), lambda g, o: (0, g)),
        ],
        out_shape=[
            jax.ShapeDtypeStruct((length, full), BF),
            jax.ShapeDtypeStruct((length, out), F32),
            jax.ShapeDtypeStruct((length, out), F32),
            jax.ShapeDtypeStruct((length, out), BF),
            jax.ShapeDtypeStruct((8, length), F32),
        ],
    )


def head_scales(sums_refs, full):
    total = sums_refs[0][...]
    for ref in sums_refs[1:]:
        total = total + ref[...]
    return jnp.transpose(lax.rsqrt(total / full + EPSILON))


def masked_scores(query, key, first, prefix):
    scores = dot_t(query, key) * (HEAD_DIM**-0.5)
    row = first + lax.broadcasted_iota(jnp.int32, scores.shape, 0)
    col = lax.broadcasted_iota(jnp.int32, scores.shape, 1)
    return jnp.where((col <= row) | (col < prefix), scores, MASKED)


def attn_forward_kernel(full, size, prefix_ref, q_ref, k_ref, v_ref, gq_ref, gk_ref, cos_ref, sin_ref, *rest):
    sums_refs, (att_ref, lse_ref, qr_ref, kr_ref) = rest[:size], rest[size:]
    length = q_ref.shape[0]
    rows = min(256, length)
    scales = head_scales(sums_refs, full)
    cosine, sine = cos_ref[...], sin_ref[...]
    for pre_ref, gain_ref, out_ref, at in ((q_ref, gq_ref, qr_ref, 0), (k_ref, gk_ref, kr_ref, 1)):
        field = pre_ref[...] * scales[:, at : at + 1] * gain_ref[...].astype(F32)
        out_ref[...] = (field * cosine + pltpu.roll(field, HEAD_DIM // 2, 1) * sine).astype(BF)
    prefix = prefix_ref[0]
    for first in range(0, length, rows):
        last = min(length, max(PREFIX_MAX, first + rows))
        scores = masked_scores(qr_ref[first : first + rows, :], kr_ref[:last, :], first, prefix)
        highest = jnp.max(scores, axis=1, keepdims=True)
        exponent = jnp.exp(scores - highest)
        total = jnp.sum(exponent, axis=1, keepdims=True)
        mixed = dot(exponent.astype(BF), v_ref[:last, :])
        att_ref[first : first + rows, :] = (mixed / total).astype(BF)
        lse_ref[first : first + rows, :] = jnp.broadcast_to(
            highest + jnp.log(total), (rows, HEAD_DIM)
        )


def attn_forward(prefix, q_pre, k_pre, v_rows, gq, gk, cosine, sine, sums):
    length, width = q_pre.shape
    full = width * len(sums)
    head = pl.BlockSpec((length, HEAD_DIM), lambda h, *_: (0, h))
    gain = pl.BlockSpec((1, HEAD_DIM), lambda h, *_: (0, h))
    table = pl.BlockSpec((length, HEAD_DIM), lambda h, *_: (0, 0))
    sums_spec = pl.BlockSpec((8, length), lambda h, *_: (0, 0))
    return launch(
        functools.partial(attn_forward_kernel, full, len(sums)),
        [prefix, q_pre, k_pre, v_rows, gq, gk, cosine, sine, *sums],
        prefetch=1,
            grid=(width // HEAD_DIM,),
            in_specs=[head, head, head, gain, gain, table, table] + [sums_spec] * len(sums),
            out_specs=[head] * 4,
        out_shape=[
            jax.ShapeDtypeStruct((length, width), BF),
            jax.ShapeDtypeStruct((length, width), F32),
            jax.ShapeDtypeStruct((length, width), BF),
            jax.ShapeDtypeStruct((length, width), BF),
        ],
    )


def attn_backward_kernel(
    full, size, prefix_ref, q_ref, k_ref, qr_ref, kr_ref, v_ref, do_ref, lse_ref, gq_ref, gk_ref,
    cos_ref, sin_ref, *rest,
):
    sums_refs, rest = rest[:size], rest[size:]
    dq_ref, dk_ref, dv_ref, gains_ref, rows_ref, kacc, vacc = rest
    head = pl.program_id(0)
    length = q_ref.shape[0]
    rows = min(256, length)
    prefix = prefix_ref[0]
    factor = HEAD_DIM**-0.5
    kacc[...] = jnp.zeros_like(kacc)
    vacc[...] = jnp.zeros_like(vacc)
    contract = (((0,), (0,)), ((), ()))
    for first in range(0, length, rows):
        last = min(length, max(PREFIX_MAX, first + rows))
        here = slice(first, first + rows)
        scores = masked_scores(qr_ref[here, :], kr_ref[:last, :], first, prefix)
        weights = jnp.exp(scores - lse_ref[here, 0:1])
        grad_rows = do_ref[here, :]
        weight_grad = dot_t(grad_rows, v_ref[:last, :])
        centred = jnp.sum(weight_grad * weights, axis=1, keepdims=True)
        score_grad = (weights * (weight_grad - centred)).astype(BF)
        dq_ref[here, :] = dot(score_grad, kr_ref[:last, :]) * factor
        kacc[:last, :] += lax.dot_general(
            score_grad, qr_ref[here, :], contract, preferred_element_type=F32
        )
        vacc[:last, :] += lax.dot_general(
            weights.astype(BF), grad_rows, contract, preferred_element_type=F32
        )
    dv_ref[...] = vacc[...].astype(BF)
    scales = head_scales(sums_refs, full)
    cosine, sine = cos_ref[...], sin_ref[...]
    which = lax.broadcasted_iota(jnp.int32, (8, length), 0)
    lanes = lax.broadcasted_iota(jnp.int32, (8, HEAD_DIM), 0)
    row_terms = jnp.zeros((8, length), F32)
    gain_terms = jnp.zeros((8, HEAD_DIM), F32)
    for at, (pre_ref, gain_ref, out_ref, raw) in enumerate(
        ((q_ref, gq_ref, dq_ref, dq_ref[...]), (k_ref, gk_ref, dk_ref, kacc[...] * factor))
    ):
        raw = raw.astype(BF).astype(F32)
        normed_grad = raw * cosine - pltpu.roll(raw, HEAD_DIM // 2, 1) * sine
        out_ref[...] = normed_grad
        product = normed_grad * pre_ref[...]
        row_terms = jnp.where(
            which == at, row_sums(product * gain_ref[...].astype(F32)), row_terms
        )
        gain_terms = jnp.where(
            lanes == at,
            jnp.sum(product * scales[:, at : at + 1], axis=0, keepdims=True),
            gain_terms,
        )
    gains_ref[...] = gain_terms
    product = dv_ref[...].astype(F32) * v_ref[...].astype(F32)
    row_terms = jnp.where(which == 2, row_sums(product), row_terms)

    @pl.when(head == 0)
    def _():
        rows_ref[...] = row_terms

    @pl.when(head > 0)
    def _():
        rows_ref[...] += row_terms


def attn_backward(
    prefix, q_pre, k_pre, q_rot, k_rot, v_rows, out_grad, lse, gq, gk, cosine, sine, sums, others=()
):
    length, width = q_pre.shape
    full = width * len(sums)
    head = pl.BlockSpec((length, HEAD_DIM), lambda h, *_: (0, h))
    gain = pl.BlockSpec((1, HEAD_DIM), lambda h, *_: (0, h))
    table = pl.BlockSpec((length, HEAD_DIM), lambda h, *_: (0, 0))
    sums_spec = pl.BlockSpec((8, length), lambda h, *_: (0, 0))
    return launch(
        functools.partial(attn_backward_kernel, full, len(sums)),
        [prefix, q_pre, k_pre, q_rot, k_rot, v_rows, out_grad, lse, gq, gk, cosine, sine, *sums],
        prefetch=1,
            grid=(width // HEAD_DIM,),
            in_specs=[head] * 7 + [gain, gain, table, table] + [sums_spec] * len(sums),
            out_specs=[head, head, head, pl.BlockSpec((8, HEAD_DIM), lambda h, *_: (0, h)), sums_spec],
            scratch=[pltpu.VMEM((length, HEAD_DIM), F32)] * 2,
        out_shape=[
            jax.ShapeDtypeStruct((length, width), F32),
            jax.ShapeDtypeStruct((length, width), F32),
            jax.ShapeDtypeStruct((length, width), BF),
            jax.ShapeDtypeStruct((8, width), F32),
            jax.ShapeDtypeStruct((8, length), F32),
        ],
        others=others,
    )


def norm_back_kernel(
    full, size, q_ref, k_ref, dq_ref, dk_ref, dv_ref, gq_ref, gk_ref, branch_ref, *rest
):
    sums_refs, back_refs, (out_ref, stat_ref, copy_ref) = rest[:size], rest[size : 2 * size], rest[2 * size :]
    copy_ref[...] = branch_ref[...]
    width = q_ref.shape[1]
    scales = head_scales(sums_refs, full)
    back = back_refs[0][...]
    squares = sums_refs[0][...]
    for ref, sums_ref in zip(back_refs[1:], sums_refs[1:], strict=True):
        back = back + ref[...]
        squares = squares + sums_ref[...]
    scale = lax.rsqrt(squares / full + EPSILON)
    along = scale * back - scale * scale * scale * (back / full) * squares
    stat_ref[...] = jnp.broadcast_to(along[0:1] + along[1:2] + back[2:3], stat_ref.shape)
    back = jnp.transpose(back)
    grads = []
    for at, (pre_ref, grad_ref, gain_ref) in enumerate(
        ((q_ref, dq_ref, gq_ref), (k_ref, dk_ref, gk_ref))
    ):
        scale = scales[:, at : at + 1]
        pre = pre_ref[...]
        grad = (
            scale * gain_ref[...].astype(F32) * grad_ref[...]
            - pre * (scale * scale * scale * back[:, at : at + 1] / full)
        ).astype(BF)
        grads.append(grad)
    out_ref[:, :width] = grads[0]
    out_ref[:, width : 2 * width] = grads[1]
    out_ref[:, 2 * width :] = dv_ref[...]


def norm_back(q_pre, k_pre, dq, dk, dv, gq, gk, branch, sums, back):
    length, width = q_pre.shape
    full = width * len(sums)
    rows = min(256, length)
    tile = pl.BlockSpec((rows, width), lambda g: (g, 0))
    wide = pl.BlockSpec((rows, 3 * width), lambda g: (g, 0))
    gain = pl.BlockSpec((1, width), lambda g: (0, 0))
    chunk = branch.shape[0] * rows // length
    part = pl.BlockSpec((chunk, branch.shape[1]), lambda g: (g, 0))
    line = pl.BlockSpec((8, rows), lambda g: (0, g))
    return launch(
        functools.partial(norm_back_kernel, full, len(sums)),
        [q_pre, k_pre, dq, dk, dv, gq, gk, branch, *sums, *back],
        grid=(length // rows,),
        in_specs=[tile] * 5 + [gain, gain, part] + [line] * (2 * len(sums)),
        out_specs=[wide, line, part],
        out_shape=[
            jax.ShapeDtypeStruct((length, 3 * width), BF),
            jax.ShapeDtypeStruct((8, length), F32),
            jax.ShapeDtypeStruct(branch.shape, BF),
        ],

    )


def expert_kernel(step, aliased, chunk_ref, n2_ref, cot_ref, router_ref, keep_ref, wg_ref, wu_ref, wd_ref, *rest):
    rest = list(rest)
    own = step == 0
    res_ref = rest.pop(0) if own else None
    rest = rest[aliased:]
    h2t_ref, dg_ref, du_ref, n2t_ref, mix_ref, dn2_ref, probs_ref, mix, dn2, gates, gate_grads = rest
    expert = pl.program_id(0)
    blocks, rows, cols = cot_ref.shape
    lane = lax.broadcasted_iota(jnp.int32, (rows, 128), 1)

    @pl.when(expert == 0)
    def _():
        logits = jnp.where(lane < EXPERTS, dot(n2_ref[...], router_ref[...]), MASKED)
        exponent = jnp.exp(logits - jnp.max(logits, axis=1, keepdims=True))
        probs = exponent / jnp.sum(exponent, axis=1, keepdims=True)
        probs_ref[...] = probs
        gates[...] = probs * keep_ref[...]
        gate_grads[...] = jnp.zeros_like(gate_grads)
        n2t_ref[...] = jnp.transpose(n2_ref[...])
        dn2[...] = jnp.zeros_like(dn2)
        if own:
            mix[...] = res_ref[...]
        else:
            mix[...] = jnp.zeros_like(mix)

    normed = n2_ref[...]
    w_down = wd_ref[0]
    pre_gate = dot(normed, wg_ref[0])
    pre_up = dot(normed, wu_ref[0])
    back = dot_t(cot_ref[0], w_down[:, :cols])
    for t in range(1, blocks):
        back = back + dot_t(cot_ref[t], w_down[:, t * cols : (t + 1) * cols])
    here = lane == expert
    gate = jnp.sum(jnp.where(here, gates[...], 0.0), axis=1, keepdims=True)
    sigmoid = jax.nn.sigmoid(pre_gate)
    activated = pre_gate * sigmoid
    hidden = (activated * pre_up).astype(BF).astype(F32)
    gate_grad = jnp.sum(back * hidden, axis=1, keepdims=True)
    gate_grads[...] += jnp.where(here, gate_grad * keep_ref[...], 0.0)
    back = back * gate
    h2 = (hidden * gate).astype(BF)
    dg = (back * pre_up * sigmoid * (1.0 + pre_gate * (1.0 - sigmoid))).astype(BF)
    du = (back * activated).astype(BF)
    h2t_ref[...] = jnp.transpose(h2)
    dg_ref[...] = dg
    du_ref[...] = du
    mix[...] += dot(h2, w_down)
    dn2[...] += dot_t(dg, wg_ref[0]) + dot_t(du, wu_ref[0])

    @pl.when(expert == EXPERTS - 1)
    def _():
        dn2_ref[:, : blocks * cols] = dn2[...].astype(BF)
        high = gate_grads[...].astype(BF).astype(F32)
        low = gate_grads[...] - high
        if step:
            high = pltpu.roll(high, GROUP * 2 * step, 1)
        low = pltpu.roll(low, GROUP * (2 * step + 1), 1)
        dn2_ref[:, blocks * cols :] = (high + low).astype(BF)
        for t in range(blocks):
            mix_ref[t] = mix[:, t * cols : (t + 1) * cols].astype(BF)


def expert_call(step, chunk, n2, cot, router, keep, wg, wu, wd, residual, carried):
    rows, full = n2.shape
    blocks, length, cols = cot.shape
    hidden = wg.shape[2]
    own = step == 0
    in_specs = [
        pl.BlockSpec((rows, full), lambda e, c: (0, 0)),
        pl.BlockSpec((blocks, rows, cols), lambda e, c: (0, c[0], 0)),
        pl.BlockSpec((full, 128), lambda e, c: (0, 0)),
        pl.BlockSpec((rows, 128), lambda e, c: (c[0], 0)),
        pl.BlockSpec((1, full, hidden), lambda e, c: (e, 0, 0)),
        pl.BlockSpec((1, full, hidden), lambda e, c: (e, 0, 0)),
        pl.BlockSpec((1, hidden, full), lambda e, c: (e, 0, 0)),
    ]
    operands = [chunk, n2, cot, router, keep, wg, wu, wd]
    if own:
        in_specs.append(pl.BlockSpec((rows, full), lambda e, c: (0, 0)))
        operands.append(residual)
    aliases = {len(operands) + k: k for k in range(len(carried))}
    in_specs += [pl.BlockSpec(memory_space=pl.ANY)] * len(carried)
    operands += list(carried)
    slab = pl.BlockSpec((rows, hidden), lambda e, c: (c[0], e))
    return launch(
        functools.partial(expert_kernel, step, len(carried)),
        [*operands],
        prefetch=1,
            grid=(EXPERTS,),
            in_specs=in_specs,
            out_specs=[
                pl.BlockSpec((hidden, rows), lambda e, c: (e, c[0])),
                slab,
                slab,
                pl.BlockSpec((full, rows), lambda e, c: (0, c[0])),
                pl.BlockSpec((blocks, rows, cols), lambda e, c: (0, c[0], 0)),
                pl.BlockSpec((rows, full + 128), lambda e, c: (0, 0)),
                pl.BlockSpec((rows, 128), lambda e, c: (0, 0)),
            ],
            scratch=[
                pltpu.VMEM((rows, full), F32),
                pltpu.VMEM((rows, full), F32),
                pltpu.VMEM((rows, 128), F32),
                pltpu.VMEM((rows, 128), F32),
            ],
        out_shape=[
            jax.ShapeDtypeStruct((EXPERTS * hidden, length), BF),
            jax.ShapeDtypeStruct((length, EXPERTS * hidden), BF),
            jax.ShapeDtypeStruct((length, EXPERTS * hidden), BF),
            jax.ShapeDtypeStruct((full, length), BF),
            jax.ShapeDtypeStruct((blocks, length, cols), BF),
            jax.ShapeDtypeStruct((rows, full + 128), BF),
            jax.ShapeDtypeStruct((rows, 128), F32),
        ],
        aliases=aliases,

        token=6,
    )


def arrange_kernel(owners_ref, *refs):
    blocks, (branch_ref, rows_ref, out_ref) = refs[:-3], refs[-3:]
    for k, ref in enumerate(blocks):
        rows_ref[owners_ref[k]] = ref[...]
    out_ref[...] = branch_ref[...]


def arrange(owners, blocks, branch):
    rows, width = blocks[0].shape
    full = branch.shape[1]
    chunk = rows // 4
    return launch(
        arrange_kernel,
        [owners, *blocks, branch],
        prefetch=1,
        grid=(4,),
        in_specs=[pl.BlockSpec((chunk, width), lambda g, o: (g, 0))] * len(blocks)
        + [pl.BlockSpec((chunk, full), lambda g, o: (g, 0))],
        out_specs=[
            pl.BlockSpec((len(blocks), chunk, width), lambda g, o: (0, g, 0)),
            pl.BlockSpec((chunk, full), lambda g, o: (g, 0)),
        ],
        out_shape=[
            jax.ShapeDtypeStruct((len(blocks), rows, width), BF),
            jax.ShapeDtypeStruct((rows, full), BF),
        ],
    )


def gate_up_kernel(n2t_ref, dg_ref, du_ref, out_ref):
    turned = n2t_ref[...]
    out_ref[0, 0] = dot(turned, dg_ref[...]).astype(BF)
    out_ref[1, 0] = dot(turned, du_ref[...]).astype(BF)


def gate_up_grads(n2t, dg, du):
    full, length = n2t.shape
    hidden = dg.shape[1] // EXPERTS
    slab = pl.BlockSpec((length, hidden), lambda e: (0, e))
    return launch(
        gate_up_kernel,
        [n2t, dg, du],
        grid=(EXPERTS,),
        in_specs=[pl.BlockSpec((full, length), lambda e: (0, 0)), slab, slab],
        out_specs=pl.BlockSpec((2, 1, full, hidden), lambda e: (0, e, 0, 0)),
        out_shape=jax.ShapeDtypeStruct((2, EXPERTS, full, hidden), BF),
    )


def down_kernel(table_ref, h2t_ref, cot_ref, out_ref):
    cols = cot_ref.shape[2]
    for t in range(cot_ref.shape[0]):
        out_ref[0, :, t * cols : (t + 1) * cols] = dot(h2t_ref[...], cot_ref[t]).astype(BF)


def down_grads(table, h2t, cot, n):
    wide, length = h2t.shape
    blocks, _, cols = cot.shape
    rows = wide // n
    steps = n // 2
    return launch(
        down_kernel,
        [table, h2t, cot],
        prefetch=1,
        grid=(steps,),
        in_specs=[
            pl.BlockSpec((rows, length), lambda g, t: (t[g], 0)),
            pl.BlockSpec((blocks, length, cols), lambda g, t: (0, 0, 0)),
        ],
        out_specs=pl.BlockSpec((1, rows, blocks * cols), lambda g, t: (g, 0, 0)),
        out_shape=jax.ShapeDtypeStruct((steps, rows, blocks * cols), BF),
    )


def middle_kernel(size, owners_ref, *refs):
    heads, x_refs = refs[:size], refs[size : 2 * size]
    wo_ref, gain_ref, res_ref, n2_ref = refs[2 * size :]
    step = pl.program_id(0)
    cols = x_refs[0].shape[1]
    width = heads[0].shape[1]

    @pl.when(step == 0)
    def _():
        for k, ref in enumerate(x_refs):
            first = pl.multiple_of(owners_ref[k] * cols, 128)
            res_ref[:, pl.ds(first, cols)] = ref[...].astype(F32)

    weights = wo_ref[...].reshape(width, -1)
    for k, ref in enumerate(heads):

        @pl.when(step == k)
        def _(ref=ref):
            res_ref[...] += dot(ref[...], weights)

    @pl.when(step == size - 1)
    def _():
        residual = res_ref[...]
        scale = lax.rsqrt(jnp.mean(residual * residual, axis=1, keepdims=True) + EPSILON)
        for t in range(size):
            here = slice(t * cols, (t + 1) * cols)
            gain = gain_ref[t, 1:2, :].astype(F32)
            n2_ref[:, here] = (residual[:, here] * scale * gain).astype(BF)


def middle(owners, attended, received, w_out, x_blocks, gains):
    size = len(x_blocks)
    groups, _, part, full = w_out.shape
    width, cols = groups * part, full // size
    rows = attended.shape[0] // size
    return launch(
        functools.partial(middle_kernel, size),
        [owners, attended, *received, *x_blocks, w_out, gains],
        prefetch=1,
        grid=(size,),
        in_specs=[pl.BlockSpec((rows, width), lambda t, o: (o[0], 0))]
        + [pl.BlockSpec((rows, width), lambda t, o: (0, 0))] * (size - 1)
        + [pl.BlockSpec((rows, cols), lambda t, o: (o[0], 0))] * size
        + [
            pl.BlockSpec((groups, 1, part, full), lambda t, o: (0, o[t], 0, 0)),
            pl.BlockSpec((size, 16, cols), lambda t, o: (0, 0, 0)),
        ],
        out_specs=[pl.BlockSpec((rows, full), lambda t, o: (0, 0))] * 2,
        out_shape=[
            jax.ShapeDtypeStruct((rows, full), F32),
            jax.ShapeDtypeStruct((rows, full), BF),
        ],
    )


def middle_back_kernel(
    mine_ref, own_ref, received_ref, probs_ref, router_ref, res_ref, n2_ref, cot_ref, gain_ref, wo_ref,
    branch_ref, out_ref, parts_ref,
):
    step = pl.program_id(0)
    blocks, rows, cols = cot_ref.shape
    full = blocks * cols

    @pl.when(step == 0)
    def _():
        probs = probs_ref[...]
        parts = own_ref[:, full:].astype(F32) + received_ref[:, full:].astype(F32)
        prob_grad = parts
        for group in range(1, 2 * blocks):
            prob_grad = prob_grad + pltpu.roll(parts, 128 - GROUP * group, 1)
        lane = lax.broadcasted_iota(jnp.int32, (rows, 128), 1)
        prob_grad = jnp.where(lane < EXPERTS, prob_grad, 0.0)
        centred = jnp.sum(prob_grad * probs, axis=1, keepdims=True)
        logit_grad = (probs * (prob_grad - centred)).astype(BF)
        grad = (
            own_ref[:, :full].astype(F32)
            + received_ref[:, :full].astype(F32)
            + dot_t(logit_grad, router_ref[...])
        )
        residual = res_ref[...]
        scale = lax.rsqrt(jnp.mean(residual * residual, axis=1, keepdims=True) + EPSILON)
        stat = jnp.zeros((rows, 1), F32)
        for t in range(blocks):
            here = slice(t * cols, (t + 1) * cols)
            gain = gain_ref[t, 1:2, :].astype(F32)
            stat = stat + jnp.sum(residual[:, here] * gain * grad[:, here], axis=1, keepdims=True)
        stat = scale * scale * scale * stat / full
        for t in range(blocks):
            here = slice(t * cols, (t + 1) * cols)
            gain = gain_ref[t, 1:2, :].astype(F32)
            branch_ref[:, here] = (
                cot_ref[t].astype(F32) + scale * gain * grad[:, here] - residual[:, here] * stat
            ).astype(BF)
        router_part = lax.dot_general(
            logit_grad, n2_ref[...], (((0,), (0,)), ((), ())), preferred_element_type=F32
        )[:8]
        norm_part = jnp.sum(grad * residual * scale, axis=0, keepdims=True)
        which = lax.broadcasted_iota(jnp.int32, (8, full), 0)
        parts_ref[...] = jnp.where(which == EXPERTS, norm_part, router_part)

    out_ref[0] = dot_t(branch_ref[...], wo_ref[...].reshape(-1, full)).astype(BF)


def middle_back(mine, own, received, probs, router, residual, n2, cot, gains, w_out):
    blocks, _, cols = cot.shape
    rows, full = residual.shape
    groups, _, part, _ = w_out.shape
    width = groups * part
    whole = pl.BlockSpec((rows, full), lambda t, m: (0, 0))
    wide = pl.BlockSpec((rows, full + 128), lambda t, m: (0, 0))
    lanes = pl.BlockSpec((rows, 128), lambda t, m: (0, 0))
    return launch(
        middle_back_kernel,
        [mine, own, received, probs, router, residual, n2, cot, gains, w_out],
        prefetch=1,
            grid=(blocks,),
            in_specs=[
                wide,
                wide,
                lanes,
                pl.BlockSpec((full, 128), lambda t, m: (0, 0)),
                whole,
                whole,
                pl.BlockSpec((blocks, rows, cols), lambda t, m: (0, m[0], 0)),
                pl.BlockSpec((blocks, 16, cols), lambda t, m: (0, 0, 0)),
                pl.BlockSpec((groups, 1, part, full), lambda t, m: (0, lax.rem(m[0] + t, blocks), 0, 0)),
            ],
            out_specs=[
                whole,
                pl.BlockSpec((1, rows, width), lambda t, m: (t, 0, 0)),
                pl.BlockSpec((8, full), lambda t, m: (0, 0)),
            ],
        out_shape=[
            jax.ShapeDtypeStruct((rows, full), BF),
            jax.ShapeDtypeStruct((blocks, rows, width), BF),
            jax.ShapeDtypeStruct((8, full), F32),
        ],
    )


def reversed_bits(at, bits):
    return sum(((at >> b) & 1) << (bits - 1 - b) for b in range(bits)) if bits else at


def column_grad_kernel(left_ref, right_ref, w_ref, out_ref, gain_ref):
    product = dot(jnp.transpose(left_ref[...]), right_ref[...])
    out_ref[...] = product.astype(BF)
    gain_ref[...] = jnp.broadcast_to(row_sums(product * w_ref[...].astype(F32)), gain_ref.shape)


def column_grads(left, right, weights):
    length, full = left.shape
    width = right.shape[1]
    piece = min(512, full)
    tile = pl.BlockSpec((piece, width), lambda g: (g, 0))
    return launch(
        column_grad_kernel,
        [left, right, weights],
        grid=(full // piece,),
        in_specs=[
            pl.BlockSpec((length, piece), lambda g: (0, g)),
            pl.BlockSpec((length, width), lambda g: (0, 0)),
            tile,
        ],
        out_specs=[tile, pl.BlockSpec((8, piece), lambda g: (0, g))],
        out_shape=[
            jax.ShapeDtypeStruct((full, width), BF),
            jax.ShapeDtypeStruct((8, full), F32),
        ],
    )


def row_grad_kernel(rows_ref, left_ref, *rest):
    blocks, (out_ref, turned_left) = rest[:-2], rest[-2:]
    rows = blocks[0].shape[0]

    @pl.when(pl.program_id(0) == 0)
    def _():
        for k in range(len(blocks)):
            first = pl.multiple_of(rows_ref[k] * rows, rows)
            turned_left[:, k * rows : (k + 1) * rows] = jnp.transpose(
                left_ref[pl.ds(first, rows), :]
            )

    total = None
    for k, block in enumerate(blocks):
        term = dot(turned_left[:, k * rows : (k + 1) * rows], block[...])
        total = term if total is None else total + term
    out_ref[...] = total.astype(BF)


def row_grads(owners, left, blocks):
    length, width = left.shape
    rows, full = blocks[0].shape
    piece = min(512, full)
    return launch(
        row_grad_kernel,
        [owners, left, *blocks],
        prefetch=1,
        grid=(full // piece,),
        in_specs=[pl.BlockSpec((length, width), lambda g, o: (0, 0))]
        + [pl.BlockSpec((rows, piece), lambda g, o: (0, g))] * len(blocks),
        out_specs=pl.BlockSpec((width, piece), lambda g, o: (0, g)),
        out_shape=jax.ShapeDtypeStruct((width, full), BF),
        scratch=[pltpu.VMEM((width, length), BF)],
    )


def input_kernel(owner_ref, grad_ref, w_ref, *rest):
    total = dot_t(grad_ref[...], w_ref[...])
    if len(rest) == 2:
        total = total + rest[0][...].astype(F32)
    rest[-1][...] = total.astype(BF)


def input_grads(owner, cols, grad, w_all, received=None, work=1):
    length, width = grad.shape
    rows = min(256, length)
    tile = pl.BlockSpec((rows, cols), lambda g, o: (g, 0))
    return launch(
        input_kernel,
        [owner, grad, w_all, *([] if received is None else [received])],
        prefetch=1,
            grid=(length // rows,),
            in_specs=[
                pl.BlockSpec((rows, width), lambda g, o: (g, 0)),
                pl.BlockSpec((cols, width), lambda g, o: (o[0], 0)),
            ]
            + ([] if received is None else [tile]),
            out_specs=tile,
        out_shape=jax.ShapeDtypeStruct((length, cols), BF),

        work=work,
    )


def mix_kernel(owner_ref, mix_ref, *rest):
    if len(rest) == 1:
        rest[0][...] = mix_ref[0]
    else:
        rest[1][...] = added(mix_ref[0], rest[0][...])


def mix_block(owner, mix, received=None, work=1):
    blocks, length, cols = mix.shape
    chunk = length // 4
    tile = pl.BlockSpec((chunk, cols), lambda g, o: (g, 0))
    return launch(
        mix_kernel,
        [owner, mix, *([] if received is None else [received])],
        prefetch=1,
            grid=(4,),
            in_specs=[pl.BlockSpec((1, chunk, cols), lambda g, o: (o[0], g, 0))]
            + ([] if received is None else [tile]),
            out_specs=tile,
        out_shape=jax.ShapeDtypeStruct((length, cols), BF),
        work=work,
    )


def final_kernel(
    full, owners_ref, grad_ref, w_ref, received_ref, tokens_ref, sums_ref, stat_ref, gain_ref, *rest
):
    blocks, out_ref = rest[:-1], rest[-1]
    step = pl.program_id(0)
    branch = blocks[0][...]
    for k in range(1, len(blocks)):
        branch = jnp.where(step == k, blocks[k][...], branch)
    scale = lax.rsqrt(sums_ref[...] / full + EPSILON)
    scale_one = jnp.transpose(scale)[:, 2:3]
    stat = jnp.transpose(stat_ref[...])[:, 0:1] / full * scale_one * scale_one
    normed_grad = dot_t(grad_ref[...], w_ref[...]) + received_ref[...].astype(F32)
    out_ref[...] = (
        branch.astype(F32)
        + scale_one * gain_ref[...].astype(F32) * normed_grad
        - tokens_ref[...].astype(F32) * stat
    )


def final_grads(owners, grad, w_all, received, tokens, sums, stat, gain, blocks):
    length, cols = tokens.shape
    width = grad.shape[1]
    rows = length // len(blocks)
    tile = pl.BlockSpec((rows, cols), lambda k, o: (o[k], 0))
    line = pl.BlockSpec((8, rows), lambda k, o: (0, o[k]))
    return launch(
        functools.partial(final_kernel, cols * len(blocks)),
        [owners, grad, w_all, received, tokens, sums, stat, gain, *blocks],
        prefetch=1,
            grid=(len(blocks),),
            in_specs=[
                pl.BlockSpec((rows, width), lambda k, o: (o[k], 0)),
                pl.BlockSpec((cols, width), lambda k, o: (o[0], 0)),
                tile,
                tile,
                line,
                line,
                pl.BlockSpec((1, cols), lambda k, o: (0, 0)),
            ]
            + [pl.BlockSpec((rows, cols), lambda k, o: (0, o[0]))] * len(blocks),
            out_specs=tile,
        out_shape=jax.ShapeDtypeStruct((length, cols), F32),
    )


def piece_specs(shape, steps):
    block = (1,) + shape
    return [
        pl.BlockSpec(block, lambda a, pos: (jnp.minimum(pos[a], steps - 1), 0, 0)),
        pl.BlockSpec(block, lambda a, pos: (jnp.maximum(pos[a] - steps, 0), 0, 0)),
    ]


def pieces_kernel(steps, pos_ref, low_ref, high_ref, out_ref):
    low = pos_ref[pl.program_id(0)] < steps
    out_ref[...] = jnp.where(low, low_ref[0].astype(F32), high_ref[0].astype(F32))


def widen_pieces(pos, halves, n):
    steps, rows, width = halves[0].shape
    return launch(
        functools.partial(pieces_kernel, steps),
        [pos, *halves],
        prefetch=1,
        grid=(n,),
        in_specs=piece_specs((rows, width), steps),
        out_specs=pl.BlockSpec((rows, width), lambda a, pos: (a, 0)),
        out_shape=jax.ShapeDtypeStruct((rows * n, width), F32),
    )


def projections_kernel(sum_ref, q_ref, k_ref, v_ref):
    width = q_ref.shape[1]
    for at, out_ref in enumerate((q_ref, k_ref, v_ref)):
        out_ref[...] = sum_ref[:, at * width : (at + 1) * width].astype(F32)


def widen_projections(total):
    full, width = total.shape
    out = width // 3
    piece = min(256, full)
    tile = pl.BlockSpec((piece, out), lambda g: (g, 0))
    return launch(
        projections_kernel,
        [total],
        grid=(full // piece,),
        in_specs=[pl.BlockSpec((piece, width), lambda g: (g, 0))],
        out_specs=[tile] * 3,
        out_shape=[jax.ShapeDtypeStruct((full, out), F32)] * 3,
    )


def experts_kernel(held_ref, gate_ref, up_ref):
    gate_ref[0] = held_ref[0, 0].astype(F32)
    up_ref[0] = held_ref[1, 0].astype(F32)


def widen_experts(held):
    _, experts, full, hidden = held.shape
    tall = pl.BlockSpec((1, full, hidden), lambda e: (e, 0, 0))
    return launch(
        experts_kernel,
        [held],
        grid=(experts,),
        in_specs=[pl.BlockSpec((2, 1, full, hidden), lambda e: (0, e, 0, 0))],
        out_specs=[tall, tall],
        out_shape=[jax.ShapeDtypeStruct((experts, full, hidden), F32)] * 2,
    )


def kept_experts(routes, order):
    length = routes.shape[0]
    token, which = order // TOP, order % TOP
    onehot = (token[:, None] == jnp.arange(length, dtype=jnp.int32)[None, :]).astype(BF)
    named = (routes[:, :, None] == jnp.arange(8, dtype=jnp.int32)).astype(BF).reshape(length, TOP * 8)
    ordered = dot(onehot, named).reshape(-1, TOP, 8)
    choose = jnp.sum(
        jnp.where(which[:, None, None] == jnp.arange(TOP)[None, :, None], ordered, 0.0), axis=1
    )
    kept = jnp.where(jnp.cumsum(choose, axis=0) <= CAP, choose, 0.0).astype(BF)
    kept = jnp.pad(kept, ((0, 0), (0, 120)))
    return lax.dot_general(onehot, kept, (((0,), (0,)), ((), ())), preferred_element_type=F32)


def on_device(
    tokens, cotangent, norm1_gain, w_query, w_key, w_value, query_gain, key_gain, w_output,
    norm2_gain, router, w_gate, w_up, w_down, routes, prefix, slot_order,
):
    size, n = lax.axis_size("tensor"), lax.axis_size("dp")
    mine, group = lax.axis_index("tensor"), lax.axis_index("dp")
    length, cols = tokens.shape
    full = cols * size
    rows = length // size
    steps = range(1, size)
    Chain.token = None

    def add(*terms):
        return functools.reduce(jnp.add, terms)

    here = mine.astype(jnp.int32)[None]

    rel = rel_table(swap_masks(n))
    table = jnp.asarray(rel, jnp.int32) ^ group
    positions = jnp.asarray([rel.index(v) for v in range(n)], jnp.int32)[
        jnp.arange(n, dtype=jnp.int32) ^ group
    ]
    half = n // 2
    owners = ((mine - jnp.arange(size)) % size).astype(jnp.int32)

    def owner(step):
        return owners[step : step + 1]

    def by_owner(own, *others):
        return place(size, [b[None] for b in others], mine, own[None])

    part = w_output.shape[0] // n
    gains = jnp.concatenate([norm1_gain[None], norm2_gain[None], jnp.zeros((14, cols), BF)])
    w_piece = jnp.concatenate(
        [
            lax.dynamic_slice_in_dim(w_output, group * part, part, 0),
            jnp.pad(gains, ((0, 0), (0, full - cols))),
        ]
    )
    w_blocks, x_blocks = [w_piece], [tokens]
    for step in steps:
        w_blocks.append(send(w_blocks[-1], 1, size))
    w_mixed = by_owner(*w_blocks)
    w_out = lax.all_gather(w_mixed[:, :part], "dp", axis=0)
    gains = w_mixed[:, part:, :cols]
    w_all = side_by_side([w_query, w_key, w_value])
    keep = kept_experts(routes, slot_order[0])
    router_wide = jnp.pad(router, ((0, 0), (0, 128 - EXPERTS)))
    halfway = HEAD_DIM // 2
    freqs = ROPE_BASE ** (-(jnp.arange(halfway, dtype=F32) * 2.0 / HEAD_DIM))
    angles = jnp.arange(length, dtype=F32)[:, None] * freqs[None, :]
    cosine = jnp.concatenate([jnp.cos(angles)] * 2, axis=1)
    sine = jnp.concatenate([-jnp.sin(angles), jnp.sin(angles)], axis=1)
    for step in steps:
        x_blocks.append(send(x_blocks[-1], 1, size))
    late_cot = copied(cotangent, (x_blocks[-1], keep, router_wide, cosine, sine))
    cot = lax.all_gather(late_cot, "tensor", axis=0)
    normed_one, q_pre, k_pre, v_rows, own_sums = qkv_call(
        owners, x_blocks, gains, w_query, w_key, w_value
    )
    sums = [own_sums] + [send(own_sums, step, size) for step in steps]

    gq, gk = query_gain[None], key_gain[None]
    attended, lse, q_rot, k_rot = attn_forward(
        prefix, q_pre, k_pre, v_rows, gq, gk, cosine, sine, sums
    )

    received = [
        send(lax.dynamic_slice_in_dim(attended, (mine + step) % size * rows, rows, 0), step, size)
        for step in steps
    ]
    residual, normed_two = middle(owners, attended, received, w_out, x_blocks, gains)

    def add_wide(a, b, work=1):
        return add_blocks(a[None], b[None], work)[0]

    chunks = [copied(normed_two, (cot,))]
    chunks.append(send(chunks[0], 1, size))
    carried, later, dn2_flying = (), [], None
    for step in range(size):
        outs = expert_call(
            step, owner(step), chunks[step], cot, router_wide, keep, w_gate, w_up, w_down,
            residual if step == 0 else None, carried,
        )
        carried = outs[:5]
        if step < size - 2:
            chunks.append(send(copied(chunks[-1]), 1, size))
        if step == 0:
            own_dn2, expert_probs = outs[5:]
        else:
            later.append(outs[5])
        if step > 3:
            dn2_flying = send(add_wide(later.pop(0), dn2_flying), 1, size)
        elif step == min(3, size - 1):
            dn2_flying = send(copied(later.pop(0)), 1, size)
    h2t, dg, du, n2t, mix = carried

    expert_grads = lax.psum(gate_up_grads(n2t, dg, du), "dp")
    dn2_flying = send(add_wide(later.pop(0), dn2_flying, LONG), 1, size)
    sum_down = Sum(n, 2, down_grads(table[half:], h2t, cot, n))
    sum_down.keep = down_grads(table[:half], h2t, cot, n)
    for term in later:
        dn2_flying = send(add_wide(term, dn2_flying), 1, size)
    sum_down.step()

    branch_rows, out_rows, small = middle_back(
        here, own_dn2, dn2_flying, expert_probs, router_wide, residual, normed_two, cot, gains, w_out
    )

    received = [send(out_rows[step], step, size) for step in steps]
    out_grad, branch_rows = arrange(owners, [out_rows[0]] + received, branch_rows)
    branch_blocks = [branch_rows, send(branch_rows, 1, size)]
    dq, dk, dv, gain_grads, own_back = attn_backward(
        prefix, q_pre, k_pre, q_rot, k_rot, v_rows, out_grad.reshape(length, -1), lse, gq, gk,
        cosine, sine, sums,
    )
    back = [own_back] + [send(own_back, step, size) for step in steps]
    sum_down.step()
    grad_qkv, stat_one, branch_copy = norm_back(
        q_pre, k_pre, dq, dk, dv, gq, gk, branch_blocks[1], sums, back
    )
    branch_blocks.append(send(branch_copy, 1, size))
    in_grads, gain_part = column_grads(normed_one, grad_qkv, w_all)
    small = jnp.concatenate([small[:7], gain_part[7:]])
    small = add(small, *[send(small, step, size) for step in steps])
    dn1 = input_grads(owner(1), cols, grad_qkv, w_all)
    branch_copy, dn1 = copied_pair(branch_blocks[2], dn1, 1)
    branch_blocks.append(send(branch_copy, 1, size))
    dn1_flying = send(dn1, 1, size)
    sum_down.step()
    for step in range(4, size):
        branch_blocks.append(send(copied(branch_blocks[-1]), 1, size))
    out_grads = row_grads(owners, attended, branch_blocks)
    packed = jnp.concatenate([small, gain_grads], axis=1)
    width = 3 * w_query.shape[1]
    extra = jnp.pad(packed.reshape(-1), (0, 32 * width - packed.size)).astype(BF).reshape(32, width)
    extra = copied(extra, (expert_grads,))
    in_grads, out_grads, extra = lax.psum((in_grads, out_grads, extra), "dp")
    mix_flying = send(mix_block(owner(1), mix, work=LONG), 1, size)
    for step in range(2, size):
        dn1_flying = send(input_grads(owner(step), cols, grad_qkv, w_all, dn1_flying), 1, size)
        sum_down.step()
        mix_flying = send(mix_block(owner(step), mix, mix_flying), 1, size)
    for _ in range(2 * len(swap_masks(n))):
        sum_down.step()

    grad_tokens = final_grads(
        owners, grad_qkv, w_all, dn1_flying, tokens, own_sums, stat_one, norm1_gain[None],
        branch_blocks,
    )
    grad_gate, grad_up = widen_experts(expert_grads)
    grad_down = widen_pieces(positions, sum_down.finish(), n).reshape(w_down.shape)

    mixed = mix_block(owner(0), mix, mix_flying)
    grad_query, grad_key, grad_value = widen_projections(in_grads)
    packed = extra.astype(F32).reshape(-1)[: packed.size].reshape(packed.shape)
    gain_total, packed = packed[:2, full:], packed[:, :full]
    grad_output = out_grads.astype(F32)

    grad_router = packed[:EXPERTS].T
    own = lax.dynamic_slice_in_dim(packed[EXPERTS:], mine * cols, cols, 1)
    grad_norm2_gain = own[0]
    grad_norm1_gain = own[1] / norm1_gain.astype(F32)
    grad_query_gain, grad_key_gain = gain_total[0], gain_total[1]
    return (
        mixed, grad_tokens, grad_norm1_gain, grad_query, grad_key, grad_value, grad_query_gain,
        grad_key_gain, grad_output, grad_norm2_gain, grad_router, grad_gate, grad_up, grad_down,
    )


def solution(mesh):
    rows, weight_cols, weight_rows = P("dp", "tensor"), P(None, "tensor"), P("tensor", None)
    vector, expert_cols, expert_rows = P("tensor"), P(None, None, "tensor"), P(None, "tensor", None)
    return jax.shard_map(
        on_device,
        mesh=mesh,
        in_specs=(
            rows, rows, vector, weight_cols, weight_cols, weight_cols, vector, vector, weight_rows,
            vector, P(), expert_cols, expert_cols, expert_rows, P("dp", None), P("dp"),
            P("dp", None),
        ),
        out_specs=(
            rows, rows, vector, weight_cols, weight_cols, weight_cols, vector, vector, weight_rows,
            vector, P(), expert_cols, expert_cols, expert_rows,
        ),
        check_vma=False,
    )
```

```python
import functools

import jax
import jax.numpy as jnp
from jax import lax
from jax.experimental import pallas as pl
from jax.experimental.pallas import tpu as pltpu
from jax.sharding import PartitionSpec as P

HEAD_DIM = 128
EXPERTS = 6
TOP = 3
CAP = 640
PREFIX_MAX = 512

EPSILON = 1e-05
ROPE_BASE = 10000.0
MASKED = -1e30
GROUP = 8
LONG = 2e13
BF = jnp.bfloat16
F32 = jnp.float32
VMEM_LIMIT = 56 * 1024 * 1024


class Chain:
    token = None


def launch(
    body, operands, *, grid, in_specs, out_specs, out_shape, work=1, prefetch=0, scratch=(), aliases=None,
    token=0, others=(),
):
    operands = list(operands)
    unread = [field for field in (Chain.token, *others) if field is not None]
    unread = [field for field in unread if all(field is not own for own in operands)]
    first, last = len(operands), len(operands) + len(unread)

    def kernel(*refs):
        body(*refs[:first], *refs[last:])

    out = pl.pallas_call(
        kernel,
        grid_spec=pltpu.PrefetchScalarGridSpec(
            num_scalar_prefetch=prefetch,
            grid=grid,
            in_specs=list(in_specs) + [pl.BlockSpec(memory_space=pl.ANY)] * len(unread),
            out_specs=out_specs,
            scratch_shapes=list(scratch),
        ),
        out_shape=out_shape,
        input_output_aliases=aliases or {},
        compiler_params=pltpu.CompilerParams(vmem_limit_bytes=VMEM_LIMIT),
        cost_estimate=pl.CostEstimate(flops=int(work), bytes_accessed=1, transcendentals=0),
    )(*operands, *unread)
    Chain.token = out[token] if isinstance(out, (list, tuple)) else out
    return out


def dot(a, b):
    return jnp.dot(a, b, preferred_element_type=F32)


def dot_t(a, b):
    return lax.dot_general(a, b, (((1,), (1,)), ((), ())), preferred_element_type=F32)


def row_sums(field):
    folded = field[:, :128]
    for at in range(128, field.shape[1], 128):
        folded = folded + field[:, at : at + 128]
    return jnp.sum(jnp.transpose(folded), axis=0, keepdims=True)


def ring(size):
    return [(at, (at + 1) % size) for at in range(size)]


def send(value, step, size):
    return lax.ppermute(value, "tensor", [(at, (at + step) % size) for at in range(size)])


def swap(value, mask, n):
    return lax.ppermute(value, "dp", [(at, at ^ mask) for at in range(n)])


def take(blocks, at):
    return lax.dynamic_slice_in_dim(blocks, at, 1, 0)


def place(size, received, mine, own):
    out = lax.dynamic_update_slice_in_dim(jnp.zeros((size,) + own.shape[1:], own.dtype), own, mine, 0)
    for step, block in enumerate(received, 1):
        out = lax.dynamic_update_slice_in_dim(out, block, (mine - step) % size, 0)
    return out


def swap(field, mask, n):
    return lax.ppermute(field, "dp", [(at, at ^ mask) for at in range(n)])


def swap_masks(n):
    return [1 << bit for bit in range(n.bit_length() - 1)]


def rel_table(masks):
    bits = len(masks)
    return [
        sum(masks[s] for s in range(bits) if (p >> (bits - 1 - s)) & 1) for p in range(1 << bits)
    ]


def blockwise(body, ins, outs, others=(), work=1):
    chunks = max(c for c in (1, 2, 3, 4) if ins[0].shape[1] % (16 * c) == 0)

    def spec(shape):
        return pl.BlockSpec((shape[0], shape[1] // chunks, shape[2]), lambda g: (0, g, 0))

    def kernel(*refs):
        body(refs[: len(ins)], refs[len(ins) :])

    return launch(
        kernel,
        [*ins],
        grid=(chunks,),
        in_specs=[spec(field.shape) for field in ins],
        out_specs=[spec(shape) for shape in outs],
        out_shape=[jax.ShapeDtypeStruct(shape, BF) for shape in outs],
        others=others,
        work=work,
    )


def added(a, b):
    return (a.astype(F32) + b.astype(F32)).astype(BF)


def copied(field, others=()):
    def body(ins, outs):
        outs[0][...] = ins[0][...]

    return blockwise(body, [field[None]], [(1,) + field.shape], others)[0][0]


def side_by_side(fields):
    def body(ins, outs):
        at = 0
        for ref in ins:
            outs[0][:, :, at : at + ref.shape[2]] = ref[...]
            at += ref.shape[2]

    width = sum(field.shape[1] for field in fields)
    return blockwise(body, [field[None] for field in fields], [(1, fields[0].shape[0], width)])[0][0]


def add_blocks(a, b, work=1):
    def body(ins, outs):
        outs[0][...] = added(ins[0][...], ins[1][...])

    return blockwise(body, [a, b], [a.shape], work=work)[0]


class Sum:
    def __init__(self, n, parts, first):
        self.n, self.parts = n, parts
        self.masks = swap_masks(n)
        self.stage = 0
        self.flying = [swap(first, self.masks[0], n)]

    def send(self, fields, stage):
        self.flying = []
        for part, field in enumerate(fields):
            mask = self.masks[stage] if part == 0 else self.masks[-stage]
            self.flying.append(swap(field, mask, self.n))

    def split(self, keeps, received):
        count, rows, width = keeps[0].shape
        wide = width // self.parts if len(keeps) < self.parts else width

        def body(ins, outs):
            for part in range(self.parts):
                at = part if len(keeps) == self.parts else 0
                here = slice(part * wide, (part + 1) * wide) if at != part else slice(0, wide)
                for i in range(count):
                    total = added(ins[2 * at][i, :, here], ins[2 * at + 1][i, :, here])
                    if part == 0:
                        away, place_at = i >= count // 2, i % (count // 2)
                    else:
                        away, place_at = i % 2 == 1, i // 2
                    outs[2 * part + (0 if away else 1)][place_at] = total

        ins = [field for pair in zip(keeps, received, strict=True) for field in pair]
        outs = blockwise(body, ins, [(count // 2, rows, wide)] * (2 * self.parts))
        return outs[0::2], outs[1::2]

    def total(self, keeps, received):
        def body(ins, outs):
            for part, out in enumerate(outs):
                out[...] = added(ins[2 * part][...], ins[2 * part + 1][...])

        ins = [field for pair in zip(keeps, received, strict=True) for field in pair]
        return blockwise(body, ins, [field.shape for field in keeps])

    def joined(self, last, keeps, received):
        count, rows, wide = keeps[0].shape

        def body(ins, outs):
            for part in range(self.parts):
                out = outs[0] if last else outs[part]
                here = slice(part * wide, (part + 1) * wide) if last else slice(0, wide)
                for i in range(count):
                    low, high = (i, count + i) if part == 0 else (2 * i, 2 * i + 1)
                    out[low, :, here] = ins[2 * part][i]
                    out[high, :, here] = ins[2 * part + 1][i]

        ins = [field for pair in zip(keeps, received, strict=True) for field in pair]
        if last:
            return blockwise(body, ins, [(2 * count, rows, wide * self.parts)])
        return blockwise(body, ins, [(2 * count, rows, wide)] * self.parts)

    def step(self):
        bits = len(self.masks)
        if self.stage == 2 * bits - 1:
            return
        received = self.flying
        self.stage += 1
        if self.stage < bits:
            keep = [self.keep] if self.stage == 1 else self.keep
            away, self.keep = self.split(keep, received)
            self.send(away, self.stage)
            return
        back = 2 * bits - 1 - self.stage
        if self.stage == bits:
            self.keep = self.total(self.keep, received)
        else:
            self.keep = self.joined(back == 0, self.keep, received)
        if back:
            self.send(self.keep, back)
        else:
            self.keep = self.keep[0]
            self.flying = [swap(self.keep, self.masks[0], self.n)]

    def finish(self):
        return self.keep, self.flying[0]


def qkv_kernel(owners_ref, *refs):
    blocks, refs = refs[:-9], refs[-9:]
    gain_ref, wq_ref, wk_ref, wv_ref, n1_ref, q_ref, k_ref, v_ref, sums_ref = refs
    rows, cols = blocks[0].shape
    full = len(blocks) * cols
    fields = [block[...].astype(F32) for block in blocks]
    squares = fields[0] * fields[0]
    for field in fields[1:]:
        squares = squares + field * field
    scale = lax.rsqrt(jnp.sum(squares, axis=1, keepdims=True) / full + EPSILON)
    for k, field in enumerate(fields):
        at = owners_ref[k]
        gain = gain_ref[at, 0:1, :].astype(F32)
        first = pl.multiple_of(at * cols, 128)
        n1_ref[:, pl.ds(first, cols)] = (field * scale * gain).astype(BF)
    normed = n1_ref[...]
    query = dot(normed, wq_ref[...])
    key = dot(normed, wk_ref[...])
    q_ref[...] = query
    k_ref[...] = key
    v_ref[...] = dot(normed, wv_ref[...]).astype(BF)
    which = lax.broadcasted_iota(jnp.int32, (8, rows), 0)
    sums_ref[...] = jnp.where(
        which == 0,
        row_sums(query * query),
        jnp.where(which == 1, row_sums(key * key), row_sums(squares)),
    )


def qkv_call(owners, blocks, gains, wq, wk, wv):
    length, cols = blocks[0].shape
    full = cols * len(blocks)
    out = wq.shape[1]
    rows = min(256, length)
    whole = pl.BlockSpec((full, out), lambda g, o: (0, 0))
    tile = pl.BlockSpec((rows, out), lambda g, o: (g, 0))
    return launch(
        qkv_kernel,
        [owners, *blocks, gains, wq, wk, wv],
        prefetch=1,
        grid=(length // rows,),
        in_specs=[pl.BlockSpec((rows, cols), lambda g, o: (g, 0))] * len(blocks)
        + [pl.BlockSpec((len(blocks), 16, cols), lambda g, o: (0, 0, 0)), whole, whole, whole],
        out_specs=[
            pl.BlockSpec((rows, full), lambda g, o: (g, 0)),
            tile,
            tile,
            tile,
            pl.BlockSpec((8, rows), lambda g, o: (0, g)),
        ],
        out_shape=[
            jax.ShapeDtypeStruct((length, full), BF),
            jax.ShapeDtypeStruct((length, out), F32),
            jax.ShapeDtypeStruct((length, out), F32),
            jax.ShapeDtypeStruct((length, out), BF),
            jax.ShapeDtypeStruct((8, length), F32),
        ],
    )


def head_scales(sums_refs, full):
    total = sums_refs[0][...]
    for ref in sums_refs[1:]:
        total = total + ref[...]
    return jnp.transpose(lax.rsqrt(total / full + EPSILON))


def masked_scores(query, key, first, prefix):
    scores = dot_t(query, key) * (HEAD_DIM**-0.5)
    row = first + lax.broadcasted_iota(jnp.int32, scores.shape, 0)
    col = lax.broadcasted_iota(jnp.int32, scores.shape, 1)
    return jnp.where((col <= row) | (col < prefix), scores, MASKED)


def attn_forward_kernel(full, size, prefix_ref, q_ref, k_ref, v_ref, gq_ref, gk_ref, cos_ref, sin_ref, *rest):
    sums_refs, (att_ref, lse_ref, qr_ref, kr_ref) = rest[:size], rest[size:]
    length = q_ref.shape[0]
    rows = min(256, length)
    scales = head_scales(sums_refs, full)
    cosine, sine = cos_ref[...], sin_ref[...]
    for pre_ref, gain_ref, out_ref, at in ((q_ref, gq_ref, qr_ref, 0), (k_ref, gk_ref, kr_ref, 1)):
        field = pre_ref[...] * scales[:, at : at + 1] * gain_ref[...].astype(F32)
        out_ref[...] = (field * cosine + pltpu.roll(field, HEAD_DIM // 2, 1) * sine).astype(BF)
    prefix = prefix_ref[0]
    for first in range(0, length, rows):
        last = min(length, max(PREFIX_MAX, first + rows))
        scores = masked_scores(qr_ref[first : first + rows, :], kr_ref[:last, :], first, prefix)
        highest = jnp.max(scores, axis=1, keepdims=True)
        exponent = jnp.exp(scores - highest)
        total = jnp.sum(exponent, axis=1, keepdims=True)
        mixed = dot(exponent.astype(BF), v_ref[:last, :])
        att_ref[first : first + rows, :] = (mixed / total).astype(BF)
        lse_ref[first : first + rows, :] = jnp.broadcast_to(
            highest + jnp.log(total), (rows, HEAD_DIM)
        )


def attn_forward(prefix, q_pre, k_pre, v_rows, gq, gk, cosine, sine, sums):
    length, width = q_pre.shape
    full = width * len(sums)
    head = pl.BlockSpec((length, HEAD_DIM), lambda h, *_: (0, h))
    gain = pl.BlockSpec((1, HEAD_DIM), lambda h, *_: (0, h))
    table = pl.BlockSpec((length, HEAD_DIM), lambda h, *_: (0, 0))
    sums_spec = pl.BlockSpec((8, length), lambda h, *_: (0, 0))
    return launch(
        functools.partial(attn_forward_kernel, full, len(sums)),
        [prefix, q_pre, k_pre, v_rows, gq, gk, cosine, sine, *sums],
        prefetch=1,
            grid=(width // HEAD_DIM,),
            in_specs=[head, head, head, gain, gain, table, table] + [sums_spec] * len(sums),
            out_specs=[head] * 4,
        out_shape=[
            jax.ShapeDtypeStruct((length, width), BF),
            jax.ShapeDtypeStruct((length, width), F32),
            jax.ShapeDtypeStruct((length, width), BF),
            jax.ShapeDtypeStruct((length, width), BF),
        ],
    )


def attn_backward_kernel(
    full, size, prefix_ref, q_ref, k_ref, qr_ref, kr_ref, v_ref, do_ref, lse_ref, gq_ref, gk_ref,
    cos_ref, sin_ref, *rest,
):
    sums_refs, rest = rest[:size], rest[size:]
    dq_ref, dk_ref, dv_ref, gains_ref, rows_ref, kacc, vacc = rest
    head = pl.program_id(0)
    length = q_ref.shape[0]
    rows = min(256, length)
    prefix = prefix_ref[0]
    factor = HEAD_DIM**-0.5
    kacc[...] = jnp.zeros_like(kacc)
    vacc[...] = jnp.zeros_like(vacc)
    contract = (((0,), (0,)), ((), ()))
    for first in range(0, length, rows):
        last = min(length, max(PREFIX_MAX, first + rows))
        here = slice(first, first + rows)
        scores = masked_scores(qr_ref[here, :], kr_ref[:last, :], first, prefix)
        weights = jnp.exp(scores - lse_ref[here, 0:1])
        grad_rows = do_ref[here, :]
        weight_grad = dot_t(grad_rows, v_ref[:last, :])
        centred = jnp.sum(weight_grad * weights, axis=1, keepdims=True)
        score_grad = (weights * (weight_grad - centred)).astype(BF)
        dq_ref[here, :] = dot(score_grad, kr_ref[:last, :]) * factor
        kacc[:last, :] += lax.dot_general(
            score_grad, qr_ref[here, :], contract, preferred_element_type=F32
        )
        vacc[:last, :] += lax.dot_general(
            weights.astype(BF), grad_rows, contract, preferred_element_type=F32
        )
    dv_ref[...] = vacc[...].astype(BF)
    scales = head_scales(sums_refs, full)
    cosine, sine = cos_ref[...], sin_ref[...]
    which = lax.broadcasted_iota(jnp.int32, (8, length), 0)
    lanes = lax.broadcasted_iota(jnp.int32, (8, HEAD_DIM), 0)
    row_terms = jnp.zeros((8, length), F32)
    gain_terms = jnp.zeros((8, HEAD_DIM), F32)
    for at, (pre_ref, gain_ref, out_ref, raw) in enumerate(
        ((q_ref, gq_ref, dq_ref, dq_ref[...]), (k_ref, gk_ref, dk_ref, kacc[...] * factor))
    ):
        raw = raw.astype(BF).astype(F32)
        normed_grad = raw * cosine - pltpu.roll(raw, HEAD_DIM // 2, 1) * sine
        out_ref[...] = normed_grad
        product = normed_grad * pre_ref[...]
        row_terms = jnp.where(
            which == at, row_sums(product * gain_ref[...].astype(F32)), row_terms
        )
        gain_terms = jnp.where(
            lanes == at,
            jnp.sum(product * scales[:, at : at + 1], axis=0, keepdims=True),
            gain_terms,
        )
    gains_ref[...] = gain_terms
    product = dv_ref[...].astype(F32) * v_ref[...].astype(F32)
    row_terms = jnp.where(which == 2, row_sums(product), row_terms)

    @pl.when(head == 0)
    def _():
        rows_ref[...] = row_terms

    @pl.when(head > 0)
    def _():
        rows_ref[...] += row_terms


def attn_backward(
    prefix, q_pre, k_pre, q_rot, k_rot, v_rows, out_grad, lse, gq, gk, cosine, sine, sums, others=()
):
    length, width = q_pre.shape
    full = width * len(sums)
    head = pl.BlockSpec((length, HEAD_DIM), lambda h, *_: (0, h))
    gain = pl.BlockSpec((1, HEAD_DIM), lambda h, *_: (0, h))
    table = pl.BlockSpec((length, HEAD_DIM), lambda h, *_: (0, 0))
    sums_spec = pl.BlockSpec((8, length), lambda h, *_: (0, 0))
    return launch(
        functools.partial(attn_backward_kernel, full, len(sums)),
        [prefix, q_pre, k_pre, q_rot, k_rot, v_rows, out_grad, lse, gq, gk, cosine, sine, *sums],
        prefetch=1,
            grid=(width // HEAD_DIM,),
            in_specs=[head] * 7 + [gain, gain, table, table] + [sums_spec] * len(sums),
            out_specs=[head, head, head, pl.BlockSpec((8, HEAD_DIM), lambda h, *_: (0, h)), sums_spec],
            scratch=[pltpu.VMEM((length, HEAD_DIM), F32)] * 2,
        out_shape=[
            jax.ShapeDtypeStruct((length, width), F32),
            jax.ShapeDtypeStruct((length, width), F32),
            jax.ShapeDtypeStruct((length, width), BF),
            jax.ShapeDtypeStruct((8, width), F32),
            jax.ShapeDtypeStruct((8, length), F32),
        ],
        others=others,
    )


def norm_back_kernel(full, size, q_ref, k_ref, dq_ref, dk_ref, dv_ref, gq_ref, gk_ref, *rest):
    sums_refs, back_refs, (out_ref, stat_ref) = rest[:size], rest[size : 2 * size], rest[2 * size :]
    width = q_ref.shape[1]
    scales = head_scales(sums_refs, full)
    back = back_refs[0][...]
    squares = sums_refs[0][...]
    for ref, sums_ref in zip(back_refs[1:], sums_refs[1:], strict=True):
        back = back + ref[...]
        squares = squares + sums_ref[...]
    scale = lax.rsqrt(squares / full + EPSILON)
    along = scale * back - scale * scale * scale * (back / full) * squares
    stat_ref[...] = jnp.broadcast_to(along[0:1] + along[1:2] + back[2:3], stat_ref.shape)
    back = jnp.transpose(back)
    grads = []
    for at, (pre_ref, grad_ref, gain_ref) in enumerate(
        ((q_ref, dq_ref, gq_ref), (k_ref, dk_ref, gk_ref))
    ):
        scale = scales[:, at : at + 1]
        pre = pre_ref[...]
        grad = (
            scale * gain_ref[...].astype(F32) * grad_ref[...]
            - pre * (scale * scale * scale * back[:, at : at + 1] / full)
        ).astype(BF)
        grads.append(grad)
    out_ref[:, :width] = grads[0]
    out_ref[:, width : 2 * width] = grads[1]
    out_ref[:, 2 * width :] = dv_ref[...]


def norm_back(q_pre, k_pre, dq, dk, dv, gq, gk, sums, back):
    length, width = q_pre.shape
    full = width * len(sums)
    rows = min(256, length)
    tile = pl.BlockSpec((rows, width), lambda g: (g, 0))
    wide = pl.BlockSpec((rows, 3 * width), lambda g: (g, 0))
    gain = pl.BlockSpec((1, width), lambda g: (0, 0))
    line = pl.BlockSpec((8, rows), lambda g: (0, g))
    return launch(
        functools.partial(norm_back_kernel, full, len(sums)),
        [q_pre, k_pre, dq, dk, dv, gq, gk, *sums, *back],
        grid=(length // rows,),
        in_specs=[tile] * 5 + [gain, gain] + [line] * (2 * len(sums)),
        out_specs=[wide, line],
        out_shape=[
            jax.ShapeDtypeStruct((length, 3 * width), BF),
            jax.ShapeDtypeStruct((8, length), F32),
        ],

    )


def expert_kernel(step, aliased, chunk_ref, n2_ref, cot_ref, router_ref, keep_ref, wg_ref, wu_ref, wd_ref, *rest):
    rest = list(rest)
    own = step == 0
    res_ref = rest.pop(0) if own else None
    rest = rest[aliased:]
    h2t_ref, dg_ref, du_ref, n2t_ref, mix_ref, dn2_ref, probs_ref, mix, dn2, gates, gate_grads = rest
    expert = pl.program_id(0)
    blocks, rows, cols = cot_ref.shape
    lane = lax.broadcasted_iota(jnp.int32, (rows, 128), 1)

    @pl.when(expert == 0)
    def _():
        logits = jnp.where(lane < EXPERTS, dot(n2_ref[...], router_ref[...]), MASKED)
        exponent = jnp.exp(logits - jnp.max(logits, axis=1, keepdims=True))
        probs = exponent / jnp.sum(exponent, axis=1, keepdims=True)
        probs_ref[...] = probs
        gates[...] = probs * keep_ref[...]
        gate_grads[...] = jnp.zeros_like(gate_grads)
        n2t_ref[...] = jnp.transpose(n2_ref[...])
        dn2[...] = jnp.zeros_like(dn2)
        if own:
            mix[...] = res_ref[...]
        else:
            mix[...] = jnp.zeros_like(mix)

    normed = n2_ref[...]
    w_down = wd_ref[0]
    pre_gate = dot(normed, wg_ref[0])
    pre_up = dot(normed, wu_ref[0])
    back = dot_t(cot_ref[0], w_down[:, :cols])
    for t in range(1, blocks):
        back = back + dot_t(cot_ref[t], w_down[:, t * cols : (t + 1) * cols])
    here = lane == expert
    gate = jnp.sum(jnp.where(here, gates[...], 0.0), axis=1, keepdims=True)
    sigmoid = jax.nn.sigmoid(pre_gate)
    activated = pre_gate * sigmoid
    hidden = (activated * pre_up).astype(BF).astype(F32)
    gate_grad = jnp.sum(back * hidden, axis=1, keepdims=True)
    gate_grads[...] += jnp.where(here, gate_grad * keep_ref[...], 0.0)
    back = back * gate
    h2 = (hidden * gate).astype(BF)
    dg = (back * pre_up * sigmoid * (1.0 + pre_gate * (1.0 - sigmoid))).astype(BF)
    du = (back * activated).astype(BF)
    h2t_ref[...] = jnp.transpose(h2)
    dg_ref[...] = dg
    du_ref[...] = du
    mix[...] += dot(h2, w_down)
    dn2[...] += dot_t(dg, wg_ref[0]) + dot_t(du, wu_ref[0])

    @pl.when(expert == EXPERTS - 1)
    def _():
        dn2_ref[:, : blocks * cols] = dn2[...].astype(BF)
        high = gate_grads[...].astype(BF).astype(F32)
        low = gate_grads[...] - high
        if step:
            high = pltpu.roll(high, GROUP * 2 * step, 1)
        low = pltpu.roll(low, GROUP * (2 * step + 1), 1)
        dn2_ref[:, blocks * cols :] = (high + low).astype(BF)
        for t in range(blocks):
            mix_ref[t] = mix[:, t * cols : (t + 1) * cols].astype(BF)


def expert_call(step, chunk, n2, cot, router, keep, wg, wu, wd, residual, carried):
    rows, full = n2.shape
    blocks, length, cols = cot.shape
    hidden = wg.shape[2]
    own = step == 0
    in_specs = [
        pl.BlockSpec((rows, full), lambda e, c: (0, 0)),
        pl.BlockSpec((blocks, rows, cols), lambda e, c: (0, c[0], 0)),
        pl.BlockSpec((full, 128), lambda e, c: (0, 0)),
        pl.BlockSpec((rows, 128), lambda e, c: (c[0], 0)),
        pl.BlockSpec((1, full, hidden), lambda e, c: (e, 0, 0)),
        pl.BlockSpec((1, full, hidden), lambda e, c: (e, 0, 0)),
        pl.BlockSpec((1, hidden, full), lambda e, c: (e, 0, 0)),
    ]
    operands = [chunk, n2, cot, router, keep, wg, wu, wd]
    if own:
        in_specs.append(pl.BlockSpec((rows, full), lambda e, c: (0, 0)))
        operands.append(residual)
    aliases = {len(operands) + k: k for k in range(len(carried))}
    in_specs += [pl.BlockSpec(memory_space=pl.ANY)] * len(carried)
    operands += list(carried)
    slab = pl.BlockSpec((rows, hidden), lambda e, c: (c[0], e))
    return launch(
        functools.partial(expert_kernel, step, len(carried)),
        [*operands],
        prefetch=1,
            grid=(EXPERTS,),
            in_specs=in_specs,
            out_specs=[
                pl.BlockSpec((hidden, rows), lambda e, c: (e, c[0])),
                slab,
                slab,
                pl.BlockSpec((full, rows), lambda e, c: (0, c[0])),
                pl.BlockSpec((blocks, rows, cols), lambda e, c: (0, c[0], 0)),
                pl.BlockSpec((rows, full + 128), lambda e, c: (0, 0)),
                pl.BlockSpec((rows, 128), lambda e, c: (0, 0)),
            ],
            scratch=[
                pltpu.VMEM((rows, full), F32),
                pltpu.VMEM((rows, full), F32),
                pltpu.VMEM((rows, 128), F32),
                pltpu.VMEM((rows, 128), F32),
            ],
        out_shape=[
            jax.ShapeDtypeStruct((EXPERTS * hidden, length), BF),
            jax.ShapeDtypeStruct((length, EXPERTS * hidden), BF),
            jax.ShapeDtypeStruct((length, EXPERTS * hidden), BF),
            jax.ShapeDtypeStruct((full, length), BF),
            jax.ShapeDtypeStruct((blocks, length, cols), BF),
            jax.ShapeDtypeStruct((rows, full + 128), BF),
            jax.ShapeDtypeStruct((rows, 128), F32),
        ],
        aliases=aliases,

        token=6,
    )


def arrange_kernel(owners_ref, *refs):
    blocks, (branch_ref, rows_ref, out_ref) = refs[:-3], refs[-3:]
    for k, ref in enumerate(blocks):
        rows_ref[owners_ref[k]] = ref[...]
    out_ref[...] = branch_ref[...]


def arrange(owners, blocks, branch):
    rows, width = blocks[0].shape
    full = branch.shape[1]
    chunk = rows // 4
    return launch(
        arrange_kernel,
        [owners, *blocks, branch],
        prefetch=1,
        grid=(4,),
        in_specs=[pl.BlockSpec((chunk, width), lambda g, o: (g, 0))] * len(blocks)
        + [pl.BlockSpec((chunk, full), lambda g, o: (g, 0))],
        out_specs=[
            pl.BlockSpec((len(blocks), chunk, width), lambda g, o: (0, g, 0)),
            pl.BlockSpec((chunk, full), lambda g, o: (g, 0)),
        ],
        out_shape=[
            jax.ShapeDtypeStruct((len(blocks), rows, width), BF),
            jax.ShapeDtypeStruct((rows, full), BF),
        ],
    )


def gate_up_kernel(n2t_ref, dg_ref, du_ref, out_ref):
    turned = n2t_ref[...]
    out_ref[0, 0] = dot(turned, dg_ref[...]).astype(BF)
    out_ref[1, 0] = dot(turned, du_ref[...]).astype(BF)


def gate_up_grads(n2t, dg, du):
    full, length = n2t.shape
    hidden = dg.shape[1] // EXPERTS
    slab = pl.BlockSpec((length, hidden), lambda e: (0, e))
    return launch(
        gate_up_kernel,
        [n2t, dg, du],
        grid=(EXPERTS,),
        in_specs=[pl.BlockSpec((full, length), lambda e: (0, 0)), slab, slab],
        out_specs=pl.BlockSpec((2, 1, full, hidden), lambda e: (0, e, 0, 0)),
        out_shape=jax.ShapeDtypeStruct((2, EXPERTS, full, hidden), BF),
    )


def down_kernel(table_ref, h2t_ref, cot_ref, out_ref):
    cols = cot_ref.shape[2]
    for t in range(cot_ref.shape[0]):
        out_ref[0, :, t * cols : (t + 1) * cols] = dot(h2t_ref[...], cot_ref[t]).astype(BF)


def down_grads(table, h2t, cot, n):
    wide, length = h2t.shape
    blocks, _, cols = cot.shape
    rows = wide // n
    steps = n // 2
    return launch(
        down_kernel,
        [table, h2t, cot],
        prefetch=1,
        grid=(steps,),
        in_specs=[
            pl.BlockSpec((rows, length), lambda g, t: (t[g], 0)),
            pl.BlockSpec((blocks, length, cols), lambda g, t: (0, 0, 0)),
        ],
        out_specs=pl.BlockSpec((1, rows, blocks * cols), lambda g, t: (g, 0, 0)),
        out_shape=jax.ShapeDtypeStruct((steps, rows, blocks * cols), BF),
    )


def middle_kernel(size, owners_ref, *refs):
    heads, x_refs = refs[:size], refs[size : 2 * size]
    wo_ref, gain_ref, res_ref, n2_ref = refs[2 * size :]
    step = pl.program_id(0)
    cols = x_refs[0].shape[1]
    width = heads[0].shape[1]

    @pl.when(step == 0)
    def _():
        for k, ref in enumerate(x_refs):
            first = pl.multiple_of(owners_ref[k] * cols, 128)
            res_ref[:, pl.ds(first, cols)] = ref[...].astype(F32)

    weights = wo_ref[...].reshape(width, -1)
    for k, ref in enumerate(heads):

        @pl.when(step == k)
        def _(ref=ref):
            res_ref[...] += dot(ref[...], weights)

    @pl.when(step == size - 1)
    def _():
        residual = res_ref[...]
        scale = lax.rsqrt(jnp.mean(residual * residual, axis=1, keepdims=True) + EPSILON)
        for t in range(size):
            here = slice(t * cols, (t + 1) * cols)
            gain = gain_ref[t, 1:2, :].astype(F32)
            n2_ref[:, here] = (residual[:, here] * scale * gain).astype(BF)


def middle(owners, attended, received, w_out, x_blocks, gains):
    size = len(x_blocks)
    groups, _, part, full = w_out.shape
    width, cols = groups * part, full // size
    rows = attended.shape[0] // size
    return launch(
        functools.partial(middle_kernel, size),
        [owners, attended, *received, *x_blocks, w_out, gains],
        prefetch=1,
        grid=(size,),
        in_specs=[pl.BlockSpec((rows, width), lambda t, o: (o[0], 0))]
        + [pl.BlockSpec((rows, width), lambda t, o: (0, 0))] * (size - 1)
        + [pl.BlockSpec((rows, cols), lambda t, o: (o[0], 0))] * size
        + [
            pl.BlockSpec((groups, 1, part, full), lambda t, o: (0, o[t], 0, 0)),
            pl.BlockSpec((size, 16, cols), lambda t, o: (0, 0, 0)),
        ],
        out_specs=[pl.BlockSpec((rows, full), lambda t, o: (0, 0))] * 2,
        out_shape=[
            jax.ShapeDtypeStruct((rows, full), F32),
            jax.ShapeDtypeStruct((rows, full), BF),
        ],
    )


def middle_back_kernel(
    mine_ref, own_ref, received_ref, probs_ref, router_ref, res_ref, n2_ref, cot_ref, gain_ref, wo_ref,
    branch_ref, parts_ref, *out_refs,
):
    step = pl.program_id(0)
    blocks, rows, cols = cot_ref.shape
    full = blocks * cols

    @pl.when(step == 0)
    def _():
        probs = probs_ref[...]
        parts = own_ref[:, full:].astype(F32) + received_ref[:, full:].astype(F32)
        prob_grad = parts
        for group in range(1, 2 * blocks):
            prob_grad = prob_grad + pltpu.roll(parts, 128 - GROUP * group, 1)
        lane = lax.broadcasted_iota(jnp.int32, (rows, 128), 1)
        prob_grad = jnp.where(lane < EXPERTS, prob_grad, 0.0)
        centred = jnp.sum(prob_grad * probs, axis=1, keepdims=True)
        logit_grad = (probs * (prob_grad - centred)).astype(BF)
        grad = (
            own_ref[:, :full].astype(F32)
            + received_ref[:, :full].astype(F32)
            + dot_t(logit_grad, router_ref[...])
        )
        residual = res_ref[...]
        scale = lax.rsqrt(jnp.mean(residual * residual, axis=1, keepdims=True) + EPSILON)
        stat = jnp.zeros((rows, 1), F32)
        for t in range(blocks):
            here = slice(t * cols, (t + 1) * cols)
            gain = gain_ref[t, 1:2, :].astype(F32)
            stat = stat + jnp.sum(residual[:, here] * gain * grad[:, here], axis=1, keepdims=True)
        stat = scale * scale * scale * stat / full
        for t in range(blocks):
            here = slice(t * cols, (t + 1) * cols)
            gain = gain_ref[t, 1:2, :].astype(F32)
            branch_ref[:, here] = (
                cot_ref[t].astype(F32) + scale * gain * grad[:, here] - residual[:, here] * stat
            ).astype(BF)
        router_part = lax.dot_general(
            logit_grad, n2_ref[...], (((0,), (0,)), ((), ())), preferred_element_type=F32
        )[:8]
        norm_part = jnp.sum(grad * residual * scale, axis=0, keepdims=True)
        which = lax.broadcasted_iota(jnp.int32, (8, full), 0)
        parts_ref[...] = jnp.where(which == EXPERTS, norm_part, router_part)

    product = dot_t(branch_ref[...], wo_ref[...].reshape(-1, full)).astype(BF)
    for k, ref in enumerate(out_refs):

        @pl.when(step == k)
        def _(ref=ref):
            ref[...] = product


def middle_back(mine, own, received, probs, router, residual, n2, cot, gains, w_out):
    blocks, _, cols = cot.shape
    rows, full = residual.shape
    groups, _, part, _ = w_out.shape
    width = groups * part
    whole = pl.BlockSpec((rows, full), lambda t, m: (0, 0))
    wide = pl.BlockSpec((rows, full + 128), lambda t, m: (0, 0))
    lanes = pl.BlockSpec((rows, 128), lambda t, m: (0, 0))
    return launch(
        middle_back_kernel,
        [mine, own, received, probs, router, residual, n2, cot, gains, w_out],
        prefetch=1,
            grid=(blocks,),
            in_specs=[
                wide,
                wide,
                lanes,
                pl.BlockSpec((full, 128), lambda t, m: (0, 0)),
                whole,
                whole,
                pl.BlockSpec((blocks, rows, cols), lambda t, m: (0, m[0], 0)),
                pl.BlockSpec((blocks, 16, cols), lambda t, m: (0, 0, 0)),
                pl.BlockSpec((groups, 1, part, full), lambda t, m: (0, lax.rem(m[0] + t, blocks), 0, 0)),
            ],
            out_specs=[
                whole,
                pl.BlockSpec((8, full), lambda t, m: (0, 0)),
            ]
            + [pl.BlockSpec((rows, width), lambda t, m: (0, 0))] * blocks,
        out_shape=[
            jax.ShapeDtypeStruct((rows, full), BF),
            jax.ShapeDtypeStruct((8, full), F32),
        ]
        + [jax.ShapeDtypeStruct((rows, width), BF)] * blocks,
    )


def reversed_bits(at, bits):
    return sum(((at >> b) & 1) << (bits - 1 - b) for b in range(bits)) if bits else at


def column_grad_kernel(left_ref, right_ref, w_ref, out_ref, gain_ref):
    product = dot(jnp.transpose(left_ref[...]), right_ref[...])
    out_ref[...] = product.astype(BF)
    gain_ref[...] = jnp.broadcast_to(row_sums(product * w_ref[...].astype(F32)), gain_ref.shape)


def column_grads(left, right, weights):
    length, full = left.shape
    width = right.shape[1]
    piece = min(512, full)
    tile = pl.BlockSpec((piece, width), lambda g: (g, 0))
    return launch(
        column_grad_kernel,
        [left, right, weights],
        grid=(full // piece,),
        in_specs=[
            pl.BlockSpec((length, piece), lambda g: (0, g)),
            pl.BlockSpec((length, width), lambda g: (0, 0)),
            tile,
        ],
        out_specs=[tile, pl.BlockSpec((8, piece), lambda g: (0, g))],
        out_shape=[
            jax.ShapeDtypeStruct((full, width), BF),
            jax.ShapeDtypeStruct((8, full), F32),
        ],
    )


def row_grad_kernel(rows_ref, left_ref, *rest):
    blocks, (out_ref, turned_left) = rest[:-2], rest[-2:]
    rows = blocks[0].shape[0]

    @pl.when(pl.program_id(0) == 0)
    def _():
        for k in range(len(blocks)):
            first = pl.multiple_of(rows_ref[k] * rows, rows)
            turned_left[:, k * rows : (k + 1) * rows] = jnp.transpose(
                left_ref[pl.ds(first, rows), :]
            )

    total = None
    for k, block in enumerate(blocks):
        term = dot(turned_left[:, k * rows : (k + 1) * rows], block[...])
        total = term if total is None else total + term
    out_ref[...] = total.astype(BF)


def row_grads(owners, left, blocks):
    length, width = left.shape
    rows, full = blocks[0].shape
    piece = min(512, full)
    return launch(
        row_grad_kernel,
        [owners, left, *blocks],
        prefetch=1,
        grid=(full // piece,),
        in_specs=[pl.BlockSpec((length, width), lambda g, o: (0, 0))]
        + [pl.BlockSpec((rows, piece), lambda g, o: (0, g))] * len(blocks),
        out_specs=pl.BlockSpec((width, piece), lambda g, o: (0, g)),
        out_shape=jax.ShapeDtypeStruct((width, full), BF),
        scratch=[pltpu.VMEM((width, length), BF)],
    )


def input_kernel(owner_ref, grad_ref, w_ref, *rest):
    total = dot_t(grad_ref[...], w_ref[...])
    if len(rest) == 2:
        total = total + rest[0][...].astype(F32)
    rest[-1][...] = total.astype(BF)


def input_grads(owner, cols, grad, w_all, received=None, work=1):
    length, width = grad.shape
    rows = min(256, length)
    tile = pl.BlockSpec((rows, cols), lambda g, o: (g, 0))
    return launch(
        input_kernel,
        [owner, grad, w_all, *([] if received is None else [received])],
        prefetch=1,
            grid=(length // rows,),
            in_specs=[
                pl.BlockSpec((rows, width), lambda g, o: (g, 0)),
                pl.BlockSpec((cols, width), lambda g, o: (o[0], 0)),
            ]
            + ([] if received is None else [tile]),
            out_specs=tile,
        out_shape=jax.ShapeDtypeStruct((length, cols), BF),

        work=work,
    )


def mix_kernel(owner_ref, mix_ref, *rest):
    if len(rest) == 1:
        rest[0][...] = mix_ref[0]
    else:
        rest[1][...] = added(mix_ref[0], rest[0][...])


def mix_block(owner, mix, received=None, work=1):
    blocks, length, cols = mix.shape
    chunk = length // 4
    tile = pl.BlockSpec((chunk, cols), lambda g, o: (g, 0))
    return launch(
        mix_kernel,
        [owner, mix, *([] if received is None else [received])],
        prefetch=1,
            grid=(4,),
            in_specs=[pl.BlockSpec((1, chunk, cols), lambda g, o: (o[0], g, 0))]
            + ([] if received is None else [tile]),
            out_specs=tile,
        out_shape=jax.ShapeDtypeStruct((length, cols), BF),
        work=work,
    )


def final_kernel(
    full, owners_ref, grad_ref, w_ref, received_ref, tokens_ref, sums_ref, stat_ref, gain_ref, *rest
):
    blocks, out_ref = rest[:-1], rest[-1]
    step = pl.program_id(0)
    branch = blocks[0][...]
    for k in range(1, len(blocks)):
        branch = jnp.where(step == k, blocks[k][...], branch)
    scale = lax.rsqrt(sums_ref[...] / full + EPSILON)
    scale_one = jnp.transpose(scale)[:, 2:3]
    stat = jnp.transpose(stat_ref[...])[:, 0:1] / full * scale_one * scale_one
    normed_grad = dot_t(grad_ref[...], w_ref[...]) + received_ref[...].astype(F32)
    out_ref[...] = (
        branch.astype(F32)
        + scale_one * gain_ref[...].astype(F32) * normed_grad
        - tokens_ref[...].astype(F32) * stat
    )


def final_grads(owners, grad, w_all, received, tokens, sums, stat, gain, blocks):
    length, cols = tokens.shape
    width = grad.shape[1]
    rows = length // len(blocks)
    tile = pl.BlockSpec((rows, cols), lambda k, o: (o[k], 0))
    line = pl.BlockSpec((8, rows), lambda k, o: (0, o[k]))
    return launch(
        functools.partial(final_kernel, cols * len(blocks)),
        [owners, grad, w_all, received, tokens, sums, stat, gain, *blocks],
        prefetch=1,
            grid=(len(blocks),),
            in_specs=[
                pl.BlockSpec((rows, width), lambda k, o: (o[k], 0)),
                pl.BlockSpec((cols, width), lambda k, o: (o[0], 0)),
                tile,
                tile,
                line,
                line,
                pl.BlockSpec((1, cols), lambda k, o: (0, 0)),
            ]
            + [pl.BlockSpec((rows, cols), lambda k, o: (0, o[0]))] * len(blocks),
            out_specs=tile,
        out_shape=jax.ShapeDtypeStruct((length, cols), F32),
    )


def piece_specs(shape, steps):
    block = (1,) + shape
    return [
        pl.BlockSpec(block, lambda a, pos: (jnp.minimum(pos[a], steps - 1), 0, 0)),
        pl.BlockSpec(block, lambda a, pos: (jnp.maximum(pos[a] - steps, 0), 0, 0)),
    ]


def pieces_kernel(steps, pos_ref, low_ref, high_ref, out_ref):
    low = pos_ref[pl.program_id(0)] < steps
    out_ref[...] = jnp.where(low, low_ref[0].astype(F32), high_ref[0].astype(F32))


def widen_pieces(pos, halves, n):
    steps, rows, width = halves[0].shape
    return launch(
        functools.partial(pieces_kernel, steps),
        [pos, *halves],
        prefetch=1,
        grid=(n,),
        in_specs=piece_specs((rows, width), steps),
        out_specs=pl.BlockSpec((rows, width), lambda a, pos: (a, 0)),
        out_shape=jax.ShapeDtypeStruct((rows * n, width), F32),
    )


def projections_kernel(sum_ref, q_ref, k_ref, v_ref):
    width = q_ref.shape[1]
    for at, out_ref in enumerate((q_ref, k_ref, v_ref)):
        out_ref[...] = sum_ref[:, at * width : (at + 1) * width].astype(F32)


def widen_projections(total):
    full, width = total.shape
    out = width // 3
    piece = min(256, full)
    tile = pl.BlockSpec((piece, out), lambda g: (g, 0))
    return launch(
        projections_kernel,
        [total],
        grid=(full // piece,),
        in_specs=[pl.BlockSpec((piece, width), lambda g: (g, 0))],
        out_specs=[tile] * 3,
        out_shape=[jax.ShapeDtypeStruct((full, out), F32)] * 3,
    )


def experts_kernel(held_ref, gate_ref, up_ref):
    gate_ref[0] = held_ref[0, 0].astype(F32)
    up_ref[0] = held_ref[1, 0].astype(F32)


def widen_experts(held):
    _, experts, full, hidden = held.shape
    tall = pl.BlockSpec((1, full, hidden), lambda e: (e, 0, 0))
    return launch(
        experts_kernel,
        [held],
        grid=(experts,),
        in_specs=[pl.BlockSpec((2, 1, full, hidden), lambda e: (0, e, 0, 0))],
        out_specs=[tall, tall],
        out_shape=[jax.ShapeDtypeStruct((experts, full, hidden), F32)] * 2,
    )


def kept_experts(routes, order):
    length = routes.shape[0]
    token, which = order // TOP, order % TOP
    onehot = (token[:, None] == jnp.arange(length, dtype=jnp.int32)[None, :]).astype(BF)
    named = (routes[:, :, None] == jnp.arange(8, dtype=jnp.int32)).astype(BF).reshape(length, TOP * 8)
    ordered = dot(onehot, named).reshape(-1, TOP, 8)
    choose = jnp.sum(
        jnp.where(which[:, None, None] == jnp.arange(TOP)[None, :, None], ordered, 0.0), axis=1
    )
    kept = jnp.where(jnp.cumsum(choose, axis=0) <= CAP, choose, 0.0).astype(BF)
    kept = jnp.pad(kept, ((0, 0), (0, 120)))
    return lax.dot_general(onehot, kept, (((0,), (0,)), ((), ())), preferred_element_type=F32)


def on_device(
    tokens, cotangent, norm1_gain, w_query, w_key, w_value, query_gain, key_gain, w_output,
    norm2_gain, router, w_gate, w_up, w_down, routes, prefix, slot_order,
):
    size, n = lax.axis_size("tensor"), lax.axis_size("dp")
    mine, group = lax.axis_index("tensor"), lax.axis_index("dp")
    length, cols = tokens.shape
    full = cols * size
    rows = length // size
    steps = range(1, size)
    Chain.token = None

    def add(*terms):
        return functools.reduce(jnp.add, terms)

    here = mine.astype(jnp.int32)[None]

    rel = rel_table(swap_masks(n))
    table = jnp.asarray(rel, jnp.int32) ^ group
    positions = jnp.asarray([rel.index(v) for v in range(n)], jnp.int32)[
        jnp.arange(n, dtype=jnp.int32) ^ group
    ]
    half = n // 2
    owners = ((mine - jnp.arange(size)) % size).astype(jnp.int32)

    def owner(step):
        return owners[step : step + 1]

    def by_owner(own, *others):
        return place(size, [b[None] for b in others], mine, own[None])

    part = w_output.shape[0] // n
    gains = jnp.concatenate([norm1_gain[None], norm2_gain[None], jnp.zeros((14, cols), BF)])
    w_piece = jnp.concatenate(
        [
            lax.dynamic_slice_in_dim(w_output, group * part, part, 0),
            jnp.pad(gains, ((0, 0), (0, full - cols))),
        ]
    )
    w_blocks, x_blocks = [w_piece], [tokens]
    for step in steps:
        w_blocks.append(send(w_blocks[-1], 1, size))
    w_mixed = by_owner(*w_blocks)
    w_out = lax.all_gather(w_mixed[:, :part], "dp", axis=0)
    gains = w_mixed[:, part:, :cols]
    w_all = side_by_side([w_query, w_key, w_value])
    keep = kept_experts(routes, slot_order[0])
    router_wide = jnp.pad(router, ((0, 0), (0, 128 - EXPERTS)))
    halfway = HEAD_DIM // 2
    freqs = ROPE_BASE ** (-(jnp.arange(halfway, dtype=F32) * 2.0 / HEAD_DIM))
    angles = jnp.arange(length, dtype=F32)[:, None] * freqs[None, :]
    cosine = jnp.concatenate([jnp.cos(angles)] * 2, axis=1)
    sine = jnp.concatenate([-jnp.sin(angles), jnp.sin(angles)], axis=1)
    for step in steps:
        x_blocks.append(send(x_blocks[-1], 1, size))
    late_cot = copied(cotangent, (x_blocks[-1], keep, router_wide, cosine, sine))
    cot = lax.all_gather(late_cot, "tensor", axis=0)
    normed_one, q_pre, k_pre, v_rows, own_sums = qkv_call(
        owners, x_blocks, gains, w_query, w_key, w_value
    )
    sums = [own_sums] + [send(own_sums, step, size) for step in steps]

    gq, gk = query_gain[None], key_gain[None]
    attended, lse, q_rot, k_rot = attn_forward(
        prefix, q_pre, k_pre, v_rows, gq, gk, cosine, sine, sums
    )

    received = [
        send(lax.dynamic_slice_in_dim(attended, (mine + step) % size * rows, rows, 0), step, size)
        for step in steps
    ]
    residual, normed_two = middle(owners, attended, received, w_out, x_blocks, gains)

    def add_wide(a, b, work=1):
        return add_blocks(a[None], b[None], work)[0]

    chunks = [copied(normed_two, (cot,))]
    chunks.append(send(chunks[0], 1, size))
    carried, later, dn2_flying = (), [], None
    for step in range(size):
        outs = expert_call(
            step, owner(step), chunks[step], cot, router_wide, keep, w_gate, w_up, w_down,
            residual if step == 0 else None, carried,
        )
        carried = outs[:5]
        if step < size - 2:
            chunks.append(send(copied(chunks[-1]), 1, size))
        if step == 0:
            own_dn2, expert_probs = outs[5:]
        else:
            later.append(outs[5])
        if step > 3:
            dn2_flying = send(add_wide(later.pop(0), dn2_flying), 1, size)
        elif step == min(3, size - 1):
            dn2_flying = send(copied(later.pop(0)), 1, size)
    h2t, dg, du, n2t, mix = carried

    expert_grads = lax.psum(gate_up_grads(n2t, dg, du), "dp")
    sum_down = Sum(n, 2, down_grads(table[half:], h2t, cot, n))
    dn2_flying = send(add_wide(later.pop(0), dn2_flying, LONG), 1, size)
    sum_down.keep = down_grads(table[:half], h2t, cot, n)
    for term in later:
        dn2_flying = send(add_wide(term, dn2_flying), 1, size)
    sum_down.step()

    branch_rows, small, *out_rows = middle_back(
        here, own_dn2, dn2_flying, expert_probs, router_wide, residual, normed_two, cot, gains, w_out
    )

    received = [send(out_rows[step], step, size) for step in steps]
    out_grad, branch_rows = arrange(owners, [out_rows[0]] + received, branch_rows)
    branch_blocks = [branch_rows, send(branch_rows, 1, size)]
    sum_down.step()
    dq, dk, dv, gain_grads, own_back = attn_backward(
        prefix, q_pre, k_pre, q_rot, k_rot, v_rows, out_grad.reshape(length, -1), lse, gq, gk,
        cosine, sine, sums,
    )
    back = [own_back] + [send(own_back, step, size) for step in steps]
    sum_down.step()
    branch_blocks.append(send(copied(branch_blocks[1], tuple(back[1:])), 1, size))
    grad_qkv, stat_one = norm_back(q_pre, k_pre, dq, dk, dv, gq, gk, sums, back)
    in_grads, gain_part = column_grads(normed_one, grad_qkv, w_all)
    sum_down.step()
    for step in range(3, size):
        branch_blocks.append(send(copied(branch_blocks[-1]), 1, size))
    packed = jnp.concatenate([jnp.concatenate([small[:7], gain_part[7:]]), gain_grads], axis=1)
    width = 3 * w_query.shape[1]
    extra = jnp.pad(packed.reshape(-1), (0, 32 * width - packed.size)).astype(BF).reshape(32, width)
    out_grads = row_grads(owners, attended, branch_blocks)
    extra = copied(extra, (expert_grads,))
    in_grads, out_grads, extra = lax.psum((in_grads, out_grads, extra), "dp")
    dn1_flying = send(input_grads(owner(1), cols, grad_qkv, w_all, work=LONG), 1, size)
    mix_flying = send(mix_block(owner(1), mix), 1, size)
    sum_down.step()
    for step in range(2, size):
        dn1_flying = send(input_grads(owner(step), cols, grad_qkv, w_all, dn1_flying), 1, size)
        sum_down.step()
        if step == 2:
            grad_gate, grad_up = widen_experts(expert_grads)
        if step < size - 1:
            mix_flying = send(mix_block(owner(step), mix, mix_flying), 1, size)
    mix_flying = send(mix_block(owner(size - 1), mix, mix_flying), 1, size)

    grad_tokens = final_grads(
        owners, grad_qkv, w_all, dn1_flying, tokens, own_sums, stat_one, norm1_gain[None],
        branch_blocks,
    )
    for _ in range(2 * len(swap_masks(n))):
        sum_down.step()
    grad_down = widen_pieces(positions, sum_down.finish(), n).reshape(w_down.shape)

    mixed = mix_block(owner(0), mix, mix_flying)
    extra = copied(extra)
    packed = extra.astype(F32).reshape(-1)[: packed.size].reshape(packed.shape)
    gain_total, packed = packed[:2, full:], packed[:, :full]
    packed = [packed] + [send(packed, step, size) for step in steps]
    grad_query, grad_key, grad_value = widen_projections(in_grads)
    grad_output = out_grads.astype(F32)

    packed = add(*packed)
    grad_router = packed[:EXPERTS].T
    own = lax.dynamic_slice_in_dim(packed[EXPERTS:], mine * cols, cols, 1)
    grad_norm2_gain = own[0]
    grad_norm1_gain = own[1] / norm1_gain.astype(F32)
    grad_query_gain, grad_key_gain = gain_total[0], gain_total[1]
    return (
        mixed, grad_tokens, grad_norm1_gain, grad_query, grad_key, grad_value, grad_query_gain,
        grad_key_gain, grad_output, grad_norm2_gain, grad_router, grad_gate, grad_up, grad_down,
    )


def solution(mesh):
    rows, weight_cols, weight_rows = P("dp", "tensor"), P(None, "tensor"), P("tensor", None)
    vector, expert_cols, expert_rows = P("tensor"), P(None, None, "tensor"), P(None, "tensor", None)
    return jax.shard_map(
        on_device,
        mesh=mesh,
        in_specs=(
            rows, rows, vector, weight_cols, weight_cols, weight_cols, vector, vector, weight_rows,
            vector, P(), expert_cols, expert_cols, expert_rows, P("dp", None), P("dp"),
            P("dp", None),
        ),
        out_specs=(
            rows, rows, vector, weight_cols, weight_cols, weight_cols, vector, vector, weight_rows,
            vector, P(), expert_cols, expert_cols, expert_rows,
        ),
        check_vma=False,
    )
```

```python
import functools

import jax
import jax.numpy as jnp
from jax import lax
from jax.experimental import pallas as pl
from jax.experimental.pallas import tpu as pltpu
from jax.sharding import PartitionSpec as P

HEAD_DIM = 128
EXPERTS = 6
TOP = 3
CAP = 640
PREFIX_MAX = 512

EPSILON = 1e-05
ROPE_BASE = 10000.0
MASKED = -1e30
GROUP = 8
LONG = 2e13
BF = jnp.bfloat16
F32 = jnp.float32
VMEM_LIMIT = 56 * 1024 * 1024


class Chain:
    token = None


def launch(
    body, operands, *, grid, in_specs, out_specs, out_shape, work=1, prefetch=0, scratch=(), aliases=None,
    token=0, others=(),
):
    operands = list(operands)
    unread = [field for field in (Chain.token, *others) if field is not None]
    unread = [field for field in unread if all(field is not own for own in operands)]
    first, last = len(operands), len(operands) + len(unread)

    def kernel(*refs):
        body(*refs[:first], *refs[last:])

    out = pl.pallas_call(
        kernel,
        grid_spec=pltpu.PrefetchScalarGridSpec(
            num_scalar_prefetch=prefetch,
            grid=grid,
            in_specs=list(in_specs) + [pl.BlockSpec(memory_space=pl.ANY)] * len(unread),
            out_specs=out_specs,
            scratch_shapes=list(scratch),
        ),
        out_shape=out_shape,
        input_output_aliases=aliases or {},
        compiler_params=pltpu.CompilerParams(vmem_limit_bytes=VMEM_LIMIT),
        cost_estimate=pl.CostEstimate(flops=int(work), bytes_accessed=1, transcendentals=0),
    )(*operands, *unread)
    Chain.token = out[token] if isinstance(out, (list, tuple)) else out
    return out


def dot(a, b):
    return jnp.dot(a, b, preferred_element_type=F32)


def dot_t(a, b):
    return lax.dot_general(a, b, (((1,), (1,)), ((), ())), preferred_element_type=F32)


def row_sums(field):
    folded = field[:, :128]
    for at in range(128, field.shape[1], 128):
        folded = folded + field[:, at : at + 128]
    return jnp.sum(jnp.transpose(folded), axis=0, keepdims=True)


def ring(size):
    return [(at, (at + 1) % size) for at in range(size)]


def send(value, step, size):
    return lax.ppermute(value, "tensor", [(at, (at + step) % size) for at in range(size)])


def swap(value, mask, n):
    return lax.ppermute(value, "dp", [(at, at ^ mask) for at in range(n)])


def take(blocks, at):
    return lax.dynamic_slice_in_dim(blocks, at, 1, 0)


def place(size, received, mine, own):
    out = lax.dynamic_update_slice_in_dim(jnp.zeros((size,) + own.shape[1:], own.dtype), own, mine, 0)
    for step, block in enumerate(received, 1):
        out = lax.dynamic_update_slice_in_dim(out, block, (mine - step) % size, 0)
    return out


def swap(field, mask, n):
    return lax.ppermute(field, "dp", [(at, at ^ mask) for at in range(n)])


def swap_masks(n):
    return [1 << bit for bit in range(n.bit_length() - 1)]


def rel_table(masks):
    bits = len(masks)
    return [
        sum(masks[s] for s in range(bits) if (p >> (bits - 1 - s)) & 1) for p in range(1 << bits)
    ]


def blockwise(body, ins, outs, others=(), work=1):
    chunks = 2 if ins[0].shape[1] % 32 == 0 else 1

    def spec(shape):
        return pl.BlockSpec((shape[0], shape[1] // chunks, shape[2]), lambda g: (0, g, 0))

    def kernel(*refs):
        body(refs[: len(ins)], refs[len(ins) :])

    return launch(
        kernel,
        [*ins],
        grid=(chunks,),
        in_specs=[spec(field.shape) for field in ins],
        out_specs=[spec(shape) for shape in outs],
        out_shape=[jax.ShapeDtypeStruct(shape, BF) for shape in outs],
        others=others,
        work=work,
    )


def added(a, b):
    return (a.astype(F32) + b.astype(F32)).astype(BF)


def copied(field, others=()):
    def body(ins, outs):
        outs[0][...] = ins[0][...]

    return blockwise(body, [field[None]], [(1,) + field.shape], others)[0][0]


def side_by_side(fields):
    def body(ins, outs):
        at = 0
        for ref in ins:
            outs[0][:, :, at : at + ref.shape[2]] = ref[...]
            at += ref.shape[2]

    width = sum(field.shape[1] for field in fields)
    return blockwise(body, [field[None] for field in fields], [(1, fields[0].shape[0], width)])[0][0]


def add_blocks(a, b, work=1):
    def body(ins, outs):
        outs[0][...] = added(ins[0][...], ins[1][...])

    return blockwise(body, [a, b], [a.shape], work=work)[0]


class Sum:
    def __init__(self, n, parts, first):
        self.n, self.parts = n, parts
        self.masks = swap_masks(n)
        self.stage = 0
        self.flying = [swap(first, self.masks[0], n)]

    def send(self, fields, stage):
        self.flying = []
        for part, field in enumerate(fields):
            mask = self.masks[stage] if part == 0 else self.masks[-stage]
            self.flying.append(swap(field, mask, self.n))

    def split(self, keeps, received):
        count, rows, width = keeps[0].shape
        wide = width // self.parts if len(keeps) < self.parts else width

        def body(ins, outs):
            for part in range(self.parts):
                at = part if len(keeps) == self.parts else 0
                here = slice(part * wide, (part + 1) * wide) if at != part else slice(0, wide)
                for i in range(count):
                    total = added(ins[2 * at][i, :, here], ins[2 * at + 1][i, :, here])
                    if part == 0:
                        away, place_at = i >= count // 2, i % (count // 2)
                    else:
                        away, place_at = i % 2 == 1, i // 2
                    outs[2 * part + (0 if away else 1)][place_at] = total

        ins = [field for pair in zip(keeps, received, strict=True) for field in pair]
        outs = blockwise(body, ins, [(count // 2, rows, wide)] * (2 * self.parts))
        return outs[0::2], outs[1::2]

    def total(self, keeps, received):
        def body(ins, outs):
            for part, out in enumerate(outs):
                out[...] = added(ins[2 * part][...], ins[2 * part + 1][...])

        ins = [field for pair in zip(keeps, received, strict=True) for field in pair]
        return blockwise(body, ins, [field.shape for field in keeps])

    def joined(self, last, keeps, received):
        count, rows, wide = keeps[0].shape

        def body(ins, outs):
            for part in range(self.parts):
                out = outs[0] if last else outs[part]
                here = slice(part * wide, (part + 1) * wide) if last else slice(0, wide)
                for i in range(count):
                    low, high = (i, count + i) if part == 0 else (2 * i, 2 * i + 1)
                    out[low, :, here] = ins[2 * part][i]
                    out[high, :, here] = ins[2 * part + 1][i]

        ins = [field for pair in zip(keeps, received, strict=True) for field in pair]
        if last:
            return blockwise(body, ins, [(2 * count, rows, wide * self.parts)])
        return blockwise(body, ins, [(2 * count, rows, wide)] * self.parts)

    def step(self):
        bits = len(self.masks)
        if self.stage == 2 * bits - 1:
            return
        received = self.flying
        self.stage += 1
        if self.stage < bits:
            keep = [self.keep] if self.stage == 1 else self.keep
            away, self.keep = self.split(keep, received)
            self.send(away, self.stage)
            return
        back = 2 * bits - 1 - self.stage
        if self.stage == bits:
            self.keep = self.total(self.keep, received)
        else:
            self.keep = self.joined(back == 0, self.keep, received)
        if back:
            self.send(self.keep, back)
        else:
            self.keep = self.keep[0]
            self.flying = [swap(self.keep, self.masks[0], self.n)]

    def finish(self):
        return self.keep, self.flying[0]


def qkv_kernel(owners_ref, *refs):
    blocks, refs = refs[:-9], refs[-9:]
    gain_ref, wq_ref, wk_ref, wv_ref, n1_ref, q_ref, k_ref, v_ref, sums_ref = refs
    rows, cols = blocks[0].shape
    full = len(blocks) * cols
    fields = [block[...].astype(F32) for block in blocks]
    squares = fields[0] * fields[0]
    for field in fields[1:]:
        squares = squares + field * field
    scale = lax.rsqrt(jnp.sum(squares, axis=1, keepdims=True) / full + EPSILON)
    for k, field in enumerate(fields):
        at = owners_ref[k]
        gain = gain_ref[at, 0:1, :].astype(F32)
        first = pl.multiple_of(at * cols, 128)
        normed = (field * scale * gain).astype(BF)
        n1_ref[:, pl.ds(first, cols)] = normed
        terms = [dot(normed, ref[pl.ds(first, cols), :]) for ref in (wq_ref, wk_ref, wv_ref)]
        total = terms if k == 0 else [a + b for a, b in zip(total, terms, strict=True)]
    query, key, value = total
    q_ref[...] = query
    k_ref[...] = key
    v_ref[...] = value.astype(BF)
    which = lax.broadcasted_iota(jnp.int32, (8, rows), 0)
    sums_ref[...] = jnp.where(
        which == 0,
        row_sums(query * query),
        jnp.where(which == 1, row_sums(key * key), row_sums(squares)),
    )


def qkv_call(owners, blocks, gains, wq, wk, wv):
    length, cols = blocks[0].shape
    full = cols * len(blocks)
    out = wq.shape[1]
    rows = min(256, length)
    whole = pl.BlockSpec((full, out), lambda g, o: (0, 0))
    tile = pl.BlockSpec((rows, out), lambda g, o: (g, 0))
    return launch(
        qkv_kernel,
        [owners, *blocks, gains, wq, wk, wv],
        prefetch=1,
        grid=(length // rows,),
        in_specs=[pl.BlockSpec((rows, cols), lambda g, o: (g, 0))] * len(blocks)
        + [pl.BlockSpec((len(blocks), 16, cols), lambda g, o: (0, 0, 0)), whole, whole, whole],
        out_specs=[
            pl.BlockSpec((rows, full), lambda g, o: (g, 0)),
            tile,
            tile,
            tile,
            pl.BlockSpec((8, rows), lambda g, o: (0, g)),
        ],
        out_shape=[
            jax.ShapeDtypeStruct((length, full), BF),
            jax.ShapeDtypeStruct((length, out), F32),
            jax.ShapeDtypeStruct((length, out), F32),
            jax.ShapeDtypeStruct((length, out), BF),
            jax.ShapeDtypeStruct((8, length), F32),
        ],
    )


def head_scales(sums_refs, full):
    total = sums_refs[0][...]
    for ref in sums_refs[1:]:
        total = total + ref[...]
    return jnp.transpose(lax.rsqrt(total / full + EPSILON))


def masked_scores(query, key, first, prefix):
    scores = dot_t(query, key) * (HEAD_DIM**-0.5)
    row = first + lax.broadcasted_iota(jnp.int32, scores.shape, 0)
    col = lax.broadcasted_iota(jnp.int32, scores.shape, 1)
    return jnp.where((col <= row) | (col < prefix), scores, MASKED)


def attn_forward_kernel(full, size, prefix_ref, q_ref, k_ref, v_ref, gq_ref, gk_ref, cos_ref, sin_ref, *rest):
    sums_refs, (att_ref, lse_ref, qr_ref, kr_ref) = rest[:size], rest[size:]
    length = q_ref.shape[0]
    rows = min(256, length)
    scales = head_scales(sums_refs, full)
    cosine, sine = cos_ref[...], sin_ref[...]
    for pre_ref, gain_ref, out_ref, at in ((q_ref, gq_ref, qr_ref, 0), (k_ref, gk_ref, kr_ref, 1)):
        field = pre_ref[...] * scales[:, at : at + 1] * gain_ref[...].astype(F32)
        out_ref[...] = (field * cosine + pltpu.roll(field, HEAD_DIM // 2, 1) * sine).astype(BF)
    prefix = prefix_ref[0]
    for first in range(0, length, rows):
        last = min(length, max(PREFIX_MAX, first + rows))
        scores = masked_scores(qr_ref[first : first + rows, :], kr_ref[:last, :], first, prefix)
        highest = jnp.max(scores, axis=1, keepdims=True)
        exponent = jnp.exp(scores - highest)
        total = jnp.sum(exponent, axis=1, keepdims=True)
        mixed = dot(exponent.astype(BF), v_ref[:last, :])
        att_ref[first : first + rows, :] = (mixed / total).astype(BF)
        lse_ref[first : first + rows, :] = jnp.broadcast_to(
            highest + jnp.log(total), (rows, HEAD_DIM)
        )


def attn_forward(prefix, q_pre, k_pre, v_rows, gq, gk, cosine, sine, sums):
    length, width = q_pre.shape
    full = width * len(sums)
    head = pl.BlockSpec((length, HEAD_DIM), lambda h, *_: (0, h))
    gain = pl.BlockSpec((1, HEAD_DIM), lambda h, *_: (0, h))
    table = pl.BlockSpec((length, HEAD_DIM), lambda h, *_: (0, 0))
    sums_spec = pl.BlockSpec((8, length), lambda h, *_: (0, 0))
    return launch(
        functools.partial(attn_forward_kernel, full, len(sums)),
        [prefix, q_pre, k_pre, v_rows, gq, gk, cosine, sine, *sums],
        prefetch=1,
            grid=(width // HEAD_DIM,),
            in_specs=[head, head, head, gain, gain, table, table] + [sums_spec] * len(sums),
            out_specs=[head] * 4,
        out_shape=[
            jax.ShapeDtypeStruct((length, width), BF),
            jax.ShapeDtypeStruct((length, width), F32),
            jax.ShapeDtypeStruct((length, width), BF),
            jax.ShapeDtypeStruct((length, width), BF),
        ],
    )


def attn_backward_kernel(
    full, size, prefix_ref, q_ref, k_ref, qr_ref, kr_ref, v_ref, do_ref, lse_ref, gq_ref, gk_ref,
    cos_ref, sin_ref, *rest,
):
    sums_refs, rest = rest[:size], rest[size:]
    dq_ref, dk_ref, dv_ref, gains_ref, rows_ref, kacc, vacc = rest
    head = pl.program_id(0)
    length = q_ref.shape[0]
    rows = min(512, length)
    prefix = prefix_ref[0]
    factor = HEAD_DIM**-0.5
    kacc[...] = jnp.zeros_like(kacc)
    vacc[...] = jnp.zeros_like(vacc)
    contract = (((0,), (0,)), ((), ()))
    for first in range(0, length, rows):
        last = min(length, max(PREFIX_MAX, first + rows))
        here = slice(first, first + rows)
        scores = masked_scores(qr_ref[here, :], kr_ref[:last, :], first, prefix)
        weights = jnp.exp(scores - lse_ref[here, 0:1])
        grad_rows = do_ref[here, :]
        weight_grad = dot_t(grad_rows, v_ref[:last, :])
        centred = jnp.sum(weight_grad * weights, axis=1, keepdims=True)
        score_grad = (weights * (weight_grad - centred)).astype(BF)
        dq_ref[here, :] = dot(score_grad, kr_ref[:last, :]) * factor
        kacc[:last, :] += lax.dot_general(
            score_grad, qr_ref[here, :], contract, preferred_element_type=F32
        )
        vacc[:last, :] += lax.dot_general(
            weights.astype(BF), grad_rows, contract, preferred_element_type=F32
        )
    dv_ref[...] = vacc[...].astype(BF)
    scales = head_scales(sums_refs, full)
    cosine, sine = cos_ref[...], sin_ref[...]
    which = lax.broadcasted_iota(jnp.int32, (8, length), 0)
    lanes = lax.broadcasted_iota(jnp.int32, (8, HEAD_DIM), 0)
    row_terms = jnp.zeros((8, length), F32)
    gain_terms = jnp.zeros((8, HEAD_DIM), F32)
    for at, (pre_ref, gain_ref, out_ref, raw) in enumerate(
        ((q_ref, gq_ref, dq_ref, dq_ref[...]), (k_ref, gk_ref, dk_ref, kacc[...] * factor))
    ):
        raw = raw.astype(BF).astype(F32)
        normed_grad = raw * cosine - pltpu.roll(raw, HEAD_DIM // 2, 1) * sine
        out_ref[...] = normed_grad
        product = normed_grad * pre_ref[...]
        row_terms = jnp.where(
            which == at, row_sums(product * gain_ref[...].astype(F32)), row_terms
        )
        gain_terms = jnp.where(
            lanes == at,
            jnp.sum(product * scales[:, at : at + 1], axis=0, keepdims=True),
            gain_terms,
        )
    gains_ref[...] = gain_terms
    product = dv_ref[...].astype(F32) * v_ref[...].astype(F32)
    row_terms = jnp.where(which == 2, row_sums(product), row_terms)

    @pl.when(head == 0)
    def _():
        rows_ref[...] = row_terms

    @pl.when(head > 0)
    def _():
        rows_ref[...] += row_terms


def attn_backward(
    prefix, q_pre, k_pre, q_rot, k_rot, v_rows, out_grad, lse, gq, gk, cosine, sine, sums, others=()
):
    length, width = q_pre.shape
    full = width * len(sums)
    head = pl.BlockSpec((length, HEAD_DIM), lambda h, *_: (0, h))
    gain = pl.BlockSpec((1, HEAD_DIM), lambda h, *_: (0, h))
    table = pl.BlockSpec((length, HEAD_DIM), lambda h, *_: (0, 0))
    sums_spec = pl.BlockSpec((8, length), lambda h, *_: (0, 0))
    return launch(
        functools.partial(attn_backward_kernel, full, len(sums)),
        [prefix, q_pre, k_pre, q_rot, k_rot, v_rows, out_grad, lse, gq, gk, cosine, sine, *sums],
        prefetch=1,
            grid=(width // HEAD_DIM,),
            in_specs=[head] * 7 + [gain, gain, table, table] + [sums_spec] * len(sums),
            out_specs=[head, head, head, pl.BlockSpec((8, HEAD_DIM), lambda h, *_: (0, h)), sums_spec],
            scratch=[pltpu.VMEM((length, HEAD_DIM), F32)] * 2,
        out_shape=[
            jax.ShapeDtypeStruct((length, width), F32),
            jax.ShapeDtypeStruct((length, width), F32),
            jax.ShapeDtypeStruct((length, width), BF),
            jax.ShapeDtypeStruct((8, width), F32),
            jax.ShapeDtypeStruct((8, length), F32),
        ],
        others=others,
    )


def norm_back_kernel(full, size, q_ref, k_ref, dq_ref, dk_ref, dv_ref, gq_ref, gk_ref, *rest):
    sums_refs, back_refs, (out_ref, stat_ref) = rest[:size], rest[size : 2 * size], rest[2 * size :]
    width = q_ref.shape[1]
    scales = head_scales(sums_refs, full)
    back = back_refs[0][...]
    squares = sums_refs[0][...]
    for ref, sums_ref in zip(back_refs[1:], sums_refs[1:], strict=True):
        back = back + ref[...]
        squares = squares + sums_ref[...]
    scale = lax.rsqrt(squares / full + EPSILON)
    along = scale * back - scale * scale * scale * (back / full) * squares
    stat_ref[...] = jnp.broadcast_to(along[0:1] + along[1:2] + back[2:3], stat_ref.shape)
    back = jnp.transpose(back)
    grads = []
    for at, (pre_ref, grad_ref, gain_ref) in enumerate(
        ((q_ref, dq_ref, gq_ref), (k_ref, dk_ref, gk_ref))
    ):
        scale = scales[:, at : at + 1]
        pre = pre_ref[...]
        grad = (
            scale * gain_ref[...].astype(F32) * grad_ref[...]
            - pre * (scale * scale * scale * back[:, at : at + 1] / full)
        ).astype(BF)
        grads.append(grad)
    out_ref[:, :width] = grads[0]
    out_ref[:, width : 2 * width] = grads[1]
    out_ref[:, 2 * width :] = dv_ref[...]


def norm_back(q_pre, k_pre, dq, dk, dv, gq, gk, sums, back):
    length, width = q_pre.shape
    full = width * len(sums)
    rows = min(256, length)
    tile = pl.BlockSpec((rows, width), lambda g: (g, 0))
    wide = pl.BlockSpec((rows, 3 * width), lambda g: (g, 0))
    gain = pl.BlockSpec((1, width), lambda g: (0, 0))
    line = pl.BlockSpec((8, rows), lambda g: (0, g))
    return launch(
        functools.partial(norm_back_kernel, full, len(sums)),
        [q_pre, k_pre, dq, dk, dv, gq, gk, *sums, *back],
        grid=(length // rows,),
        in_specs=[tile] * 5 + [gain, gain] + [line] * (2 * len(sums)),
        out_specs=[wide, line],
        out_shape=[
            jax.ShapeDtypeStruct((length, 3 * width), BF),
            jax.ShapeDtypeStruct((8, length), F32),
        ],

    )


def expert_kernel(step, aliased, chunk_ref, n2_ref, cot_ref, router_ref, keep_ref, wg_ref, wu_ref, wd_ref, *rest):
    rest = list(rest)
    own = step == 0
    res_ref = rest.pop(0) if own else None
    rest = rest[aliased:]
    h2t_ref, dg_ref, du_ref, n2t_ref, mix_ref, dn2_ref, probs_ref, mix, dn2, gates, gate_grads = rest
    expert = pl.program_id(0)
    blocks, rows, cols = cot_ref.shape
    lane = lax.broadcasted_iota(jnp.int32, (rows, 128), 1)

    @pl.when(expert == 0)
    def _():
        logits = jnp.where(lane < EXPERTS, dot(n2_ref[...], router_ref[...]), MASKED)
        exponent = jnp.exp(logits - jnp.max(logits, axis=1, keepdims=True))
        probs = exponent / jnp.sum(exponent, axis=1, keepdims=True)
        probs_ref[...] = probs
        gates[...] = probs * keep_ref[...]
        gate_grads[...] = jnp.zeros_like(gate_grads)
        n2t_ref[...] = jnp.transpose(n2_ref[...])
        dn2[...] = jnp.zeros_like(dn2)
        if own:
            mix[...] = res_ref[...]
        else:
            mix[...] = jnp.zeros_like(mix)

    normed = n2_ref[...]
    w_down = wd_ref[0]
    pre_gate = dot(normed, wg_ref[0])
    pre_up = dot(normed, wu_ref[0])
    back = dot_t(cot_ref[0], w_down[:, :cols])
    for t in range(1, blocks):
        back = back + dot_t(cot_ref[t], w_down[:, t * cols : (t + 1) * cols])
    here = lane == expert
    gate = jnp.sum(jnp.where(here, gates[...], 0.0), axis=1, keepdims=True)
    sigmoid = jax.nn.sigmoid(pre_gate)
    activated = pre_gate * sigmoid
    hidden = (activated * pre_up).astype(BF).astype(F32)
    gate_grad = jnp.sum(back * hidden, axis=1, keepdims=True)
    gate_grads[...] += jnp.where(here, gate_grad * keep_ref[...], 0.0)
    back = back * gate
    h2 = (hidden * gate).astype(BF)
    dg = (back * pre_up * sigmoid * (1.0 + pre_gate * (1.0 - sigmoid))).astype(BF)
    du = (back * activated).astype(BF)
    h2t_ref[...] = jnp.transpose(h2)
    dg_ref[...] = dg
    du_ref[...] = du
    mix[...] += dot(h2, w_down)
    dn2[...] += dot_t(dg, wg_ref[0]) + dot_t(du, wu_ref[0])

    @pl.when(expert == EXPERTS - 1)
    def _():
        dn2_ref[:, : blocks * cols] = dn2[...].astype(BF)
        high = gate_grads[...].astype(BF).astype(F32)
        low = gate_grads[...] - high
        if step:
            high = pltpu.roll(high, GROUP * 2 * step, 1)
        low = pltpu.roll(low, GROUP * (2 * step + 1), 1)
        dn2_ref[:, blocks * cols :] = (high + low).astype(BF)
        for t in range(blocks):
            mix_ref[t] = mix[:, t * cols : (t + 1) * cols].astype(BF)


def expert_call(step, chunk, n2, cot, router, keep, wg, wu, wd, residual, carried):
    rows, full = n2.shape
    blocks, length, cols = cot.shape
    hidden = wg.shape[2]
    own = step == 0
    in_specs = [
        pl.BlockSpec((rows, full), lambda e, c: (0, 0)),
        pl.BlockSpec((blocks, rows, cols), lambda e, c: (0, c[0], 0)),
        pl.BlockSpec((full, 128), lambda e, c: (0, 0)),
        pl.BlockSpec((rows, 128), lambda e, c: (c[0], 0)),
        pl.BlockSpec((1, full, hidden), lambda e, c: (e, 0, 0)),
        pl.BlockSpec((1, full, hidden), lambda e, c: (e, 0, 0)),
        pl.BlockSpec((1, hidden, full), lambda e, c: (e, 0, 0)),
    ]
    operands = [chunk, n2, cot, router, keep, wg, wu, wd]
    if own:
        in_specs.append(pl.BlockSpec((rows, full), lambda e, c: (0, 0)))
        operands.append(residual)
    aliases = {len(operands) + k: k for k in range(len(carried))}
    in_specs += [pl.BlockSpec(memory_space=pl.ANY)] * len(carried)
    operands += list(carried)
    slab = pl.BlockSpec((rows, hidden), lambda e, c: (c[0], e))
    return launch(
        functools.partial(expert_kernel, step, len(carried)),
        [*operands],
        prefetch=1,
            grid=(EXPERTS,),
            in_specs=in_specs,
            out_specs=[
                pl.BlockSpec((hidden, rows), lambda e, c: (e, c[0])),
                slab,
                slab,
                pl.BlockSpec((full, rows), lambda e, c: (0, c[0])),
                pl.BlockSpec((blocks, rows, cols), lambda e, c: (0, c[0], 0)),
                pl.BlockSpec((rows, full + 128), lambda e, c: (0, 0)),
                pl.BlockSpec((rows, 128), lambda e, c: (0, 0)),
            ],
            scratch=[
                pltpu.VMEM((rows, full), F32),
                pltpu.VMEM((rows, full), F32),
                pltpu.VMEM((rows, 128), F32),
                pltpu.VMEM((rows, 128), F32),
            ],
        out_shape=[
            jax.ShapeDtypeStruct((EXPERTS * hidden, length), BF),
            jax.ShapeDtypeStruct((length, EXPERTS * hidden), BF),
            jax.ShapeDtypeStruct((length, EXPERTS * hidden), BF),
            jax.ShapeDtypeStruct((full, length), BF),
            jax.ShapeDtypeStruct((blocks, length, cols), BF),
            jax.ShapeDtypeStruct((rows, full + 128), BF),
            jax.ShapeDtypeStruct((rows, 128), F32),
        ],
        aliases=aliases,

        token=6,
    )


def arrange_kernel(owners_ref, *refs):
    blocks, (branch_ref, rows_ref, out_ref) = refs[:-3], refs[-3:]
    for k, ref in enumerate(blocks):
        rows_ref[owners_ref[k]] = ref[...]
    out_ref[...] = branch_ref[...]


def arrange(owners, blocks, branch):
    rows, width = blocks[0].shape
    full = branch.shape[1]
    chunk = rows // 2
    return launch(
        arrange_kernel,
        [owners, *blocks, branch],
        prefetch=1,
        grid=(2,),
        in_specs=[pl.BlockSpec((chunk, width), lambda g, o: (g, 0))] * len(blocks)
        + [pl.BlockSpec((chunk, full), lambda g, o: (g, 0))],
        out_specs=[
            pl.BlockSpec((len(blocks), chunk, width), lambda g, o: (0, g, 0)),
            pl.BlockSpec((chunk, full), lambda g, o: (g, 0)),
        ],
        out_shape=[
            jax.ShapeDtypeStruct((len(blocks), rows, width), BF),
            jax.ShapeDtypeStruct((rows, full), BF),
        ],
    )


def gate_up_kernel(n2t_ref, dg_ref, du_ref, out_ref):
    turned = n2t_ref[...]
    out_ref[0, 0] = dot(turned, dg_ref[...]).astype(BF)
    out_ref[1, 0] = dot(turned, du_ref[...]).astype(BF)


def gate_up_grads(n2t, dg, du):
    full, length = n2t.shape
    hidden = dg.shape[1] // EXPERTS
    slab = pl.BlockSpec((length, hidden), lambda e: (0, e))
    return launch(
        gate_up_kernel,
        [n2t, dg, du],
        grid=(EXPERTS,),
        in_specs=[pl.BlockSpec((full, length), lambda e: (0, 0)), slab, slab],
        out_specs=pl.BlockSpec((2, 1, full, hidden), lambda e: (0, e, 0, 0)),
        out_shape=jax.ShapeDtypeStruct((2, EXPERTS, full, hidden), BF),
    )


def down_kernel(table_ref, h2t_ref, cot_ref, out_ref):
    cols = cot_ref.shape[2]
    for t in range(cot_ref.shape[0]):
        out_ref[0, :, t * cols : (t + 1) * cols] = dot(h2t_ref[...], cot_ref[t]).astype(BF)


def down_grads(table, h2t, cot, n):
    wide, length = h2t.shape
    blocks, _, cols = cot.shape
    rows = wide // n
    steps = n // 2
    return launch(
        down_kernel,
        [table, h2t, cot],
        prefetch=1,
        grid=(steps,),
        in_specs=[
            pl.BlockSpec((rows, length), lambda g, t: (t[g], 0)),
            pl.BlockSpec((blocks, length, cols), lambda g, t: (0, 0, 0)),
        ],
        out_specs=pl.BlockSpec((1, rows, blocks * cols), lambda g, t: (g, 0, 0)),
        out_shape=jax.ShapeDtypeStruct((steps, rows, blocks * cols), BF),
    )


def middle_kernel(size, owners_ref, *refs):
    heads, x_refs = refs[:size], refs[size : 2 * size]
    wo_ref, gain_ref, res_ref, n2_ref = refs[2 * size :]
    step = pl.program_id(0)
    cols = x_refs[0].shape[1]
    width = heads[0].shape[1]

    @pl.when(step == 0)
    def _():
        for k, ref in enumerate(x_refs):
            first = pl.multiple_of(owners_ref[k] * cols, 128)
            res_ref[:, pl.ds(first, cols)] = ref[...].astype(F32)

    weights = wo_ref[...].reshape(width, -1)
    for k, ref in enumerate(heads):

        @pl.when(step == k)
        def _(ref=ref):
            res_ref[...] += dot(ref[...], weights)

    @pl.when(step == size - 1)
    def _():
        residual = res_ref[...]
        scale = lax.rsqrt(jnp.mean(residual * residual, axis=1, keepdims=True) + EPSILON)
        for t in range(size):
            here = slice(t * cols, (t + 1) * cols)
            gain = gain_ref[t, 1:2, :].astype(F32)
            n2_ref[:, here] = (residual[:, here] * scale * gain).astype(BF)


def middle(owners, attended, received, w_out, x_blocks, gains):
    size = len(x_blocks)
    groups, _, part, full = w_out.shape
    width, cols = groups * part, full // size
    rows = attended.shape[0] // size
    return launch(
        functools.partial(middle_kernel, size),
        [owners, attended, *received, *x_blocks, w_out, gains],
        prefetch=1,
        grid=(size,),
        in_specs=[pl.BlockSpec((rows, width), lambda t, o: (o[0], 0))]
        + [pl.BlockSpec((rows, width), lambda t, o: (0, 0))] * (size - 1)
        + [pl.BlockSpec((rows, cols), lambda t, o: (o[0], 0))] * size
        + [
            pl.BlockSpec((groups, 1, part, full), lambda t, o: (0, o[t], 0, 0)),
            pl.BlockSpec((size, 16, cols), lambda t, o: (0, 0, 0)),
        ],
        out_specs=[pl.BlockSpec((rows, full), lambda t, o: (0, 0))] * 2,
        out_shape=[
            jax.ShapeDtypeStruct((rows, full), F32),
            jax.ShapeDtypeStruct((rows, full), BF),
        ],
    )


def middle_back_kernel(
    mine_ref, own_ref, received_ref, probs_ref, router_ref, res_ref, n2_ref, cot_ref, gain_ref, wo_ref,
    branch_ref, parts_ref, *out_refs,
):
    step = pl.program_id(0)
    blocks, rows, cols = cot_ref.shape
    full = blocks * cols

    @pl.when(step == 0)
    def _():
        probs = probs_ref[...]
        parts = own_ref[:, full:].astype(F32) + received_ref[:, full:].astype(F32)
        prob_grad = parts
        for group in range(1, 2 * blocks):
            prob_grad = prob_grad + pltpu.roll(parts, 128 - GROUP * group, 1)
        lane = lax.broadcasted_iota(jnp.int32, (rows, 128), 1)
        prob_grad = jnp.where(lane < EXPERTS, prob_grad, 0.0)
        centred = jnp.sum(prob_grad * probs, axis=1, keepdims=True)
        logit_grad = (probs * (prob_grad - centred)).astype(BF)
        grad = (
            own_ref[:, :full].astype(F32)
            + received_ref[:, :full].astype(F32)
            + dot_t(logit_grad, router_ref[...])
        )
        residual = res_ref[...]
        scale = lax.rsqrt(jnp.mean(residual * residual, axis=1, keepdims=True) + EPSILON)
        stat = jnp.zeros((rows, 1), F32)
        for t in range(blocks):
            here = slice(t * cols, (t + 1) * cols)
            gain = gain_ref[t, 1:2, :].astype(F32)
            stat = stat + jnp.sum(residual[:, here] * gain * grad[:, here], axis=1, keepdims=True)
        stat = scale * scale * scale * stat / full
        for t in range(blocks):
            here = slice(t * cols, (t + 1) * cols)
            gain = gain_ref[t, 1:2, :].astype(F32)
            branch_ref[:, here] = (
                cot_ref[t].astype(F32) + scale * gain * grad[:, here] - residual[:, here] * stat
            ).astype(BF)
        router_part = lax.dot_general(
            logit_grad, n2_ref[...], (((0,), (0,)), ((), ())), preferred_element_type=F32
        )[:8]
        norm_part = jnp.sum(grad * residual * scale, axis=0, keepdims=True)
        which = lax.broadcasted_iota(jnp.int32, (8, full), 0)
        parts_ref[...] = jnp.where(which == EXPERTS, norm_part, router_part)

    product = dot_t(branch_ref[...], wo_ref[...].reshape(-1, full)).astype(BF)
    for k, ref in enumerate(out_refs):

        @pl.when(step == k)
        def _(ref=ref):
            ref[...] = product


def middle_back(mine, own, received, probs, router, residual, n2, cot, gains, w_out):
    blocks, _, cols = cot.shape
    rows, full = residual.shape
    groups, _, part, _ = w_out.shape
    width = groups * part
    whole = pl.BlockSpec((rows, full), lambda t, m: (0, 0))
    wide = pl.BlockSpec((rows, full + 128), lambda t, m: (0, 0))
    lanes = pl.BlockSpec((rows, 128), lambda t, m: (0, 0))
    return launch(
        middle_back_kernel,
        [mine, own, received, probs, router, residual, n2, cot, gains, w_out],
        prefetch=1,
            grid=(blocks,),
            in_specs=[
                wide,
                wide,
                lanes,
                pl.BlockSpec((full, 128), lambda t, m: (0, 0)),
                whole,
                whole,
                pl.BlockSpec((blocks, rows, cols), lambda t, m: (0, m[0], 0)),
                pl.BlockSpec((blocks, 16, cols), lambda t, m: (0, 0, 0)),
                pl.BlockSpec((groups, 1, part, full), lambda t, m: (0, lax.rem(m[0] + t, blocks), 0, 0)),
            ],
            out_specs=[
                whole,
                pl.BlockSpec((8, full), lambda t, m: (0, 0)),
            ]
            + [pl.BlockSpec((rows, width), lambda t, m: (0, 0))] * blocks,
        out_shape=[
            jax.ShapeDtypeStruct((rows, full), BF),
            jax.ShapeDtypeStruct((8, full), F32),
        ]
        + [jax.ShapeDtypeStruct((rows, width), BF)] * blocks,
    )


def reversed_bits(at, bits):
    return sum(((at >> b) & 1) << (bits - 1 - b) for b in range(bits)) if bits else at


def column_grad_kernel(left_ref, right_ref, w_ref, out_ref, gain_ref):
    product = dot(jnp.transpose(left_ref[...]), right_ref[...])
    out_ref[...] = product.astype(BF)
    gain_ref[...] = jnp.broadcast_to(row_sums(product * w_ref[...].astype(F32)), gain_ref.shape)


def column_grads(left, right, weights):
    length, full = left.shape
    width = right.shape[1]
    piece = min(512, full)
    tile = pl.BlockSpec((piece, width), lambda g: (g, 0))
    return launch(
        column_grad_kernel,
        [left, right, weights],
        grid=(full // piece,),
        in_specs=[
            pl.BlockSpec((length, piece), lambda g: (0, g)),
            pl.BlockSpec((length, width), lambda g: (0, 0)),
            tile,
        ],
        out_specs=[tile, pl.BlockSpec((8, piece), lambda g: (0, g))],
        out_shape=[
            jax.ShapeDtypeStruct((full, width), BF),
            jax.ShapeDtypeStruct((8, full), F32),
        ],
    )


def row_grad_kernel(rows_ref, left_ref, *rest):
    blocks, (out_ref, turned_left) = rest[:-2], rest[-2:]
    rows = blocks[0].shape[0]

    @pl.when(pl.program_id(0) == 0)
    def _():
        for k in range(len(blocks)):
            first = pl.multiple_of(rows_ref[k] * rows, rows)
            turned_left[:, k * rows : (k + 1) * rows] = jnp.transpose(
                left_ref[pl.ds(first, rows), :]
            )

    total = None
    for k, block in enumerate(blocks):
        term = dot(turned_left[:, k * rows : (k + 1) * rows], block[...])
        total = term if total is None else total + term
    out_ref[...] = total.astype(BF)


def row_grads(owners, left, blocks):
    length, width = left.shape
    rows, full = blocks[0].shape
    piece = min(512, full)
    return launch(
        row_grad_kernel,
        [owners, left, *blocks],
        prefetch=1,
        grid=(full // piece,),
        in_specs=[pl.BlockSpec((length, width), lambda g, o: (0, 0))]
        + [pl.BlockSpec((rows, piece), lambda g, o: (0, g))] * len(blocks),
        out_specs=pl.BlockSpec((width, piece), lambda g, o: (0, g)),
        out_shape=jax.ShapeDtypeStruct((width, full), BF),
        scratch=[pltpu.VMEM((width, length), BF)],
    )


def input_kernel(owner_ref, grad_ref, w_ref, *rest):
    total = dot_t(grad_ref[...], w_ref[...])
    if len(rest) == 2:
        total = total + rest[0][...].astype(F32)
    rest[-1][...] = total.astype(BF)


def input_grads(owner, cols, grad, w_all, received=None, work=1):
    length, width = grad.shape
    rows = min(256, length)
    tile = pl.BlockSpec((rows, cols), lambda g, o: (g, 0))
    return launch(
        input_kernel,
        [owner, grad, w_all, *([] if received is None else [received])],
        prefetch=1,
            grid=(length // rows,),
            in_specs=[
                pl.BlockSpec((rows, width), lambda g, o: (g, 0)),
                pl.BlockSpec((cols, width), lambda g, o: (o[0], 0)),
            ]
            + ([] if received is None else [tile]),
            out_specs=tile,
        out_shape=jax.ShapeDtypeStruct((length, cols), BF),

        work=work,
    )


def mix_kernel(owner_ref, mix_ref, *rest):
    if len(rest) == 1:
        rest[0][...] = mix_ref[0]
    else:
        rest[1][...] = added(mix_ref[0], rest[0][...])


def mix_block(owner, mix, received=None, work=1):
    blocks, length, cols = mix.shape
    chunk = length // 2
    tile = pl.BlockSpec((chunk, cols), lambda g, o: (g, 0))
    return launch(
        mix_kernel,
        [owner, mix, *([] if received is None else [received])],
        prefetch=1,
            grid=(2,),
            in_specs=[pl.BlockSpec((1, chunk, cols), lambda g, o: (o[0], g, 0))]
            + ([] if received is None else [tile]),
            out_specs=tile,
        out_shape=jax.ShapeDtypeStruct((length, cols), BF),
        work=work,
    )


def final_kernel(
    full, owners_ref, grad_ref, w_ref, received_ref, tokens_ref, sums_ref, stat_ref, gain_ref, *rest
):
    blocks, out_ref = rest[:-1], rest[-1]
    step = pl.program_id(0)
    branch = blocks[0][...]
    for k in range(1, len(blocks)):
        branch = jnp.where(step == k, blocks[k][...], branch)
    scale = lax.rsqrt(sums_ref[...] / full + EPSILON)
    scale_one = jnp.transpose(scale)[:, 2:3]
    stat = jnp.transpose(stat_ref[...])[:, 0:1] / full * scale_one * scale_one
    normed_grad = dot_t(grad_ref[...], w_ref[...]) + received_ref[...].astype(F32)
    out_ref[...] = (
        branch.astype(F32)
        + scale_one * gain_ref[...].astype(F32) * normed_grad
        - tokens_ref[...].astype(F32) * stat
    )


def final_grads(owners, grad, w_all, received, tokens, sums, stat, gain, blocks):
    length, cols = tokens.shape
    width = grad.shape[1]
    rows = length // len(blocks)
    tile = pl.BlockSpec((rows, cols), lambda k, o: (o[k], 0))
    line = pl.BlockSpec((8, rows), lambda k, o: (0, o[k]))
    return launch(
        functools.partial(final_kernel, cols * len(blocks)),
        [owners, grad, w_all, received, tokens, sums, stat, gain, *blocks],
        prefetch=1,
            grid=(len(blocks),),
            in_specs=[
                pl.BlockSpec((rows, width), lambda k, o: (o[k], 0)),
                pl.BlockSpec((cols, width), lambda k, o: (o[0], 0)),
                tile,
                tile,
                line,
                line,
                pl.BlockSpec((1, cols), lambda k, o: (0, 0)),
            ]
            + [pl.BlockSpec((rows, cols), lambda k, o: (0, o[0]))] * len(blocks),
            out_specs=tile,
        out_shape=jax.ShapeDtypeStruct((length, cols), F32),
    )


def piece_specs(shape, steps):
    block = (1,) + shape
    return [
        pl.BlockSpec(block, lambda a, pos: (jnp.minimum(pos[a], steps - 1), 0, 0)),
        pl.BlockSpec(block, lambda a, pos: (jnp.maximum(pos[a] - steps, 0), 0, 0)),
    ]


def pieces_kernel(steps, pos_ref, low_ref, high_ref, out_ref):
    low = pos_ref[pl.program_id(0)] < steps
    out_ref[...] = jnp.where(low, low_ref[0].astype(F32), high_ref[0].astype(F32))


def widen_pieces(pos, halves, n):
    steps, rows, width = halves[0].shape
    return launch(
        functools.partial(pieces_kernel, steps),
        [pos, *halves],
        prefetch=1,
        grid=(n,),
        in_specs=piece_specs((rows, width), steps),
        out_specs=pl.BlockSpec((rows, width), lambda a, pos: (a, 0)),
        out_shape=jax.ShapeDtypeStruct((rows * n, width), F32),
    )


def projections_kernel(sum_ref, q_ref, k_ref, v_ref):
    width = q_ref.shape[1]
    for at, out_ref in enumerate((q_ref, k_ref, v_ref)):
        out_ref[...] = sum_ref[:, at * width : (at + 1) * width].astype(F32)


def widen_projections(total):
    full, width = total.shape
    out = width // 3
    piece = min(256, full)
    tile = pl.BlockSpec((piece, out), lambda g: (g, 0))
    return launch(
        projections_kernel,
        [total],
        grid=(full // piece,),
        in_specs=[pl.BlockSpec((piece, width), lambda g: (g, 0))],
        out_specs=[tile] * 3,
        out_shape=[jax.ShapeDtypeStruct((full, out), F32)] * 3,
    )


def experts_kernel(held_ref, gate_ref, up_ref):
    gate_ref[0] = held_ref[0, 0].astype(F32)
    up_ref[0] = held_ref[1, 0].astype(F32)


def widen_experts(held):
    _, experts, full, hidden = held.shape
    tall = pl.BlockSpec((1, full, hidden), lambda e: (e, 0, 0))
    return launch(
        experts_kernel,
        [held],
        grid=(experts,),
        in_specs=[pl.BlockSpec((2, 1, full, hidden), lambda e: (0, e, 0, 0))],
        out_specs=[tall, tall],
        out_shape=[jax.ShapeDtypeStruct((experts, full, hidden), F32)] * 2,
    )


def kept_experts(routes, order):
    length = routes.shape[0]
    token, which = order // TOP, order % TOP
    onehot = (token[:, None] == jnp.arange(length, dtype=jnp.int32)[None, :]).astype(BF)
    named = (routes[:, :, None] == jnp.arange(8, dtype=jnp.int32)).astype(BF).reshape(length, TOP * 8)
    ordered = dot(onehot, named).reshape(-1, TOP, 8)
    choose = jnp.sum(
        jnp.where(which[:, None, None] == jnp.arange(TOP)[None, :, None], ordered, 0.0), axis=1
    )
    kept = jnp.where(jnp.cumsum(choose, axis=0) <= CAP, choose, 0.0).astype(BF)
    kept = jnp.pad(kept, ((0, 0), (0, 120)))
    return lax.dot_general(onehot, kept, (((0,), (0,)), ((), ())), preferred_element_type=F32)


def on_device(
    tokens, cotangent, norm1_gain, w_query, w_key, w_value, query_gain, key_gain, w_output,
    norm2_gain, router, w_gate, w_up, w_down, routes, prefix, slot_order,
):
    size, n = lax.axis_size("tensor"), lax.axis_size("dp")
    mine, group = lax.axis_index("tensor"), lax.axis_index("dp")
    length, cols = tokens.shape
    full = cols * size
    rows = length // size
    steps = range(1, size)
    Chain.token = None

    def add(*terms):
        return functools.reduce(jnp.add, terms)

    here = mine.astype(jnp.int32)[None]

    rel = rel_table(swap_masks(n))
    table = jnp.asarray(rel, jnp.int32) ^ group
    positions = jnp.asarray([rel.index(v) for v in range(n)], jnp.int32)[
        jnp.arange(n, dtype=jnp.int32) ^ group
    ]
    half = n // 2
    owners = ((mine - jnp.arange(size)) % size).astype(jnp.int32)

    def owner(step):
        return owners[step : step + 1]

    def by_owner(own, *others):
        return place(size, [b[None] for b in others], mine, own[None])

    part = w_output.shape[0] // n
    gains = jnp.concatenate([norm1_gain[None], norm2_gain[None], jnp.zeros((14, cols), BF)])
    w_piece = jnp.concatenate(
        [
            lax.dynamic_slice_in_dim(w_output, group * part, part, 0),
            jnp.pad(gains, ((0, 0), (0, full - cols))),
        ]
    )
    w_blocks, x_blocks = [w_piece], [tokens]
    for step in steps:
        w_blocks.append(send(w_blocks[-1], 1, size))
    w_mixed = by_owner(*w_blocks)
    w_out = lax.all_gather(w_mixed[:, :part], "dp", axis=0)
    gains = w_mixed[:, part:, :cols]
    w_all = side_by_side([w_query, w_key, w_value])
    keep = kept_experts(routes, slot_order[0])
    router_wide = jnp.pad(router, ((0, 0), (0, 128 - EXPERTS)))
    halfway = HEAD_DIM // 2
    freqs = ROPE_BASE ** (-(jnp.arange(halfway, dtype=F32) * 2.0 / HEAD_DIM))
    angles = jnp.arange(length, dtype=F32)[:, None] * freqs[None, :]
    cosine = jnp.concatenate([jnp.cos(angles)] * 2, axis=1)
    sine = jnp.concatenate([-jnp.sin(angles), jnp.sin(angles)], axis=1)
    for step in steps:
        x_blocks.append(send(x_blocks[-1], 1, size))
    late_cot = copied(cotangent, (x_blocks[-2], keep, router_wide, cosine, sine))
    cot = lax.all_gather(late_cot, "tensor", axis=0)
    normed_one, q_pre, k_pre, v_rows, own_sums = qkv_call(
        owners, x_blocks, gains, w_query, w_key, w_value
    )
    sums = [own_sums] + [send(own_sums, step, size) for step in steps]

    gq, gk = query_gain[None], key_gain[None]
    attended, lse, q_rot, k_rot = attn_forward(
        prefix, q_pre, k_pre, v_rows, gq, gk, cosine, sine, sums
    )

    received = [
        send(lax.dynamic_slice_in_dim(attended, (mine + step) % size * rows, rows, 0), step, size)
        for step in steps
    ]
    residual, normed_two = middle(owners, attended, received, w_out, x_blocks, gains)

    def add_wide(a, b, work=1):
        return add_blocks(a[None], b[None], work)[0]

    chunks = [copied(normed_two, (cot,))]
    chunks.append(send(chunks[0], 1, size))
    carried, later, dn2_flying = (), [], None
    for step in range(size):
        outs = expert_call(
            step, owner(step), chunks[step], cot, router_wide, keep, w_gate, w_up, w_down,
            residual if step == 0 else None, carried,
        )
        carried = outs[:5]
        if step < size - 2:
            chunks.append(send(copied(chunks[-1]), 1, size))
        if step == 0:
            own_dn2, expert_probs = outs[5:]
        else:
            later.append(outs[5])
        if step > 3:
            dn2_flying = send(add_wide(later.pop(0), dn2_flying), 1, size)
        elif step == min(3, size - 1):
            dn2_flying = send(copied(later.pop(0)), 1, size)
    h2t, dg, du, n2t, mix = carried

    expert_grads = lax.psum(gate_up_grads(n2t, dg, du), "dp")
    sum_down = Sum(n, 2, down_grads(table[half:], h2t, cot, n))
    dn2_flying = send(add_wide(later.pop(0), dn2_flying, LONG), 1, size)
    sum_down.keep = down_grads(table[:half], h2t, cot, n)
    for term in later:
        dn2_flying = send(add_wide(term, dn2_flying), 1, size)
    sum_down.step()

    branch_rows, small, *out_rows = middle_back(
        here, own_dn2, dn2_flying, expert_probs, router_wide, residual, normed_two, cot, gains, w_out
    )

    received = [send(out_rows[step], step, size) for step in steps]
    out_grad, branch_rows = arrange(owners, [out_rows[0]] + received, branch_rows)
    branch_blocks = [branch_rows, send(branch_rows, 1, size)]
    sum_down.step()
    dq, dk, dv, gain_grads, own_back = attn_backward(
        prefix, q_pre, k_pre, q_rot, k_rot, v_rows, out_grad.reshape(length, -1), lse, gq, gk,
        cosine, sine, sums,
    )
    back = [own_back] + [send(own_back, step, size) for step in steps]
    sum_down.step()
    branch_blocks.append(send(copied(branch_blocks[1], tuple(back[1:])), 1, size))
    grad_qkv, stat_one = norm_back(q_pre, k_pre, dq, dk, dv, gq, gk, sums, back)
    in_grads, gain_part = column_grads(normed_one, grad_qkv, w_all)
    sum_down.step()
    for step in range(3, size):
        branch_blocks.append(send(copied(branch_blocks[-1]), 1, size))
    packed = jnp.concatenate([jnp.concatenate([small[:7], gain_part[7:]]), gain_grads], axis=1)
    width = 3 * w_query.shape[1]
    extra = jnp.pad(packed.reshape(-1), (0, 32 * width - packed.size)).astype(BF).reshape(32, width)
    out_grads = row_grads(owners, attended, branch_blocks)
    extra = copied(extra, (expert_grads,))
    in_grads, out_grads, extra = lax.psum((in_grads, out_grads, extra), "dp")
    dn1_flying = send(input_grads(owner(1), cols, grad_qkv, w_all, work=LONG), 1, size)
    mix_flying = send(mix_block(owner(1), mix), 1, size)
    sum_down.step()
    for step in range(2, size):
        dn1_flying = send(input_grads(owner(step), cols, grad_qkv, w_all, dn1_flying), 1, size)
        sum_down.step()
        if step == 2:
            grad_gate, grad_up = widen_experts(expert_grads)
        if step < size - 1:
            mix_flying = send(mix_block(owner(step), mix, mix_flying), 1, size)
    mix_flying = send(mix_block(owner(size - 1), mix, mix_flying), 1, size)

    grad_tokens = final_grads(
        owners, grad_qkv, w_all, dn1_flying, tokens, own_sums, stat_one, norm1_gain[None],
        branch_blocks,
    )
    for _ in range(2 * len(swap_masks(n))):
        sum_down.step()
    grad_down = widen_pieces(positions, sum_down.finish(), n).reshape(w_down.shape)

    mixed = mix_block(owner(0), mix, mix_flying)
    extra = copied(extra)
    packed = extra.astype(F32).reshape(-1)[: packed.size].reshape(packed.shape)
    gain_total, packed = packed[:2, full:], packed[:, :full]
    packed = [packed] + [send(packed, step, size) for step in steps]
    grad_query, grad_key, grad_value = widen_projections(in_grads)
    grad_output = out_grads.astype(F32)

    packed = add(*packed)
    grad_router = packed[:EXPERTS].T
    own = lax.dynamic_slice_in_dim(packed[EXPERTS:], mine * cols, cols, 1)
    grad_norm2_gain = own[0]
    grad_norm1_gain = own[1] / norm1_gain.astype(F32)
    grad_query_gain, grad_key_gain = gain_total[0], gain_total[1]
    return (
        mixed, grad_tokens, grad_norm1_gain, grad_query, grad_key, grad_value, grad_query_gain,
        grad_key_gain, grad_output, grad_norm2_gain, grad_router, grad_gate, grad_up, grad_down,
    )


def solution(mesh):
    rows, weight_cols, weight_rows = P("dp", "tensor"), P(None, "tensor"), P("tensor", None)
    vector, expert_cols, expert_rows = P("tensor"), P(None, None, "tensor"), P(None, "tensor", None)
    return jax.shard_map(
        on_device,
        mesh=mesh,
        in_specs=(
            rows, rows, vector, weight_cols, weight_cols, weight_cols, vector, vector, weight_rows,
            vector, P(), expert_cols, expert_cols, expert_rows, P("dp", None), P("dp"),
            P("dp", None),
        ),
        out_specs=(
            rows, rows, vector, weight_cols, weight_cols, weight_cols, vector, vector, weight_rows,
            vector, P(), expert_cols, expert_cols, expert_rows,
        ),
        check_vma=False,
    )
```

```python
import functools

import jax
import jax.numpy as jnp
from jax import lax
from jax.experimental import pallas as pl
from jax.experimental.pallas import tpu as pltpu
from jax.sharding import PartitionSpec as P

HEAD_DIM = 128
EXPERTS = 6
TOP = 3
CAP = 640
PREFIX_MAX = 512

EPSILON = 1e-05
ROPE_BASE = 10000.0
MASKED = -1e30
GROUP = 8
LONG = 2e13
BF = jnp.bfloat16
F32 = jnp.float32
VMEM_LIMIT = 56 * 1024 * 1024


class Chain:
    token = None


def launch(
    body, operands, *, grid, in_specs, out_specs, out_shape, work=1, prefetch=0, scratch=(), aliases=None,
    token=0, others=(),
):
    operands = list(operands)
    unread = [field for field in (Chain.token, *others) if field is not None]
    unread = [field for field in unread if all(field is not own for own in operands)]
    first, last = len(operands), len(operands) + len(unread)

    def kernel(*refs):
        body(*refs[:first], *refs[last:])

    out = pl.pallas_call(
        kernel,
        grid_spec=pltpu.PrefetchScalarGridSpec(
            num_scalar_prefetch=prefetch,
            grid=grid,
            in_specs=list(in_specs) + [pl.BlockSpec(memory_space=pl.ANY)] * len(unread),
            out_specs=out_specs,
            scratch_shapes=list(scratch),
        ),
        out_shape=out_shape,
        input_output_aliases=aliases or {},
        compiler_params=pltpu.CompilerParams(vmem_limit_bytes=VMEM_LIMIT),
        cost_estimate=pl.CostEstimate(flops=int(work), bytes_accessed=1, transcendentals=0),
    )(*operands, *unread)
    Chain.token = out[token] if isinstance(out, (list, tuple)) else out
    return out


def dot(a, b):
    return jnp.dot(a, b, preferred_element_type=F32)


def dot_t(a, b):
    return lax.dot_general(a, b, (((1,), (1,)), ((), ())), preferred_element_type=F32)


def row_sums(field):
    folded = field[:, :128]
    for at in range(128, field.shape[1], 128):
        folded = folded + field[:, at : at + 128]
    return jnp.sum(jnp.transpose(folded), axis=0, keepdims=True)


def ring(size):
    return [(at, (at + 1) % size) for at in range(size)]


def send(value, step, size):
    return lax.ppermute(value, "tensor", [(at, (at + step) % size) for at in range(size)])


def swap(value, mask, n):
    return lax.ppermute(value, "dp", [(at, at ^ mask) for at in range(n)])


def take(blocks, at):
    return lax.dynamic_slice_in_dim(blocks, at, 1, 0)


def place(size, received, mine, own):
    out = lax.dynamic_update_slice_in_dim(jnp.zeros((size,) + own.shape[1:], own.dtype), own, mine, 0)
    for step, block in enumerate(received, 1):
        out = lax.dynamic_update_slice_in_dim(out, block, (mine - step) % size, 0)
    return out


def swap(field, mask, n):
    return lax.ppermute(field, "dp", [(at, at ^ mask) for at in range(n)])


def swap_masks(n):
    return [1 << bit for bit in range(n.bit_length() - 1)]


def rel_table(masks):
    bits = len(masks)
    return [
        sum(masks[s] for s in range(bits) if (p >> (bits - 1 - s)) & 1) for p in range(1 << bits)
    ]


def blockwise(body, ins, outs, others=(), work=1):
    chunks = 2 if ins[0].shape[1] % 32 == 0 else 1

    def spec(shape):
        return pl.BlockSpec((shape[0], shape[1] // chunks, shape[2]), lambda g: (0, g, 0))

    def kernel(*refs):
        body(refs[: len(ins)], refs[len(ins) :])

    return launch(
        kernel,
        [*ins],
        grid=(chunks,),
        in_specs=[spec(field.shape) for field in ins],
        out_specs=[spec(shape) for shape in outs],
        out_shape=[jax.ShapeDtypeStruct(shape, BF) for shape in outs],
        others=others,
        work=work,
    )


def added(a, b):
    return (a.astype(F32) + b.astype(F32)).astype(BF)


def copied(field, others=()):
    def body(ins, outs):
        outs[0][...] = ins[0][...]

    return blockwise(body, [field[None]], [(1,) + field.shape], others)[0][0]


def side_by_side(fields):
    def body(ins, outs):
        at = 0
        for ref in ins:
            outs[0][:, :, at : at + ref.shape[2]] = ref[...]
            at += ref.shape[2]

    width = sum(field.shape[1] for field in fields)
    return blockwise(body, [field[None] for field in fields], [(1, fields[0].shape[0], width)])[0][0]


def add_blocks(a, b, work=1):
    def body(ins, outs):
        outs[0][...] = added(ins[0][...], ins[1][...])

    return blockwise(body, [a, b], [a.shape], work=work)[0]


class Sum:
    def __init__(self, n, parts, first):
        self.n, self.parts = n, parts
        self.masks = swap_masks(n)
        self.stage = 0
        self.flying = [swap(first, self.masks[0], n)]

    def send(self, fields, stage):
        self.flying = []
        for part, field in enumerate(fields):
            mask = self.masks[stage] if part == 0 else self.masks[-stage]
            self.flying.append(swap(field, mask, self.n))

    def split(self, keeps, received):
        count, rows, width = keeps[0].shape
        wide = width // self.parts if len(keeps) < self.parts else width

        def body(ins, outs):
            for part in range(self.parts):
                at = part if len(keeps) == self.parts else 0
                here = slice(part * wide, (part + 1) * wide) if at != part else slice(0, wide)
                for i in range(count):
                    total = added(ins[2 * at][i, :, here], ins[2 * at + 1][i, :, here])
                    if part == 0:
                        away, place_at = i >= count // 2, i % (count // 2)
                    else:
                        away, place_at = i % 2 == 1, i // 2
                    outs[2 * part + (0 if away else 1)][place_at] = total

        ins = [field for pair in zip(keeps, received, strict=True) for field in pair]
        outs = blockwise(body, ins, [(count // 2, rows, wide)] * (2 * self.parts))
        return outs[0::2], outs[1::2]

    def total(self, keeps, received):
        def body(ins, outs):
            for part, out in enumerate(outs):
                out[...] = added(ins[2 * part][...], ins[2 * part + 1][...])

        ins = [field for pair in zip(keeps, received, strict=True) for field in pair]
        return blockwise(body, ins, [field.shape for field in keeps])

    def joined(self, last, keeps, received):
        count, rows, wide = keeps[0].shape

        def body(ins, outs):
            for part in range(self.parts):
                out = outs[0] if last else outs[part]
                here = slice(part * wide, (part + 1) * wide) if last else slice(0, wide)
                for i in range(count):
                    low, high = (i, count + i) if part == 0 else (2 * i, 2 * i + 1)
                    out[low, :, here] = ins[2 * part][i]
                    out[high, :, here] = ins[2 * part + 1][i]

        ins = [field for pair in zip(keeps, received, strict=True) for field in pair]
        if last:
            return blockwise(body, ins, [(2 * count, rows, wide * self.parts)])
        return blockwise(body, ins, [(2 * count, rows, wide)] * self.parts)

    def step(self):
        bits = len(self.masks)
        if self.stage == 2 * bits - 1:
            return
        received = self.flying
        self.stage += 1
        if self.stage < bits:
            keep = [self.keep] if self.stage == 1 else self.keep
            away, self.keep = self.split(keep, received)
            self.send(away, self.stage)
            return
        back = 2 * bits - 1 - self.stage
        if self.stage == bits:
            self.keep = self.total(self.keep, received)
        else:
            self.keep = self.joined(back == 0, self.keep, received)
        if back:
            self.send(self.keep, back)
        else:
            self.keep = self.keep[0]
            self.flying = [swap(self.keep, self.masks[0], self.n)]

    def finish(self):
        return self.keep, self.flying[0]


def query_key_kernel(owners_ref, *refs):
    blocks, refs = refs[:-7], refs[-7:]
    gain_ref, wq_ref, wk_ref, n1_ref, q_ref, k_ref, sums_ref = refs
    rows, cols = blocks[0].shape
    full = len(blocks) * cols
    fields = [block[...].astype(F32) for block in blocks]
    squares = fields[0] * fields[0]
    for field in fields[1:]:
        squares = squares + field * field
    scale = lax.rsqrt(jnp.sum(squares, axis=1, keepdims=True) / full + EPSILON)
    for k, field in enumerate(fields):
        at = owners_ref[k]
        gain = gain_ref[at, 0:1, :].astype(F32)
        first = pl.multiple_of(at * cols, 128)
        normed = (field * scale * gain).astype(BF)
        n1_ref[:, pl.ds(first, cols)] = normed
        terms = [dot(normed, ref[pl.ds(first, cols), :]) for ref in (wq_ref, wk_ref)]
        total = terms if k == 0 else [a + b for a, b in zip(total, terms, strict=True)]
    query, key = total
    q_ref[...] = query
    k_ref[...] = key
    which = lax.broadcasted_iota(jnp.int32, (8, rows), 0)
    sums_ref[...] = jnp.where(
        which == 0,
        row_sums(query * query),
        jnp.where(which == 1, row_sums(key * key), row_sums(squares)),
    )


def query_key_call(owners, blocks, gains, wq, wk):
    length, cols = blocks[0].shape
    full = cols * len(blocks)
    out = wq.shape[1]
    rows = min(256, length)
    whole = pl.BlockSpec((full, out), lambda g, o: (0, 0))
    tile = pl.BlockSpec((rows, out), lambda g, o: (g, 0))
    return launch(
        query_key_kernel,
        [owners, *blocks, gains, wq, wk],
        prefetch=1,
        grid=(length // rows,),
        in_specs=[pl.BlockSpec((rows, cols), lambda g, o: (g, 0))] * len(blocks)
        + [pl.BlockSpec((len(blocks), 16, cols), lambda g, o: (0, 0, 0)), whole, whole],
        out_specs=[
            pl.BlockSpec((rows, full), lambda g, o: (g, 0)),
            tile,
            tile,
            pl.BlockSpec((8, rows), lambda g, o: (0, g)),
        ],
        out_shape=[
            jax.ShapeDtypeStruct((length, full), BF),
            jax.ShapeDtypeStruct((length, out), F32),
            jax.ShapeDtypeStruct((length, out), F32),
            jax.ShapeDtypeStruct((8, length), F32),
        ],
    )


def value_kernel(n1_ref, wv_ref, v_ref):
    v_ref[...] = dot(n1_ref[...], wv_ref[...]).astype(BF)


def value_call(normed, wv):
    length, full = normed.shape
    out = wv.shape[1]
    rows = min(256, length)
    return launch(
        value_kernel,
        [normed, wv],
        grid=(length // rows,),
        in_specs=[
            pl.BlockSpec((rows, full), lambda g: (g, 0)),
            pl.BlockSpec((full, out), lambda g: (0, 0)),
        ],
        out_specs=pl.BlockSpec((rows, out), lambda g: (g, 0)),
        out_shape=jax.ShapeDtypeStruct((length, out), BF),
    )


def head_scales(sums_refs, full):
    total = sums_refs[0][...]
    for ref in sums_refs[1:]:
        total = total + ref[...]
    return jnp.transpose(lax.rsqrt(total / full + EPSILON))


def masked_scores(query, key, first, prefix):
    scores = dot_t(query, key) * (HEAD_DIM**-0.5)
    row = first + lax.broadcasted_iota(jnp.int32, scores.shape, 0)
    col = lax.broadcasted_iota(jnp.int32, scores.shape, 1)
    return jnp.where((col <= row) | (col < prefix), scores, MASKED)


def attn_forward_kernel(full, size, prefix_ref, q_ref, k_ref, v_ref, gq_ref, gk_ref, cos_ref, sin_ref, *rest):
    sums_refs, (att_ref, lse_ref, qr_ref, kr_ref) = rest[:size], rest[size:]
    length = q_ref.shape[0]
    rows = min(256, length)
    scales = head_scales(sums_refs, full)
    cosine, sine = cos_ref[...], sin_ref[...]
    for pre_ref, gain_ref, out_ref, at in ((q_ref, gq_ref, qr_ref, 0), (k_ref, gk_ref, kr_ref, 1)):
        field = pre_ref[...] * scales[:, at : at + 1] * gain_ref[...].astype(F32)
        out_ref[...] = (field * cosine + pltpu.roll(field, HEAD_DIM // 2, 1) * sine).astype(BF)
    prefix = prefix_ref[0]
    for first in range(0, length, rows):
        last = min(length, max(PREFIX_MAX, first + rows))
        scores = masked_scores(qr_ref[first : first + rows, :], kr_ref[:last, :], first, prefix)
        highest = jnp.max(scores, axis=1, keepdims=True)
        exponent = jnp.exp(scores - highest)
        total = jnp.sum(exponent, axis=1, keepdims=True)
        mixed = dot(exponent.astype(BF), v_ref[:last, :])
        att_ref[first : first + rows, :] = (mixed / total).astype(BF)
        lse_ref[first : first + rows, :] = jnp.broadcast_to(
            highest + jnp.log(total), (rows, HEAD_DIM)
        )


def attn_forward(prefix, q_pre, k_pre, v_rows, gq, gk, cosine, sine, sums):
    length, width = q_pre.shape
    full = width * len(sums)
    head = pl.BlockSpec((length, HEAD_DIM), lambda h, *_: (0, h))
    gain = pl.BlockSpec((1, HEAD_DIM), lambda h, *_: (0, h))
    table = pl.BlockSpec((length, HEAD_DIM), lambda h, *_: (0, 0))
    sums_spec = pl.BlockSpec((8, length), lambda h, *_: (0, 0))
    return launch(
        functools.partial(attn_forward_kernel, full, len(sums)),
        [prefix, q_pre, k_pre, v_rows, gq, gk, cosine, sine, *sums],
        prefetch=1,
            grid=(width // HEAD_DIM,),
            in_specs=[head, head, head, gain, gain, table, table] + [sums_spec] * len(sums),
            out_specs=[head] * 4,
        out_shape=[
            jax.ShapeDtypeStruct((length, width), BF),
            jax.ShapeDtypeStruct((length, width), F32),
            jax.ShapeDtypeStruct((length, width), BF),
            jax.ShapeDtypeStruct((length, width), BF),
        ],
    )


def attn_backward_kernel(
    full, size, prefix_ref, q_ref, k_ref, qr_ref, kr_ref, v_ref, do_ref, lse_ref, gq_ref, gk_ref,
    cos_ref, sin_ref, *rest,
):
    sums_refs, rest = rest[:size], rest[size:]
    dq_ref, dk_ref, dv_ref, gains_ref, rows_ref, kacc, vacc = rest
    head = pl.program_id(0)
    length = q_ref.shape[0]
    rows = min(512, length)
    prefix = prefix_ref[0]
    factor = HEAD_DIM**-0.5
    kacc[...] = jnp.zeros_like(kacc)
    vacc[...] = jnp.zeros_like(vacc)
    contract = (((0,), (0,)), ((), ()))
    for first in range(0, length, rows):
        last = min(length, max(PREFIX_MAX, first + rows))
        here = slice(first, first + rows)
        scores = masked_scores(qr_ref[here, :], kr_ref[:last, :], first, prefix)
        weights = jnp.exp(scores - lse_ref[here, 0:1])
        grad_rows = do_ref[here, :]
        weight_grad = dot_t(grad_rows, v_ref[:last, :])
        centred = jnp.sum(weight_grad * weights, axis=1, keepdims=True)
        score_grad = (weights * (weight_grad - centred)).astype(BF)
        dq_ref[here, :] = dot(score_grad, kr_ref[:last, :]) * factor
        kacc[:last, :] += lax.dot_general(
            score_grad, qr_ref[here, :], contract, preferred_element_type=F32
        )
        vacc[:last, :] += lax.dot_general(
            weights.astype(BF), grad_rows, contract, preferred_element_type=F32
        )
    dv_ref[...] = vacc[...].astype(BF)
    scales = head_scales(sums_refs, full)
    cosine, sine = cos_ref[...], sin_ref[...]
    which = lax.broadcasted_iota(jnp.int32, (8, length), 0)
    lanes = lax.broadcasted_iota(jnp.int32, (8, HEAD_DIM), 0)
    row_terms = jnp.zeros((8, length), F32)
    gain_terms = jnp.zeros((8, HEAD_DIM), F32)
    for at, (pre_ref, gain_ref, out_ref, raw) in enumerate(
        ((q_ref, gq_ref, dq_ref, dq_ref[...]), (k_ref, gk_ref, dk_ref, kacc[...] * factor))
    ):
        raw = raw.astype(BF).astype(F32)
        normed_grad = raw * cosine - pltpu.roll(raw, HEAD_DIM // 2, 1) * sine
        out_ref[...] = normed_grad
        product = normed_grad * pre_ref[...]
        row_terms = jnp.where(
            which == at, row_sums(product * gain_ref[...].astype(F32)), row_terms
        )
        gain_terms = jnp.where(
            lanes == at,
            jnp.sum(product * scales[:, at : at + 1], axis=0, keepdims=True),
            gain_terms,
        )
    gains_ref[...] = gain_terms
    product = dv_ref[...].astype(F32) * v_ref[...].astype(F32)
    row_terms = jnp.where(which == 2, row_sums(product), row_terms)

    @pl.when(head == 0)
    def _():
        rows_ref[...] = row_terms

    @pl.when(head > 0)
    def _():
        rows_ref[...] += row_terms


def attn_backward(
    prefix, q_pre, k_pre, q_rot, k_rot, v_rows, out_grad, lse, gq, gk, cosine, sine, sums, others=()
):
    length, width = q_pre.shape
    full = width * len(sums)
    head = pl.BlockSpec((length, HEAD_DIM), lambda h, *_: (0, h))
    gain = pl.BlockSpec((1, HEAD_DIM), lambda h, *_: (0, h))
    table = pl.BlockSpec((length, HEAD_DIM), lambda h, *_: (0, 0))
    sums_spec = pl.BlockSpec((8, length), lambda h, *_: (0, 0))
    return launch(
        functools.partial(attn_backward_kernel, full, len(sums)),
        [prefix, q_pre, k_pre, q_rot, k_rot, v_rows, out_grad, lse, gq, gk, cosine, sine, *sums],
        prefetch=1,
            grid=(width // HEAD_DIM,),
            in_specs=[head] * 7 + [gain, gain, table, table] + [sums_spec] * len(sums),
            out_specs=[head, head, head, pl.BlockSpec((8, HEAD_DIM), lambda h, *_: (0, h)), sums_spec],
            scratch=[pltpu.VMEM((length, HEAD_DIM), F32)] * 2,
        out_shape=[
            jax.ShapeDtypeStruct((length, width), F32),
            jax.ShapeDtypeStruct((length, width), F32),
            jax.ShapeDtypeStruct((length, width), BF),
            jax.ShapeDtypeStruct((8, width), F32),
            jax.ShapeDtypeStruct((8, length), F32),
        ],
        others=others,
    )


def norm_back_kernel(full, size, q_ref, k_ref, dq_ref, dk_ref, dv_ref, gq_ref, gk_ref, *rest):
    sums_refs, back_refs, (out_ref, stat_ref) = rest[:size], rest[size : 2 * size], rest[2 * size :]
    width = q_ref.shape[1]
    scales = head_scales(sums_refs, full)
    back = back_refs[0][...]
    squares = sums_refs[0][...]
    for ref, sums_ref in zip(back_refs[1:], sums_refs[1:], strict=True):
        back = back + ref[...]
        squares = squares + sums_ref[...]
    scale = lax.rsqrt(squares / full + EPSILON)
    along = scale * back - scale * scale * scale * (back / full) * squares
    stat_ref[...] = jnp.broadcast_to(along[0:1] + along[1:2] + back[2:3], stat_ref.shape)
    back = jnp.transpose(back)
    grads = []
    for at, (pre_ref, grad_ref, gain_ref) in enumerate(
        ((q_ref, dq_ref, gq_ref), (k_ref, dk_ref, gk_ref))
    ):
        scale = scales[:, at : at + 1]
        pre = pre_ref[...]
        grad = (
            scale * gain_ref[...].astype(F32) * grad_ref[...]
            - pre * (scale * scale * scale * back[:, at : at + 1] / full)
        ).astype(BF)
        grads.append(grad)
    out_ref[:, :width] = grads[0]
    out_ref[:, width : 2 * width] = grads[1]
    out_ref[:, 2 * width :] = dv_ref[...]


def norm_back(q_pre, k_pre, dq, dk, dv, gq, gk, sums, back):
    length, width = q_pre.shape
    full = width * len(sums)
    rows = min(256, length)
    tile = pl.BlockSpec((rows, width), lambda g: (g, 0))
    wide = pl.BlockSpec((rows, 3 * width), lambda g: (g, 0))
    gain = pl.BlockSpec((1, width), lambda g: (0, 0))
    line = pl.BlockSpec((8, rows), lambda g: (0, g))
    return launch(
        functools.partial(norm_back_kernel, full, len(sums)),
        [q_pre, k_pre, dq, dk, dv, gq, gk, *sums, *back],
        grid=(length // rows,),
        in_specs=[tile] * 5 + [gain, gain] + [line] * (2 * len(sums)),
        out_specs=[wide, line],
        out_shape=[
            jax.ShapeDtypeStruct((length, 3 * width), BF),
            jax.ShapeDtypeStruct((8, length), F32),
        ],

    )


def expert_kernel(step, aliased, chunk_ref, n2_ref, cot_ref, router_ref, keep_ref, wg_ref, wu_ref, wd_ref, *rest):
    rest = list(rest)
    own = step == 0
    res_ref = rest.pop(0) if own else None
    rest = rest[aliased:]
    h2t_ref, dg_ref, du_ref, n2t_ref, mix_ref, dn2_ref, probs_ref, mix, dn2, gates, gate_grads = rest
    expert = pl.program_id(0)
    blocks, rows, cols = cot_ref.shape
    lane = lax.broadcasted_iota(jnp.int32, (rows, 128), 1)

    @pl.when(expert == 0)
    def _():
        logits = jnp.where(lane < EXPERTS, dot(n2_ref[...], router_ref[...]), MASKED)
        exponent = jnp.exp(logits - jnp.max(logits, axis=1, keepdims=True))
        probs = exponent / jnp.sum(exponent, axis=1, keepdims=True)
        probs_ref[...] = probs
        gates[...] = probs * keep_ref[...]
        gate_grads[...] = jnp.zeros_like(gate_grads)
        n2t_ref[...] = jnp.transpose(n2_ref[...])
        dn2[...] = jnp.zeros_like(dn2)
        if own:
            mix[...] = res_ref[...]
        else:
            mix[...] = jnp.zeros_like(mix)

    normed = n2_ref[...]
    w_down = wd_ref[0]
    pre_gate = dot(normed, wg_ref[0])
    pre_up = dot(normed, wu_ref[0])
    back = dot_t(cot_ref[0], w_down[:, :cols])
    for t in range(1, blocks):
        back = back + dot_t(cot_ref[t], w_down[:, t * cols : (t + 1) * cols])
    here = lane == expert
    gate = jnp.sum(jnp.where(here, gates[...], 0.0), axis=1, keepdims=True)
    sigmoid = jax.nn.sigmoid(pre_gate)
    activated = pre_gate * sigmoid
    hidden = (activated * pre_up).astype(BF).astype(F32)
    gate_grad = jnp.sum(back * hidden, axis=1, keepdims=True)
    gate_grads[...] += jnp.where(here, gate_grad * keep_ref[...], 0.0)
    back = back * gate
    h2 = (hidden * gate).astype(BF)
    dg = (back * pre_up * sigmoid * (1.0 + pre_gate * (1.0 - sigmoid))).astype(BF)
    du = (back * activated).astype(BF)
    h2t_ref[...] = jnp.transpose(h2)
    dg_ref[...] = dg
    du_ref[...] = du
    mix[...] += dot(h2, w_down)
    dn2[...] += dot_t(dg, wg_ref[0]) + dot_t(du, wu_ref[0])

    @pl.when(expert == EXPERTS - 1)
    def _():
        dn2_ref[:, : blocks * cols] = dn2[...].astype(BF)
        high = gate_grads[...].astype(BF).astype(F32)
        low = gate_grads[...] - high
        if step:
            high = pltpu.roll(high, GROUP * 2 * step, 1)
        low = pltpu.roll(low, GROUP * (2 * step + 1), 1)
        dn2_ref[:, blocks * cols :] = (high + low).astype(BF)
        for t in range(blocks):
            mix_ref[t] = mix[:, t * cols : (t + 1) * cols].astype(BF)


def expert_call(step, chunk, n2, cot, router, keep, wg, wu, wd, residual, carried):
    rows, full = n2.shape
    blocks, length, cols = cot.shape
    hidden = wg.shape[2]
    own = step == 0
    in_specs = [
        pl.BlockSpec((rows, full), lambda e, c: (0, 0)),
        pl.BlockSpec((blocks, rows, cols), lambda e, c: (0, c[0], 0)),
        pl.BlockSpec((full, 128), lambda e, c: (0, 0)),
        pl.BlockSpec((rows, 128), lambda e, c: (c[0], 0)),
        pl.BlockSpec((1, full, hidden), lambda e, c: (e, 0, 0)),
        pl.BlockSpec((1, full, hidden), lambda e, c: (e, 0, 0)),
        pl.BlockSpec((1, hidden, full), lambda e, c: (e, 0, 0)),
    ]
    operands = [chunk, n2, cot, router, keep, wg, wu, wd]
    if own:
        in_specs.append(pl.BlockSpec((rows, full), lambda e, c: (0, 0)))
        operands.append(residual)
    aliases = {len(operands) + k: k for k in range(len(carried))}
    in_specs += [pl.BlockSpec(memory_space=pl.ANY)] * len(carried)
    operands += list(carried)
    slab = pl.BlockSpec((rows, hidden), lambda e, c: (c[0], e))
    return launch(
        functools.partial(expert_kernel, step, len(carried)),
        [*operands],
        prefetch=1,
            grid=(EXPERTS,),
            in_specs=in_specs,
            out_specs=[
                pl.BlockSpec((hidden, rows), lambda e, c: (e, c[0])),
                slab,
                slab,
                pl.BlockSpec((full, rows), lambda e, c: (0, c[0])),
                pl.BlockSpec((blocks, rows, cols), lambda e, c: (0, c[0], 0)),
                pl.BlockSpec((rows, full + 128), lambda e, c: (0, 0)),
                pl.BlockSpec((rows, 128), lambda e, c: (0, 0)),
            ],
            scratch=[
                pltpu.VMEM((rows, full), F32),
                pltpu.VMEM((rows, full), F32),
                pltpu.VMEM((rows, 128), F32),
                pltpu.VMEM((rows, 128), F32),
            ],
        out_shape=[
            jax.ShapeDtypeStruct((EXPERTS * hidden, length), BF),
            jax.ShapeDtypeStruct((length, EXPERTS * hidden), BF),
            jax.ShapeDtypeStruct((length, EXPERTS * hidden), BF),
            jax.ShapeDtypeStruct((full, length), BF),
            jax.ShapeDtypeStruct((blocks, length, cols), BF),
            jax.ShapeDtypeStruct((rows, full + 128), BF),
            jax.ShapeDtypeStruct((rows, 128), F32),
        ],
        aliases=aliases,

        token=6,
    )


def arrange_kernel(owners_ref, *refs):
    blocks, (branch_ref, rows_ref, out_ref) = refs[:-3], refs[-3:]
    for k, ref in enumerate(blocks):
        rows_ref[owners_ref[k]] = ref[...]
    out_ref[...] = branch_ref[...]


def arrange(owners, blocks, branch):
    rows, width = blocks[0].shape
    full = branch.shape[1]
    chunk = rows // 2
    return launch(
        arrange_kernel,
        [owners, *blocks, branch],
        prefetch=1,
        grid=(2,),
        in_specs=[pl.BlockSpec((chunk, width), lambda g, o: (g, 0))] * len(blocks)
        + [pl.BlockSpec((chunk, full), lambda g, o: (g, 0))],
        out_specs=[
            pl.BlockSpec((len(blocks), chunk, width), lambda g, o: (0, g, 0)),
            pl.BlockSpec((chunk, full), lambda g, o: (g, 0)),
        ],
        out_shape=[
            jax.ShapeDtypeStruct((len(blocks), rows, width), BF),
            jax.ShapeDtypeStruct((rows, full), BF),
        ],
    )


def gate_up_kernel(n2t_ref, dg_ref, du_ref, out_ref):
    turned = n2t_ref[...]
    out_ref[0, 0] = dot(turned, dg_ref[...]).astype(BF)
    out_ref[1, 0] = dot(turned, du_ref[...]).astype(BF)


def gate_up_grads(n2t, dg, du):
    full, length = n2t.shape
    hidden = dg.shape[1] // EXPERTS
    slab = pl.BlockSpec((length, hidden), lambda e: (0, e))
    return launch(
        gate_up_kernel,
        [n2t, dg, du],
        grid=(EXPERTS,),
        in_specs=[pl.BlockSpec((full, length), lambda e: (0, 0)), slab, slab],
        out_specs=pl.BlockSpec((2, 1, full, hidden), lambda e: (0, e, 0, 0)),
        out_shape=jax.ShapeDtypeStruct((2, EXPERTS, full, hidden), BF),
    )


def down_kernel(table_ref, h2t_ref, cot_ref, out_ref):
    cols = cot_ref.shape[2]
    for t in range(cot_ref.shape[0]):
        out_ref[0, :, t * cols : (t + 1) * cols] = dot(h2t_ref[...], cot_ref[t]).astype(BF)


def down_grads(table, h2t, cot, n):
    wide, length = h2t.shape
    blocks, _, cols = cot.shape
    rows = wide // n
    steps = n // 2
    return launch(
        down_kernel,
        [table, h2t, cot],
        prefetch=1,
        grid=(steps,),
        in_specs=[
            pl.BlockSpec((rows, length), lambda g, t: (t[g], 0)),
            pl.BlockSpec((blocks, length, cols), lambda g, t: (0, 0, 0)),
        ],
        out_specs=pl.BlockSpec((1, rows, blocks * cols), lambda g, t: (g, 0, 0)),
        out_shape=jax.ShapeDtypeStruct((steps, rows, blocks * cols), BF),
    )


def middle_kernel(size, owners_ref, *refs):
    heads, x_refs = refs[:size], refs[size : 2 * size]
    wo_ref, gain_ref, res_ref, n2_ref = refs[2 * size :]
    step = pl.program_id(0)
    cols = x_refs[0].shape[1]
    width = heads[0].shape[1]

    @pl.when(step == 0)
    def _():
        for k, ref in enumerate(x_refs):
            first = pl.multiple_of(owners_ref[k] * cols, 128)
            res_ref[:, pl.ds(first, cols)] = ref[...].astype(F32)

    weights = wo_ref[...].reshape(width, -1)
    for k, ref in enumerate(heads):

        @pl.when(step == k)
        def _(ref=ref):
            res_ref[...] += dot(ref[...], weights)

    @pl.when(step == size - 1)
    def _():
        residual = res_ref[...]
        scale = lax.rsqrt(jnp.mean(residual * residual, axis=1, keepdims=True) + EPSILON)
        for t in range(size):
            here = slice(t * cols, (t + 1) * cols)
            gain = gain_ref[t, 1:2, :].astype(F32)
            n2_ref[:, here] = (residual[:, here] * scale * gain).astype(BF)


def middle(owners, attended, received, w_out, x_blocks, gains):
    size = len(x_blocks)
    groups, _, part, full = w_out.shape
    width, cols = groups * part, full // size
    rows = attended.shape[0] // size
    return launch(
        functools.partial(middle_kernel, size),
        [owners, attended, *received, *x_blocks, w_out, gains],
        prefetch=1,
        grid=(size,),
        in_specs=[pl.BlockSpec((rows, width), lambda t, o: (o[0], 0))]
        + [pl.BlockSpec((rows, width), lambda t, o: (0, 0))] * (size - 1)
        + [pl.BlockSpec((rows, cols), lambda t, o: (o[0], 0))] * size
        + [
            pl.BlockSpec((groups, 1, part, full), lambda t, o: (0, o[t], 0, 0)),
            pl.BlockSpec((size, 16, cols), lambda t, o: (0, 0, 0)),
        ],
        out_specs=[pl.BlockSpec((rows, full), lambda t, o: (0, 0))] * 2,
        out_shape=[
            jax.ShapeDtypeStruct((rows, full), F32),
            jax.ShapeDtypeStruct((rows, full), BF),
        ],
    )


def middle_back_kernel(
    mine_ref, own_ref, received_ref, probs_ref, router_ref, res_ref, n2_ref, cot_ref, gain_ref, wo_ref,
    branch_ref, parts_ref, *out_refs,
):
    step = pl.program_id(0)
    blocks, rows, cols = cot_ref.shape
    full = blocks * cols

    @pl.when(step == 0)
    def _():
        probs = probs_ref[...]
        parts = own_ref[:, full:].astype(F32) + received_ref[:, full:].astype(F32)
        prob_grad = parts
        for group in range(1, 2 * blocks):
            prob_grad = prob_grad + pltpu.roll(parts, 128 - GROUP * group, 1)
        lane = lax.broadcasted_iota(jnp.int32, (rows, 128), 1)
        prob_grad = jnp.where(lane < EXPERTS, prob_grad, 0.0)
        centred = jnp.sum(prob_grad * probs, axis=1, keepdims=True)
        logit_grad = (probs * (prob_grad - centred)).astype(BF)
        grad = (
            own_ref[:, :full].astype(F32)
            + received_ref[:, :full].astype(F32)
            + dot_t(logit_grad, router_ref[...])
        )
        residual = res_ref[...]
        scale = lax.rsqrt(jnp.mean(residual * residual, axis=1, keepdims=True) + EPSILON)
        stat = jnp.zeros((rows, 1), F32)
        for t in range(blocks):
            here = slice(t * cols, (t + 1) * cols)
            gain = gain_ref[t, 1:2, :].astype(F32)
            stat = stat + jnp.sum(residual[:, here] * gain * grad[:, here], axis=1, keepdims=True)
        stat = scale * scale * scale * stat / full
        for t in range(blocks):
            here = slice(t * cols, (t + 1) * cols)
            gain = gain_ref[t, 1:2, :].astype(F32)
            branch_ref[:, here] = (
                cot_ref[t].astype(F32) + scale * gain * grad[:, here] - residual[:, here] * stat
            ).astype(BF)
        router_part = lax.dot_general(
            logit_grad, n2_ref[...], (((0,), (0,)), ((), ())), preferred_element_type=F32
        )[:8]
        norm_part = jnp.sum(grad * residual * scale, axis=0, keepdims=True)
        which = lax.broadcasted_iota(jnp.int32, (8, full), 0)
        parts_ref[...] = jnp.where(which == EXPERTS, norm_part, router_part)

    product = dot_t(branch_ref[...], wo_ref[...].reshape(-1, full)).astype(BF)
    for k, ref in enumerate(out_refs):

        @pl.when(step == k)
        def _(ref=ref):
            ref[...] = product


def middle_back(mine, own, received, probs, router, residual, n2, cot, gains, w_out):
    blocks, _, cols = cot.shape
    rows, full = residual.shape
    groups, _, part, _ = w_out.shape
    width = groups * part
    whole = pl.BlockSpec((rows, full), lambda t, m: (0, 0))
    wide = pl.BlockSpec((rows, full + 128), lambda t, m: (0, 0))
    lanes = pl.BlockSpec((rows, 128), lambda t, m: (0, 0))
    return launch(
        middle_back_kernel,
        [mine, own, received, probs, router, residual, n2, cot, gains, w_out],
        prefetch=1,
            grid=(blocks,),
            in_specs=[
                wide,
                wide,
                lanes,
                pl.BlockSpec((full, 128), lambda t, m: (0, 0)),
                whole,
                whole,
                pl.BlockSpec((blocks, rows, cols), lambda t, m: (0, m[0], 0)),
                pl.BlockSpec((blocks, 16, cols), lambda t, m: (0, 0, 0)),
                pl.BlockSpec((groups, 1, part, full), lambda t, m: (0, lax.rem(m[0] + t, blocks), 0, 0)),
            ],
            out_specs=[
                whole,
                pl.BlockSpec((8, full), lambda t, m: (0, 0)),
            ]
            + [pl.BlockSpec((rows, width), lambda t, m: (0, 0))] * blocks,
        out_shape=[
            jax.ShapeDtypeStruct((rows, full), BF),
            jax.ShapeDtypeStruct((8, full), F32),
        ]
        + [jax.ShapeDtypeStruct((rows, width), BF)] * blocks,
    )


def reversed_bits(at, bits):
    return sum(((at >> b) & 1) << (bits - 1 - b) for b in range(bits)) if bits else at


def column_grad_kernel(left_ref, right_ref, w_ref, out_ref, gain_ref):
    product = dot(jnp.transpose(left_ref[...]), right_ref[...])
    out_ref[...] = product.astype(BF)
    gain_ref[...] = jnp.broadcast_to(row_sums(product * w_ref[...].astype(F32)), gain_ref.shape)


def column_grads(left, right, weights):
    length, full = left.shape
    width = right.shape[1]
    piece = min(512, full)
    tile = pl.BlockSpec((piece, width), lambda g: (g, 0))
    return launch(
        column_grad_kernel,
        [left, right, weights],
        grid=(full // piece,),
        in_specs=[
            pl.BlockSpec((length, piece), lambda g: (0, g)),
            pl.BlockSpec((length, width), lambda g: (0, 0)),
            tile,
        ],
        out_specs=[tile, pl.BlockSpec((8, piece), lambda g: (0, g))],
        out_shape=[
            jax.ShapeDtypeStruct((full, width), BF),
            jax.ShapeDtypeStruct((8, full), F32),
        ],
    )


def row_grad_kernel(rows_ref, left_ref, *rest):
    blocks, (out_ref, turned_left) = rest[:-2], rest[-2:]
    rows = blocks[0].shape[0]

    @pl.when(pl.program_id(0) == 0)
    def _():
        for k in range(len(blocks)):
            first = pl.multiple_of(rows_ref[k] * rows, rows)
            turned_left[:, k * rows : (k + 1) * rows] = jnp.transpose(
                left_ref[pl.ds(first, rows), :]
            )

    total = None
    for k, block in enumerate(blocks):
        term = dot(turned_left[:, k * rows : (k + 1) * rows], block[...])
        total = term if total is None else total + term
    out_ref[...] = total.astype(BF)


def row_grads(owners, left, blocks):
    length, width = left.shape
    rows, full = blocks[0].shape
    piece = min(512, full)
    return launch(
        row_grad_kernel,
        [owners, left, *blocks],
        prefetch=1,
        grid=(full // piece,),
        in_specs=[pl.BlockSpec((length, width), lambda g, o: (0, 0))]
        + [pl.BlockSpec((rows, piece), lambda g, o: (0, g))] * len(blocks),
        out_specs=pl.BlockSpec((width, piece), lambda g, o: (0, g)),
        out_shape=jax.ShapeDtypeStruct((width, full), BF),
        scratch=[pltpu.VMEM((width, length), BF)],
    )


def input_kernel(owner_ref, grad_ref, w_ref, *rest):
    total = dot_t(grad_ref[...], w_ref[...])
    if len(rest) == 2:
        total = total + rest[0][...].astype(F32)
    rest[-1][...] = total.astype(BF)


def input_grads(owner, cols, grad, w_all, received=None, work=1):
    length, width = grad.shape
    rows = min(256, length)
    tile = pl.BlockSpec((rows, cols), lambda g, o: (g, 0))
    return launch(
        input_kernel,
        [owner, grad, w_all, *([] if received is None else [received])],
        prefetch=1,
            grid=(length // rows,),
            in_specs=[
                pl.BlockSpec((rows, width), lambda g, o: (g, 0)),
                pl.BlockSpec((cols, width), lambda g, o: (o[0], 0)),
            ]
            + ([] if received is None else [tile]),
            out_specs=tile,
        out_shape=jax.ShapeDtypeStruct((length, cols), BF),

        work=work,
    )


def mix_kernel(owner_ref, mix_ref, *rest):
    if len(rest) == 1:
        rest[0][...] = mix_ref[0]
    else:
        rest[1][...] = added(mix_ref[0], rest[0][...])


def mix_block(owner, mix, received=None, work=1):
    blocks, length, cols = mix.shape
    chunk = length // 2
    tile = pl.BlockSpec((chunk, cols), lambda g, o: (g, 0))
    return launch(
        mix_kernel,
        [owner, mix, *([] if received is None else [received])],
        prefetch=1,
            grid=(2,),
            in_specs=[pl.BlockSpec((1, chunk, cols), lambda g, o: (o[0], g, 0))]
            + ([] if received is None else [tile]),
            out_specs=tile,
        out_shape=jax.ShapeDtypeStruct((length, cols), BF),
        work=work,
    )


def final_kernel(
    full, owners_ref, grad_ref, w_ref, received_ref, tokens_ref, sums_ref, stat_ref, gain_ref, *rest
):
    blocks, out_ref = rest[:-1], rest[-1]
    step = pl.program_id(0)
    branch = blocks[0][...]
    for k in range(1, len(blocks)):
        branch = jnp.where(step == k, blocks[k][...], branch)
    scale = lax.rsqrt(sums_ref[...] / full + EPSILON)
    scale_one = jnp.transpose(scale)[:, 2:3]
    stat = jnp.transpose(stat_ref[...])[:, 0:1] / full * scale_one * scale_one
    normed_grad = dot_t(grad_ref[...], w_ref[...]) + received_ref[...].astype(F32)
    out_ref[...] = (
        branch.astype(F32)
        + scale_one * gain_ref[...].astype(F32) * normed_grad
        - tokens_ref[...].astype(F32) * stat
    )


def final_grads(owners, grad, w_all, received, tokens, sums, stat, gain, blocks):
    length, cols = tokens.shape
    width = grad.shape[1]
    rows = length // len(blocks)
    tile = pl.BlockSpec((rows, cols), lambda k, o: (o[k], 0))
    line = pl.BlockSpec((8, rows), lambda k, o: (0, o[k]))
    return launch(
        functools.partial(final_kernel, cols * len(blocks)),
        [owners, grad, w_all, received, tokens, sums, stat, gain, *blocks],
        prefetch=1,
            grid=(len(blocks),),
            in_specs=[
                pl.BlockSpec((rows, width), lambda k, o: (o[k], 0)),
                pl.BlockSpec((cols, width), lambda k, o: (o[0], 0)),
                tile,
                tile,
                line,
                line,
                pl.BlockSpec((1, cols), lambda k, o: (0, 0)),
            ]
            + [pl.BlockSpec((rows, cols), lambda k, o: (0, o[0]))] * len(blocks),
            out_specs=tile,
        out_shape=jax.ShapeDtypeStruct((length, cols), F32),
    )


def piece_specs(shape, steps):
    block = (1,) + shape
    return [
        pl.BlockSpec(block, lambda a, pos: (jnp.minimum(pos[a], steps - 1), 0, 0)),
        pl.BlockSpec(block, lambda a, pos: (jnp.maximum(pos[a] - steps, 0), 0, 0)),
    ]


def pieces_kernel(steps, pos_ref, low_ref, high_ref, out_ref):
    low = pos_ref[pl.program_id(0)] < steps
    out_ref[...] = jnp.where(low, low_ref[0].astype(F32), high_ref[0].astype(F32))


def widen_pieces(pos, halves, n):
    steps, rows, width = halves[0].shape
    return launch(
        functools.partial(pieces_kernel, steps),
        [pos, *halves],
        prefetch=1,
        grid=(n,),
        in_specs=piece_specs((rows, width), steps),
        out_specs=pl.BlockSpec((rows, width), lambda a, pos: (a, 0)),
        out_shape=jax.ShapeDtypeStruct((rows * n, width), F32),
    )


def projections_kernel(sum_ref, q_ref, k_ref, v_ref):
    width = q_ref.shape[1]
    for at, out_ref in enumerate((q_ref, k_ref, v_ref)):
        out_ref[...] = sum_ref[:, at * width : (at + 1) * width].astype(F32)


def widen_projections(total):
    full, width = total.shape
    out = width // 3
    piece = min(256, full)
    tile = pl.BlockSpec((piece, out), lambda g: (g, 0))
    return launch(
        projections_kernel,
        [total],
        grid=(full // piece,),
        in_specs=[pl.BlockSpec((piece, width), lambda g: (g, 0))],
        out_specs=[tile] * 3,
        out_shape=[jax.ShapeDtypeStruct((full, out), F32)] * 3,
    )


def experts_kernel(held_ref, gate_ref, up_ref):
    gate_ref[0] = held_ref[0, 0].astype(F32)
    up_ref[0] = held_ref[1, 0].astype(F32)


def widen_experts(held):
    _, experts, full, hidden = held.shape
    tall = pl.BlockSpec((1, full, hidden), lambda e: (e, 0, 0))
    return launch(
        experts_kernel,
        [held],
        grid=(experts,),
        in_specs=[pl.BlockSpec((2, 1, full, hidden), lambda e: (0, e, 0, 0))],
        out_specs=[tall, tall],
        out_shape=[jax.ShapeDtypeStruct((experts, full, hidden), F32)] * 2,
    )


def kept_experts(routes, order):
    length = routes.shape[0]
    token, which = order // TOP, order % TOP
    onehot = (token[:, None] == jnp.arange(length, dtype=jnp.int32)[None, :]).astype(BF)
    named = (routes[:, :, None] == jnp.arange(8, dtype=jnp.int32)).astype(BF).reshape(length, TOP * 8)
    ordered = dot(onehot, named).reshape(-1, TOP, 8)
    choose = jnp.sum(
        jnp.where(which[:, None, None] == jnp.arange(TOP)[None, :, None], ordered, 0.0), axis=1
    )
    kept = jnp.where(jnp.cumsum(choose, axis=0) <= CAP, choose, 0.0).astype(BF)
    kept = jnp.pad(kept, ((0, 0), (0, 120)))
    return lax.dot_general(onehot, kept, (((0,), (0,)), ((), ())), preferred_element_type=F32)


def on_device(
    tokens, cotangent, norm1_gain, w_query, w_key, w_value, query_gain, key_gain, w_output,
    norm2_gain, router, w_gate, w_up, w_down, routes, prefix, slot_order,
):
    size, n = lax.axis_size("tensor"), lax.axis_size("dp")
    mine, group = lax.axis_index("tensor"), lax.axis_index("dp")
    length, cols = tokens.shape
    full = cols * size
    rows = length // size
    steps = range(1, size)
    Chain.token = None

    def add(*terms):
        return functools.reduce(jnp.add, terms)

    here = mine.astype(jnp.int32)[None]

    rel = rel_table(swap_masks(n))
    table = jnp.asarray(rel, jnp.int32) ^ group
    positions = jnp.asarray([rel.index(v) for v in range(n)], jnp.int32)[
        jnp.arange(n, dtype=jnp.int32) ^ group
    ]
    half = n // 2
    owners = ((mine - jnp.arange(size)) % size).astype(jnp.int32)

    def owner(step):
        return owners[step : step + 1]

    def by_owner(own, *others):
        return place(size, [b[None] for b in others], mine, own[None])

    part = w_output.shape[0] // n
    gains = jnp.concatenate([norm1_gain[None], norm2_gain[None], jnp.zeros((14, cols), BF)])
    w_piece = jnp.concatenate(
        [
            lax.dynamic_slice_in_dim(w_output, group * part, part, 0),
            jnp.pad(gains, ((0, 0), (0, full - cols))),
        ]
    )
    w_blocks, x_blocks = [w_piece], [tokens]
    for step in steps:
        w_blocks.append(send(w_blocks[-1], 1, size))
    w_mixed = by_owner(*w_blocks)
    w_out = lax.all_gather(w_mixed[:, :part], "dp", axis=0)
    gains = w_mixed[:, part:, :cols]
    w_all = side_by_side([w_query, w_key, w_value])
    keep = kept_experts(routes, slot_order[0])
    router_wide = jnp.pad(router, ((0, 0), (0, 128 - EXPERTS)))
    halfway = HEAD_DIM // 2
    freqs = ROPE_BASE ** (-(jnp.arange(halfway, dtype=F32) * 2.0 / HEAD_DIM))
    angles = jnp.arange(length, dtype=F32)[:, None] * freqs[None, :]
    cosine = jnp.concatenate([jnp.cos(angles)] * 2, axis=1)
    sine = jnp.concatenate([-jnp.sin(angles), jnp.sin(angles)], axis=1)
    for step in steps:
        x_blocks.append(send(x_blocks[-1], 1, size))
    late_cot = copied(cotangent, (x_blocks[-2], keep, router_wide, cosine, sine))
    cot = lax.all_gather(late_cot, "tensor", axis=0)
    normed_one, q_pre, k_pre, own_sums = query_key_call(owners, x_blocks, gains, w_query, w_key)
    sums = [own_sums] + [send(own_sums, step, size) for step in steps]
    v_rows = value_call(normed_one, w_value)

    gq, gk = query_gain[None], key_gain[None]
    attended, lse, q_rot, k_rot = attn_forward(
        prefix, q_pre, k_pre, v_rows, gq, gk, cosine, sine, sums
    )

    received = [
        send(lax.dynamic_slice_in_dim(attended, (mine + step) % size * rows, rows, 0), step, size)
        for step in steps
    ]
    residual, normed_two = middle(owners, attended, received, w_out, x_blocks, gains)

    def add_wide(a, b, work=1):
        return add_blocks(a[None], b[None], work)[0]

    chunks = [copied(normed_two, (cot,))]
    chunks.append(send(chunks[0], 1, size))
    carried, later, dn2_flying = (), [], None
    for step in range(size):
        outs = expert_call(
            step, owner(step), chunks[step], cot, router_wide, keep, w_gate, w_up, w_down,
            residual if step == 0 else None, carried,
        )
        carried = outs[:5]
        if step < size - 2:
            chunks.append(send(copied(chunks[-1]), 1, size))
        if step == 0:
            own_dn2, expert_probs = outs[5:]
        else:
            later.append(outs[5])
        if step > 3:
            dn2_flying = send(add_wide(later.pop(0), dn2_flying), 1, size)
        elif step == min(3, size - 1):
            dn2_flying = send(copied(later.pop(0)), 1, size)
    h2t, dg, du, n2t, mix = carried

    expert_grads = lax.psum(gate_up_grads(n2t, dg, du), "dp")
    sum_down = Sum(n, 2, down_grads(table[half:], h2t, cot, n))
    dn2_flying = send(add_wide(later.pop(0), dn2_flying, LONG), 1, size)
    sum_down.keep = down_grads(table[:half], h2t, cot, n)
    for term in later:
        dn2_flying = send(add_wide(term, dn2_flying), 1, size)
    sum_down.step()

    branch_rows, small, *out_rows = middle_back(
        here, own_dn2, dn2_flying, expert_probs, router_wide, residual, normed_two, cot, gains, w_out
    )

    received = [send(out_rows[step], step, size) for step in steps]
    out_grad, branch_rows = arrange(owners, [out_rows[0]] + received, branch_rows)
    branch_blocks = [branch_rows, send(branch_rows, 1, size)]
    sum_down.step()
    dq, dk, dv, gain_grads, own_back = attn_backward(
        prefix, q_pre, k_pre, q_rot, k_rot, v_rows, out_grad.reshape(length, -1), lse, gq, gk,
        cosine, sine, sums,
    )
    back = [own_back] + [send(own_back, step, size) for step in steps]
    sum_down.step()
    branch_blocks.append(send(copied(branch_blocks[1], tuple(back[1:])), 1, size))
    grad_qkv, stat_one = norm_back(q_pre, k_pre, dq, dk, dv, gq, gk, sums, back)
    in_grads, gain_part = column_grads(normed_one, grad_qkv, w_all)
    sum_down.step()
    for step in range(3, size):
        branch_blocks.append(send(copied(branch_blocks[-1]), 1, size))
    packed = jnp.concatenate([jnp.concatenate([small[:7], gain_part[7:]]), gain_grads], axis=1)
    width = 3 * w_query.shape[1]
    extra = jnp.pad(packed.reshape(-1), (0, 32 * width - packed.size)).astype(BF).reshape(32, width)
    out_grads = row_grads(owners, attended, branch_blocks)
    extra = copied(extra, (expert_grads,))
    in_grads, out_grads, extra = lax.psum((in_grads, out_grads, extra), "dp")
    dn1_flying = send(input_grads(owner(1), cols, grad_qkv, w_all, work=LONG), 1, size)
    mix_flying = send(mix_block(owner(1), mix), 1, size)
    sum_down.step()
    for step in range(2, size):
        dn1_flying = send(input_grads(owner(step), cols, grad_qkv, w_all, dn1_flying), 1, size)
        sum_down.step()
        if step == 2:
            grad_gate, grad_up = widen_experts(expert_grads)
        if step < size - 1:
            mix_flying = send(mix_block(owner(step), mix, mix_flying), 1, size)
    mix_flying = send(mix_block(owner(size - 1), mix, mix_flying), 1, size)

    grad_tokens = final_grads(
        owners, grad_qkv, w_all, dn1_flying, tokens, own_sums, stat_one, norm1_gain[None],
        branch_blocks,
    )
    for _ in range(2 * len(swap_masks(n))):
        sum_down.step()
    grad_down = widen_pieces(positions, sum_down.finish(), n).reshape(w_down.shape)

    mixed = mix_block(owner(0), mix, mix_flying)
    extra = copied(extra)
    packed = extra.astype(F32).reshape(-1)[: packed.size].reshape(packed.shape)
    gain_total, packed = packed[:2, full:], packed[:, :full]
    packed = [packed] + [send(packed, step, size) for step in steps]
    grad_query, grad_key, grad_value = widen_projections(in_grads)
    grad_output = out_grads.astype(F32)

    packed = add(*packed)
    grad_router = packed[:EXPERTS].T
    own = lax.dynamic_slice_in_dim(packed[EXPERTS:], mine * cols, cols, 1)
    grad_norm2_gain = own[0]
    grad_norm1_gain = own[1] / norm1_gain.astype(F32)
    grad_query_gain, grad_key_gain = gain_total[0], gain_total[1]
    return (
        mixed, grad_tokens, grad_norm1_gain, grad_query, grad_key, grad_value, grad_query_gain,
        grad_key_gain, grad_output, grad_norm2_gain, grad_router, grad_gate, grad_up, grad_down,
    )


def solution(mesh):
    rows, weight_cols, weight_rows = P("dp", "tensor"), P(None, "tensor"), P("tensor", None)
    vector, expert_cols, expert_rows = P("tensor"), P(None, None, "tensor"), P(None, "tensor", None)
    return jax.shard_map(
        on_device,
        mesh=mesh,
        in_specs=(
            rows, rows, vector, weight_cols, weight_cols, weight_cols, vector, vector, weight_rows,
            vector, P(), expert_cols, expert_cols, expert_rows, P("dp", None), P("dp"),
            P("dp", None),
        ),
        out_specs=(
            rows, rows, vector, weight_cols, weight_cols, weight_cols, vector, vector, weight_rows,
            vector, P(), expert_cols, expert_cols, expert_rows,
        ),
        check_vma=False,
    )
```
